32 devices in a mesh: dp: 8 (over y, x, core), fsdp: 4 (over z).
Axes of the slice: x: 2, y: 2, z: 4, core: 2. Of those that a mesh axis runs over, the one named last changes fastest.
Arguments:
- tokens: bfloat16 [32, 1024, 768], P(('dp', 'fsdp')), may hold values from -6 to 6
- cotangent: bfloat16 [32, 1024, 768], P(('dp', 'fsdp')), may hold values from -6 to 6
- lengths: int32 [32], P(('dp', 'fsdp')), may hold values from 64 to 1024, as said below
- inward_weight: float32 [768, 2304], P('fsdp'), may hold values from -0.21875 to 0.21875
- inward_moment: float32 [768, 2304], P('fsdp'), may hold values from -640 to 640
- inward_square: float32 [768, 2304], P('fsdp'), may hold values from 12544 to 50176
- outward_weight: float32 [768, 768], P('fsdp'), may hold values from -3.5 to 3.5
- outward_moment: float32 [768, 768], P('fsdp'), may hold values from -40 to 40
- outward_square: float32 [768, 768], P('fsdp'), may hold values from 49 to 196
- expand_weight: float32 [768, 3072], P('fsdp'), may hold values from -0.21875 to 0.21875
- expand_moment: float32 [768, 3072], P('fsdp'), may hold values from -320 to 320
- expand_square: float32 [768, 3072], P('fsdp'), may hold values from 2508 to 10035
- shrink_weight: float32 [3072, 768], P('fsdp'), may hold values from -0.109375 to 0.109375
- shrink_moment: float32 [3072, 768], P('fsdp'), may hold values from -512 to 512
- shrink_square: float32 [3072, 768], P('fsdp'), may hold values from 6272 to 25088
- vectors: float32 [13, 768], P(None, 'fsdp'), may hold values from -2 to 2
- vector_moment: float32 [13, 768], P(None, 'fsdp'), may hold values from -640 to 640
- vector_square: float32 [13, 768], P(None, 'fsdp'), may hold values from 12544 to 50176
Outputs:
- layer_output: bfloat16 [32, 1024, 768], P(('dp', 'fsdp'))
- token_gradient: bfloat16 [32, 1024, 768], P(('dp', 'fsdp'))
- inward_master: float32 [768, 2304], P('fsdp')
- inward_momentum: float32 [768, 2304], P('fsdp')
- inward_squares: float32 [768, 2304], P('fsdp')
- outward_master: float32 [768, 768], P('fsdp')
- outward_momentum: float32 [768, 768], P('fsdp')
- outward_squares: float32 [768, 768], P('fsdp')
- expand_master: float32 [768, 3072], P('fsdp')
- expand_momentum: float32 [768, 3072], P('fsdp')
- expand_squares: float32 [768, 3072], P('fsdp')
- shrink_master: float32 [3072, 768], P('fsdp')
- shrink_momentum: float32 [3072, 768], P('fsdp')
- shrink_squares: float32 [3072, 768], P('fsdp')
- vector_master: float32 [13, 768], P(None, 'fsdp')
- vector_momentum: float32 [13, 768], P(None, 'fsdp')
- vector_squares: float32 [13, 768], P(None, 'fsdp')
The draws below stay inside these ranges and needn't reach their ends.
Inputs may be any that keep to these rules, and one draw needn't show every extreme that they name: Row r holds one sequence in positions 0 to lengths[r] - 1 and padding after it; some row has exactly 1024.
All inputs are finite; a program needn't handle non-finite values.
Results may differ from the reference program's by a relative error of at most 0.015.
The reference program's roundings to bfloat16 on the way count: a program that leaves them out, or rounds other values in their place, can miss the bound.
Values may be sent and summed in bfloat16 or wider, within the bound.
No kernel may reach another device: no remote copies, remote signals or barrier semaphores. Data moves between devices by JAX's collectives and lax.ppermute only.
A program may use at most 256 MiB of HBM per device.

```python
import math
import jax
import jax.numpy as jnp
from jax import lax

D = 768
HEADS = 12
HEAD = 64
FF = 3072
L = 1024
MINLEN = 64
STEP = 10
ROWS = 32
LIVE = 25088
OUT_FAN = 3


def draw_lengths(key, part):
    key = jax.random.fold_in(key, 7)
    one_key, two_key, pick_key = jax.random.split(key, 3)
    length_span = L - MINLEN
    factor_one = jax.random.randint(one_key, (ROWS,), 0, length_span + 1)
    factor_two = jax.random.randint(two_key, (ROWS,), 0, length_span + 1)
    lengths_out = L - factor_one * factor_two // max(length_span, 1)
    longest = jax.random.randint(pick_key, (), 0, ROWS)
    return jnp.where(jnp.arange(ROWS) == longest, L, lengths_out).astype(jnp.int32)


def draw_vectors(key, part):
    key = jax.random.fold_in(key, 11)
    random_vals = jnp.clip(jax.random.normal(key, (13, D), jnp.float32), -4.0, 4.0)
    row_index = jnp.arange(13)[:, None]
    return jnp.where(row_index < 2, 1.0 + 0.1 * random_vals, 0.5 * random_vals)


def block_levels(stream_key, dims, cuts, least, top_value):
    loudness, own = 1.0, jax.random.fold_in(stream_key, 6)
    for position, blocks in cuts:
        draws = jnp.exp(jax.random.uniform(jax.random.fold_in(own, position), (blocks,), jnp.float32, least / len(cuts), top_value / len(cuts)))
        loudness = loudness * jnp.repeat(draws, dims[position] // blocks).reshape([-1 if axis == position else 1 for axis in range(len(dims))])
    return loudness


def noise(own_key, shape, scale, reach, cuts=(), kind=jnp.bfloat16):
    level = block_levels(own_key, shape, cuts, -0.22, 0.18) if cuts else 1.0
    array = jax.random.normal(own_key, shape, jnp.float32) * scale * level
    return jnp.minimum(jnp.maximum(array, -reach), reach).astype(kind)


def setup_inputs(seed: int = 0) -> dict:
    key_of = jax.random.split(jax.random.key(seed), 19)
    tokens = noise(key_of[0], (ROWS, L, D), 1.0, 6.0, ((0, 32),))
    cotangent = noise(key_of[1], (ROWS, L, D), 1.0, 6.0, ((0, 32),))
    lengths = draw_lengths(jax.random.fold_in(key_of[18], 71), 0)
    inward_weight = noise(key_of[3], (D, 3 * D), D ** -0.5, 0.21875, ((0, 4),), jnp.float32)
    inward_moment = noise(key_of[4], (D, 3 * D), ((LIVE // 2) ** 0.5), 640.0, ((0, 4),), jnp.float32)
    inward_square = jnp.clip(jnp.exp(math.log(50176.0) - 1.3862944 * jax.random.uniform(key_of[5], (D, 3 * D), jnp.float32) ** block_levels(key_of[5], (D, 3 * D), ((0, 4),), -0.2, 0.2)), 12544.0, 50176.0)
    outward_weight = noise(key_of[6], (D, D), OUT_FAN ** -0.5, 3.5, ((0, 4),), jnp.float32)
    outward_moment = noise(key_of[7], (D, D), ((LIVE * OUT_FAN // (2 * D)) ** 0.5), 40.0, ((0, 4),), jnp.float32)
    outward_square = jnp.clip(jnp.exp(math.log(196.0) - 1.3862944 * jax.random.uniform(key_of[8], (D, D), jnp.float32) ** block_levels(key_of[8], (D, D), ((0, 4),), -0.2, 0.2)), 49.0, 196.0)
    expand_weight = noise(key_of[9], (D, FF), D ** -0.5, 0.21875, ((0, 4),), jnp.float32)
    expand_moment = noise(key_of[10], (D, FF), ((LIVE // 10) ** 0.5), 320.0, ((0, 4),), jnp.float32)
    expand_square = jnp.clip(jnp.exp(math.log(10035.0) - 1.3865934 * jax.random.uniform(key_of[11], (D, FF), jnp.float32) ** block_levels(key_of[11], (D, FF), ((0, 4),), -0.2, 0.2)), 2508.0, 10035.0)
    shrink_weight = noise(key_of[12], (FF, D), FF ** -0.5, 0.109375, ((0, 4),), jnp.float32)
    shrink_moment = noise(key_of[13], (FF, D), ((LIVE // 4) ** 0.5), 512.0, ((0, 4),), jnp.float32)
    shrink_square = jnp.clip(jnp.exp(math.log(25088.0) - 1.3862944 * jax.random.uniform(key_of[14], (FF, D), jnp.float32) ** block_levels(key_of[14], (FF, D), ((0, 4),), -0.2, 0.2)), 6272.0, 25088.0)
    vectors = draw_vectors(jax.random.fold_in(key_of[18], 71), 0)
    vector_moment = noise(key_of[16], (13, D), ((LIVE // 2) ** 0.5), 640.0, ((1, 4),), jnp.float32)
    vector_square = jnp.clip(jnp.exp(math.log(50176.0) - 1.3862944 * jax.random.uniform(key_of[17], (13, D), jnp.float32) ** block_levels(key_of[17], (13, D), ((1, 4),), -0.2, 0.2)), 12544.0, 50176.0)
    return {"tokens": tokens, "cotangent": cotangent, "lengths": lengths, "inward_weight": inward_weight, "inward_moment": inward_moment, "inward_square": inward_square, "outward_weight": outward_weight, "outward_moment": outward_moment, "outward_square": outward_square, "expand_weight": expand_weight, "expand_moment": expand_moment, "expand_square": expand_square, "shrink_weight": shrink_weight, "shrink_moment": shrink_moment, "shrink_square": shrink_square, "vectors": vectors, "vector_moment": vector_moment, "vector_square": vector_square}


NEG_FILL = -1000000000.0
NORM_EPS = 1e-12
BETA_ONE = 0.5
BETA_TWO = 0.5
ADAM_EPS = 1e-08
WEIGHT_DECAY = 0.01

@jax.custom_vjp
def low(v):
    return lax.optimization_barrier(v.astype(jnp.bfloat16)).astype(jnp.float32)

@jax.custom_vjp
def low_back(v):
    return v

def low_keep(v):
    return (low(v), None)

def low_pass(kept, grad):
    return (grad,)

def back_keep(v):
    return (v, None)

def back_low(kept, grad):
    return (low(grad),)
low.defvjp(low_keep, low_pass)
low_back.defvjp(back_keep, back_low)

def rotary_tables(length, head_size, head_count):
    column = jnp.arange(head_size * head_count) % head_size // 2
    freqs = jnp.power(10000.0, column.astype(jnp.float32) * (-2.0 / head_size))
    angles = jnp.arange(length, dtype=jnp.float32)[:, None] * freqs[None, :]
    return (jnp.cos(angles), jnp.sin(angles))

def turn(values, cosine_table, sine_table):
    parity = jnp.arange(values.shape[-1]) % 2 == 0
    shifted_up = jnp.roll(values, -1, axis=-1)
    shifted_down = jnp.roll(values, 1, axis=-1)
    return values * cosine_table + jnp.where(parity, -shifted_up, shifted_down) * sine_table

def norm_apply(summed, gain_vec, shift_vec):
    center = summed - lax.optimization_barrier(jnp.mean(summed, -1, keepdims=True))
    inverse = lax.rsqrt(lax.optimization_barrier(jnp.mean(center * center, -1, keepdims=True)) + NORM_EPS)
    return center * inverse * gain_vec + shift_vec

def attend_whole(pieces):
    query_row, key_row, value_row, length_row = pieces
    highest = lax.Precision.HIGHEST
    query_heads = query_row.reshape(L, HEADS, HEAD)
    key_heads = key_row.reshape(L, HEADS, HEAD)
    value_heads = value_row.reshape(L, HEADS, HEAD)
    scores = jnp.einsum('qhd,khd->hqk', query_heads, key_heads, precision=highest) * (1.0 / math.sqrt(HEAD))
    scores = low_back(scores)
    usable = jnp.arange(L) < length_row
    scores = jnp.where(usable[None, None, :], scores, NEG_FILL)
    top_score = lax.optimization_barrier(jnp.max(scores, -1, keepdims=True))
    expons = jnp.exp(scores - top_score)
    weights = low(expons / lax.optimization_barrier(jnp.sum(expons, -1, keepdims=True)))
    mixed_out = jnp.einsum('hqk,khd->qhd', weights, value_heads, precision=highest)
    return mixed_out.reshape(L, D)

def layer_forward(token_vals, length_rows, inward, outward, expand, shrink, vector_in, cosine_table, sine_table):
    highest = lax.Precision.HIGHEST
    inward_low = low(inward)
    outward_low = low(outward)
    expand_low = low(expand)
    shrink_low = low(shrink)
    vector_low = low(vector_in)
    row_count = token_vals.shape[0]
    flat_vals = token_vals.reshape(-1, D)
    joint_proj = low_back(jnp.dot(flat_vals, inward_low, precision=highest) + vector_low[4:7].reshape(-1))
    joint_rows = joint_proj.reshape(row_count, L, 3 * D)
    queries = low(turn(joint_rows[..., :D], cosine_table, sine_table))
    keys_all = low(turn(joint_rows[..., D:2 * D], cosine_table, sine_table))
    values_all = low(joint_rows[..., 2 * D:])
    attended = lax.map(jax.checkpoint(attend_whole), (queries, keys_all, values_all, length_rows))
    attended = low(low_back(attended.reshape(-1, D)))
    branch_out = low_back(jnp.dot(attended, outward_low, precision=highest) + vector_low[7])
    first_out = norm_apply(flat_vals + branch_out, vector_low[0], vector_low[2])
    hidden = low_back(jnp.dot(low(first_out), expand_low, precision=highest) + vector_low[9:13].reshape(-1))
    active = low(jax.nn.gelu(hidden, approximate=False))
    second_out = low_back(jnp.dot(active, shrink_low, precision=highest) + vector_low[8])
    return norm_apply(first_out + second_out, vector_low[1], vector_low[3]).reshape(row_count, L, D)

def adam_update(master, moment, square, gradient, rate, decay):
    momentum = BETA_ONE * moment + (1.0 - BETA_ONE) * gradient
    squares = BETA_TWO * square + (1.0 - BETA_TWO) * gradient * gradient
    corrected = momentum / (1.0 - BETA_ONE ** STEP)
    spread = jnp.sqrt(squares / (1.0 - BETA_TWO ** STEP))
    return (master - rate * (corrected / (spread + ADAM_EPS) + decay * master), momentum, squares)

def reference(tokens, cotangent, lengths, inward_weight, inward_moment, inward_square, outward_weight, outward_moment, outward_square, expand_weight, expand_moment, expand_square, shrink_weight, shrink_moment, shrink_square, vectors, vector_moment, vector_square):
    cosine_table, sine_table = rotary_tables(L, HEAD, HEADS)
    group_rows = math.gcd(ROWS, max(1, 4096 // L))
    params = (inward_weight, outward_weight, expand_weight, shrink_weight, vectors)

    def one_group(running, pieces):
        token_rows, cot_rows, length_rows = pieces
        usable = (jnp.arange(L)[None, :] < length_rows[:, None]).astype(jnp.float32)

        def forward(token_vals, inward, outward, expand, shrink, vector_in):
            return layer_forward(token_vals, length_rows, inward, outward, expand, shrink, vector_in, cosine_table, sine_table)
        output, pullback = jax.vjp(forward, token_rows.astype(jnp.float32), *params)
        gradients = pullback(cot_rows.astype(jnp.float32) * usable[..., None])
        running = tuple((summed + portion for summed, portion in zip(running, gradients[1:])))
        return (running, (output.astype(jnp.bfloat16), gradients[0].astype(jnp.bfloat16)))
    zero_grads = tuple((jnp.zeros_like(tensor) for tensor in params))
    steps = ROWS // group_rows
    grad_sums, (outputs, token_grads) = lax.scan(one_group, zero_grads, (tokens.reshape(steps, group_rows, L, D), cotangent.reshape(steps, group_rows, L, D), lengths.reshape(steps, group_rows)))
    outputs = outputs.reshape(ROWS, L, D)
    token_grads = token_grads.reshape(ROWS, L, D)
    inward_new = adam_update(inward_weight, inward_moment, inward_square, grad_sums[0], 1.0 / math.sqrt(D), WEIGHT_DECAY)
    outward_new = adam_update(outward_weight, outward_moment, outward_square, grad_sums[1], 1.0 / math.sqrt(OUT_FAN), WEIGHT_DECAY)
    expand_new = adam_update(expand_weight, expand_moment, expand_square, grad_sums[2], 1.0 / math.sqrt(D), WEIGHT_DECAY)
    shrink_new = adam_update(shrink_weight, shrink_moment, shrink_square, grad_sums[3], 1.0 / math.sqrt(FF), WEIGHT_DECAY)
    vector_new = adam_update(vectors, vector_moment, vector_square, grad_sums[4], 0.5, 0.0)
    return (outputs, token_grads, inward_new[0], inward_new[1], inward_new[2], outward_new[0], outward_new[1], outward_new[2], expand_new[0], expand_new[1], expand_new[2], shrink_new[0], shrink_new[1], shrink_new[2], vector_new[0], vector_new[1], vector_new[2])
```

```python
import functools, math
import jax, jax.numpy as jnp
import numpy as np
from jax import lax
from jax.sharding import PartitionSpec as P
from jax.experimental import pallas as pl
from jax.experimental.pallas import tpu as pltpu

HEAD=64
BF=jnp.bfloat16
F32=jnp.float32
NEG=-1000000000.0
VLIM=60*1024*1024
ROOT_HALF = 0.7071067811865476
INV_ROOT_TAU = 0.3989422804014327

def dot_nn(a,b): return lax.dot_general(a,b,(((1,),(0,)),((),())),preferred_element_type=F32)
def dot_nt(a,b): return lax.dot_general(a,b,(((1,),(1,)),((),())),preferred_element_type=F32)
def dot_tn(a,b): return lax.dot_general(a,b,(((0,),(0,)),((),())),preferred_element_type=F32)

def tables(length):
    lane=np.arange(128)
    freq=10000.0 ** (-2.0*((lane%64)//2)/64)
    ang=np.arange(length)[:,None]*freq[None,:]
    cos=np.cos(ang); sin=np.sin(ang)
    even=(lane%2==0)[None,:]
    return (cos.astype(np.float32), np.where(even,-sin,0).astype(np.float32), np.where(even,0,sin).astype(np.float32))

def rotate(u,cos,up,down):
    return u*cos + pltpu.roll(u,127,1)*up + pltpu.roll(u,1,1)*down

def qkv_kernel(x_ref,w_ref,b_ref,cos_ref,up_ref,down_ref,o_ref):
    x=x_ref[...]
    cos=cos_ref[...]; up=up_ref[...]; down=down_ref[...]
    width=w_ref.shape[1]
    model=x.shape[1]
    for c in range(width//256):
        acc=dot_nn(x,w_ref[:,c*256:(c+1)*256])+b_ref[:,c*256:(c+1)*256]
        for t in range(2):
            lo=c*256+t*128
            u=acc[:,t*128:(t+1)*128]
            if lo<2*model:
                u=rotate(u,cos,up,down)
            if lo<model:
                u=u*0.125
            o_ref[:,lo:lo+128]=u.astype(BF)

def qkv_call(x,w,b,tabs,length,bt=256):
    n,model=x.shape
    per=length//bt
    width=w.shape[1]
    tspec=pl.BlockSpec((bt,128),lambda i:(i%per,0))
    return pl.pallas_call(qkv_kernel,grid=(n//bt,),
        in_specs=[pl.BlockSpec((bt,model),lambda i:(i,0)),
                  pl.BlockSpec((model,width),lambda i:(0,0)),
                  pl.BlockSpec((1,width),lambda i:(0,0)),tspec,tspec,tspec],
        out_specs=pl.BlockSpec((bt,width),lambda i:(i,0)),
        out_shape=jax.ShapeDtypeStruct((n,width),BF),
        cost_estimate=pl.CostEstimate(flops=2*n*model*width,bytes_accessed=2*(n*model+model*width+n*width),transcendentals=0),
        compiler_params=pltpu.CompilerParams(vmem_limit_bytes=VLIM))(x,w,b,*tabs)

def attn_kernel(len_ref,q_ref,k_ref,v_ref,o_ref,qa_ref,*,bq):
    length=q_ref.shape[0]
    live=len_ref[pl.program_id(0)]
    lane=lax.broadcasted_iota(jnp.int32,(length,128),1)
    pos=lax.broadcasted_iota(jnp.int32,(length,128),0)
    k=k_ref[...].astype(F32); v=v_ref[...].astype(F32)
    kh=[];vh=[]
    for h in range(2):
        own=(lane//64)==h
        aux=64*(1-h)
        kh.append(jnp.where(own,k,jnp.where((lane==aux)&(pos>=live),NEG,0.0)).astype(BF))
        vh.append(jnp.where(own,v,1.0).astype(BF))
    lane=lax.broadcasted_iota(jnp.int32,(bq,128),1)
    for i in range(length//bq):
        q=q_ref[i*bq:(i+1)*bq,:].astype(F32)
        parts=[]
        for h in range(2):
            own=(lane//64)==h
            aux=64*(1-h)
            qh=jnp.where(own,q,jnp.where(lane==aux,1.0,0.0)).astype(BF)
            s=dot_nt(qh,kh[h])
            m=jnp.max(s,-1,keepdims=True)
            e=jnp.exp(s-m).astype(BF)
            o=dot_nn(e,vh[h])
            parts.append(o/pltpu.roll(o,64,1))
            neg=-(m+jnp.log(o))
            hi=neg.astype(BF).astype(F32)
            mid=(neg-hi).astype(BF).astype(F32)
            low=neg-hi-mid
            qa=jnp.where(own,q,jnp.where(lane==aux,hi,jnp.where(lane==aux+1,mid,jnp.where(lane==aux+2,low,jnp.where(lane==aux+3,1.0,0.0)))))
            qa_ref[h,i*bq:(i+1)*bq,:]=qa.astype(BF)
        o_ref[i*bq:(i+1)*bq,:]=jnp.where(lane<64,parts[0],parts[1]).astype(BF)

def attn_call(lengths,qkv,length,bq=256):
    n,width=qkv.shape
    rows=n//length
    pairs=width//3//128
    gs=pltpu.PrefetchScalarGridSpec(num_scalar_prefetch=1,grid=(rows,pairs),
        in_specs=[pl.BlockSpec((length,128),lambda b,p,_:(b,p)),
                  pl.BlockSpec((length,128),lambda b,p,_:(b,pairs+p)),
                  pl.BlockSpec((length,128),lambda b,p,_:(b,2*pairs+p))],
        out_specs=[pl.BlockSpec((length,128),lambda b,p,_:(b,p)),
                   pl.BlockSpec((None,2,length,128),lambda b,p,_:(b,p,0,0))])
    return pl.pallas_call(functools.partial(attn_kernel,bq=bq),grid_spec=gs,
        out_shape=[jax.ShapeDtypeStruct((n,width//3),BF),jax.ShapeDtypeStruct((rows,2*pairs,length,128),BF)],
        cost_estimate=pl.CostEstimate(flops=rows*pairs*2*4*length*length*128,bytes_accessed=2*(n*width*2),transcendentals=rows*pairs*2*length*length),
        compiler_params=pltpu.CompilerParams(vmem_limit_bytes=VLIM))(lengths,qkv,qkv,qkv)

def back_kernel(len_ref,qa_ref,k_ref,v_ref,o_ref,do_ref,cos_ref,up_ref,down_ref,dq_ref,dk_ref,dv_ref,doa_ref,dqt_ref,*,bk):
    length=k_ref.shape[0]
    live=len_ref[pl.program_id(0)]
    lane=lax.broadcasted_iota(jnp.int32,(length,128),1)
    do=do_ref[...].astype(F32)
    prod=do*o_ref[...].astype(F32)
    for h in range(2):
        own=(lane//64)==h
        aux=64*(1-h)
        neg=-jnp.sum(jnp.where(own,prod,0.0),-1,keepdims=True)
        hi=neg.astype(BF).astype(F32)
        low=neg-hi
        doa_ref[h]=jnp.where(own,do,jnp.where(lane==aux,hi,jnp.where(lane==aux+1,low,0.0))).astype(BF)
    lane=lax.broadcasted_iota(jnp.int32,(bk,128),1)
    pos=lax.broadcasted_iota(jnp.int32,(bk,128),0)
    for i in range(length//bk):
        sl=slice(i*bk,(i+1)*bk)
        k=k_ref[sl,:].astype(F32); v=v_ref[sl,:].astype(F32)
        kt=k.T.astype(BF)
        dks=[];dvs=[]
        for h in range(2):
            own=(lane//64)==h
            aux=64*(1-h)
            ka=jnp.where(own,k,jnp.where((lane>=aux)&(lane<aux+3),1.0,jnp.where((lane==aux+3)&(pos+i*bk>=live),NEG,0.0))).astype(BF)
            va=jnp.where(own,v,jnp.where((lane==aux)|(lane==aux+1),1.0,0.0)).astype(BF)
            qa=qa_ref[h]
            doa=doa_ref[h]
            p=jnp.exp(dot_nt(ka,qa))
            ds=(p*dot_nt(va,doa)).astype(BF)
            dvs.append(dot_nn(p.astype(BF),doa))
            dks.append(dot_nn(ds,qa))
            t=dot_nn(kt[h*64:(h+1)*64,:],ds)
            if i==0: dqt_ref[h*64:(h+1)*64,:]=t
            else: dqt_ref[h*64:(h+1)*64,:]+=t
        dv_ref[sl,:]=jnp.where(lane<64,dvs[0],dvs[1]).astype(BF)
        dk=jnp.where(lane<64,dks[0],dks[1])
        dk_ref[sl,:]=rotate(dk,cos_ref[sl,:],-up_ref[sl,:],-down_ref[sl,:]).astype(BF)
    dq=dqt_ref[...].T*0.125
    dq_ref[...]=rotate(dq,cos_ref[...],-up_ref[...],-down_ref[...]).astype(BF)

def back_call(lengths,qa,qkv,attn,dattn,tabs,length,bk=256):
    n,width=qkv.shape
    rows=n//length
    pairs=width//3//128
    col=lambda b,p,_:(b,p)
    tspec=pl.BlockSpec((length,128),lambda b,p,_:(0,0))
    gs=pltpu.PrefetchScalarGridSpec(num_scalar_prefetch=1,grid=(rows,pairs),
        in_specs=[pl.BlockSpec((None,2,length,128),lambda b,p,_:(b,p,0,0)),
                  pl.BlockSpec((length,128),lambda b,p,_:(b,pairs+p)),
                  pl.BlockSpec((length,128),lambda b,p,_:(b,2*pairs+p)),
                  pl.BlockSpec((length,128),col),pl.BlockSpec((length,128),col),tspec,tspec,tspec],
        out_specs=[pl.BlockSpec((length,128),col)]*3,
        scratch_shapes=[pltpu.VMEM((2,length,128),BF),pltpu.VMEM((128,length),F32)])
    o=jax.ShapeDtypeStruct((n,width//3),BF)
    return pl.pallas_call(functools.partial(back_kernel,bk=bk),grid_spec=gs,out_shape=[o,o,o],
        cost_estimate=pl.CostEstimate(flops=rows*pairs*2*10*length*length*128,bytes_accessed=2*(n*width*3),transcendentals=rows*pairs*2*length*length),
        compiler_params=pltpu.CompilerParams(vmem_limit_bytes=VLIM))(lengths,qa,qkv,qkv,attn,dattn,*tabs)

def norm_fwd(u):
    c=u-jnp.mean(u,-1,keepdims=True)
    r=lax.rsqrt(jnp.mean(c*c,-1,keepdims=True)+1e-12)
    return c*r,r
def norm_bwd(gy,n,r,g):
    a=gy*g
    return r*(a-jnp.mean(a,-1,keepdims=True)-n*jnp.mean(a*n,-1,keepdims=True))

def ffn_kernel(len_ref,x_ref,at_ref,cot_ref,wo_ref,w1_ref,w2_ref,v_ref,
               out_ref,act_ref,dz_ref,y1_ref,dpre_ref,dr1_ref,da_ref,dat_ref,dvec_ref,slope_ref,*,length,fc):
    step=pl.program_id(0)
    bt,model=x_ref.shape
    ff=w1_ref.shape[1]
    per=length//bt
    live=len_ref[step//per]
    row=lambda i:v_ref[i:i+1,:]
    r1=x_ref[...].astype(F32)+(dot_nn(at_ref[...],wo_ref[...])+row(7))
    n1,i1=norm_fwd(r1)
    y1=n1*row(0)+row(2)
    y1b=y1.astype(BF)
    y1_ref[...]=y1b
    z=jnp.zeros((bt,model),F32)
    for c in range(ff//fc):
        sl=slice(c*fc,(c+1)*fc)
        bias=v_ref[9+c*fc//model:10+c*fc//model,(c*fc)%model:(c*fc)%model+fc]
        pre=dot_nn(y1b,w1_ref[:,sl])+bias
        phi=0.5*(1.0+lax.erf(pre*ROOT_HALF))
        act=(pre*phi).astype(BF)
        act_ref[:,sl]=act
        slope_ref[:,sl]=phi+pre*(jnp.exp(-0.5*pre*pre)*INV_ROOT_TAU)
        z=z+dot_nn(act,w2_ref[sl,:])
    r2=y1+(z+row(8))
    n2,i2=norm_fwd(r2)
    out_ref[...]=(n2*row(1)+row(3)).astype(BF)
    pos=lax.broadcasted_iota(jnp.int32,(bt,model),0)+(step%per)*bt
    e=jnp.where(pos<live,cot_ref[...].astype(F32),0.0)
    dr2=norm_bwd(e,n2,i2,row(1))
    dz=dr2.astype(BF)
    dz_ref[...]=dz
    @pl.when(step==0)
    def _():
        dvec_ref[...]=jnp.zeros_like(dvec_ref)
    def add(i,val,off=0):
        dvec_ref[i:i+1,off:off+val.shape[1]]+=jnp.sum(val,0,keepdims=True)
    add(1,e*n2); add(3,e); add(8,dz.astype(F32))
    dy=dr2
    for c in range(ff//fc):
        sl=slice(c*fc,(c+1)*fc)
        dpre=(dot_nt(dz,w2_ref[sl,:])*slope_ref[:,sl]).astype(BF)
        dpre_ref[:,sl]=dpre
        add(9+c*fc//model,dpre.astype(F32),(c*fc)%model)
        dy=dy+dot_nt(dpre,w1_ref[:,sl])
    add(0,dy*n1); add(2,dy)
    dr1=norm_bwd(dy,n1,i1,row(0))
    dr1_ref[...]=dr1
    da=dr1.astype(BF)
    da_ref[...]=da
    add(7,da.astype(F32))
    dat_ref[...]=dot_nt(da,wo_ref[...]).astype(BF)

def ffn_call(lengths,x,at,cot,wo,w1,w2,vec,length,bt=256,fc=768):
    n,model=x.shape
    ff=w1.shape[1]
    tok=pl.BlockSpec((bt,model),lambda i,_:(i,0))
    wide=pl.BlockSpec((bt,ff),lambda i,_:(i,0))
    full=lambda a:pl.BlockSpec(a.shape,lambda i,_:(0,0),pipeline_mode=pl.Buffered(1))
    gs=pltpu.PrefetchScalarGridSpec(num_scalar_prefetch=1,grid=(n//bt,),
        in_specs=[tok,tok,tok,full(wo),full(w1),full(w2),full(vec)],
        out_specs=[tok,wide,tok,tok,wide,tok,tok,tok,pl.BlockSpec((13,model),lambda i,_:(0,0))],
        scratch_shapes=[pltpu.VMEM((bt,ff),F32)])
    s=lambda w,t:jax.ShapeDtypeStruct((n,w),t)
    return pl.pallas_call(functools.partial(ffn_kernel,length=length,fc=fc),grid_spec=gs,
        out_shape=[s(model,BF),s(ff,BF),s(model,BF),s(model,BF),s(ff,BF),s(model,F32),s(model,BF),s(model,BF),jax.ShapeDtypeStruct((13,model),F32)],
        cost_estimate=pl.CostEstimate(flops=n*(4*model*model+8*model*ff),bytes_accessed=n*(model*20+ff*4)+model*ff*4,transcendentals=n*ff*2),
        compiler_params=pltpu.CompilerParams(vmem_limit_bytes=VLIM))(lengths,x,at,cot,wo,w1,w2,vec)

STEP=10
BETA_ONE=0.5
BETA_TWO=0.5
ADAM_EPS=1e-08
WEIGHT_DECAY=0.01
OUT_FAN=3


def adam_update(master, moment, square, gradient, rate, decay):
    momentum = BETA_ONE * moment + (1.0 - BETA_ONE) * gradient
    squares = BETA_TWO * square + (1.0 - BETA_TWO) * gradient * gradient
    corrected = momentum / (1.0 - BETA_ONE**STEP)
    spread = jnp.sqrt(squares / (1.0 - BETA_TWO**STEP))
    return (master - rate * (corrected / (spread + ADAM_EPS) + decay * master), momentum, squares)


def local(tokens,cotangent,lengths,inward_weight,inward_moment,inward_square,outward_weight,outward_moment,outward_square,
          expand_weight,expand_moment,expand_square,shrink_weight,shrink_moment,shrink_square,vectors,vector_moment,vector_square):
    rows,length,model=tokens.shape
    x=tokens.reshape(-1,model)
    cot=cotangent.reshape(-1,model)
    t=[jnp.asarray(a) for a in tables(length)]
    gather=lambda w,axis=0: lax.all_gather(w.astype(BF),"fsdp",axis=axis,tiled=True)
    wqkv=gather(inward_weight)
    vec=gather(vectors,1).astype(F32)
    wo=gather(outward_weight)
    w1=gather(expand_weight)
    w2=gather(shrink_weight)
    qkv=qkv_call(x,wqkv,vec[4:7].reshape(1,-1),t,length)
    attn,qa=attn_call(lengths,qkv,length)
    out,act,dz,y1,dpre,dr1,da,dat,dvec=ffn_call(lengths,x,attn,cot,wo,w1,w2,vec,length)
    dw2=dot_tn(act,dz).astype(BF)
    dw1=dot_tn(y1,dpre).astype(BF)
    dwo=dot_tn(attn,da).astype(BF)
    dq,dk,dv=back_call(lengths,qa,qkv,attn,dat,t,length)
    dwq=jnp.concatenate([dot_tn(x,g).astype(BF) for g in (dq,dk,dv)],1)
    tg=(dr1+dot_nt(dq,wqkv[:,:model])+dot_nt(dk,wqkv[:,model:2*model])+dot_nt(dv,wqkv[:,2*model:])).astype(BF)
    db=[jnp.sum(g,0,dtype=F32)[None] for g in (dq,dk,dv)]
    dvec=jnp.concatenate([dvec[:4],*db,dvec[7:]])
    def reduce(g,axis=0):
        r=lax.psum_scatter(g,"fsdp",scatter_dimension=axis,tiled=True)
        return lax.psum(r.astype(F32),"dp")
    new=[]
    for w,m,s,g,rate,decay in ((inward_weight,inward_moment,inward_square,reduce(dwq),1/math.sqrt(model),WEIGHT_DECAY),
                    (outward_weight,outward_moment,outward_square,reduce(dwo),1/math.sqrt(OUT_FAN),WEIGHT_DECAY),
                    (expand_weight,expand_moment,expand_square,reduce(dw1),1/math.sqrt(model),WEIGHT_DECAY),
                    (shrink_weight,shrink_moment,shrink_square,reduce(dw2),1/math.sqrt(w1.shape[1]),WEIGHT_DECAY),
                    (vectors,vector_moment,vector_square,reduce(dvec,1),0.5,0.0)):
        new+=list(adam_update(w,m,s,g,rate,decay))
    return (out.reshape(tokens.shape),tg.reshape(tokens.shape),*new)


def solution(mesh):
    in_specs = (
        P(("dp", "fsdp"), None, None),
        P(("dp", "fsdp"), None, None),
        P(("dp", "fsdp")),
        P("fsdp", None),
        P("fsdp", None),
        P("fsdp", None),
        P("fsdp", None),
        P("fsdp", None),
        P("fsdp", None),
        P("fsdp", None),
        P("fsdp", None),
        P("fsdp", None),
        P("fsdp", None),
        P("fsdp", None),
        P("fsdp", None),
        P(None, "fsdp"),
        P(None, "fsdp"),
        P(None, "fsdp"),
    )
    out_specs = (
        P(("dp", "fsdp"), None, None),
        P(("dp", "fsdp"), None, None),
        P("fsdp", None),
        P("fsdp", None),
        P("fsdp", None),
        P("fsdp", None),
        P("fsdp", None),
        P("fsdp", None),
        P("fsdp", None),
        P("fsdp", None),
        P("fsdp", None),
        P("fsdp", None),
        P("fsdp", None),
        P("fsdp", None),
        P(None, "fsdp"),
        P(None, "fsdp"),
        P(None, "fsdp"),
    )
    return jax.shard_map(local, mesh=mesh, in_specs=in_specs, out_specs=out_specs, check_vma=False)
```

```python
import functools
import math

import jax
import jax.numpy as jnp
import numpy as np
from jax import lax
from jax.experimental import pallas as pl
from jax.experimental.pallas import tpu as pltpu
from jax.sharding import PartitionSpec as P

BF = jnp.bfloat16
F32 = jnp.float32
HEAD = 64
STEP = 10
OUT_FAN = 3
BETA_ONE = 0.5
BETA_TWO = 0.5
ADAM_EPS = 1e-08
WEIGHT_DECAY = 0.01
NORM_EPS = 1e-12
NEG_FILL = -1000000000.0
ROOT_HALF = 0.7071067811865476
INV_ROOT_TAU = 0.3989422804014327
ANY = pl.BlockSpec(memory_space=pl.ANY)


def dot_nn(a, b):
    return lax.dot_general(a, b, (((1,), (0,)), ((), ())), preferred_element_type=F32)


def dot_nt(a, b):
    return lax.dot_general(a, b, (((1,), (1,)), ((), ())), preferred_element_type=F32)


def dot_tn(a, b):
    return lax.dot_general(a, b, (((0,), (0,)), ((), ())), preferred_element_type=F32)


def params(mebibytes):
    return pltpu.CompilerParams(vmem_limit_bytes=mebibytes * 1024 * 1024)


def cost(flops, moved, trans=0):
    return pl.CostEstimate(flops=int(flops), bytes_accessed=int(moved), transcendentals=int(trans))


def swap(x, even, odd=None):
    odd = even if odd is None else odd
    return lax.ppermute(x, "dp", [(i, i ^ (odd if i % 2 else even)) for i in range(8)])


def swap_core(x):
    return swap(x, 1)


def swap_first(x):
    return swap(x, 4, 2)


def swap_second(x):
    return swap(x, 2, 4)


def cross(x, bit):
    return lax.ppermute(x, "fsdp", [(i, i ^ bit) for i in range(4)])


def over_z(part):
    return tuple(cross(part, k) for k in (1, 2, 3))


def after(x, *others):
    return lax.optimization_barrier((x, *others))[0]


TURNED = (0, 2, 1, 3)


def exchanged(k, c):
    return jnp.where(c == 0, k, (k & 1) * 2 + (k >> 1))


def column_copies(place, own, pieces, dst, flat, first=0):
    f, j, c = place
    rows, cols = own.shape
    r, h = rows // 4, cols // 2
    out = [(own, flat)]
    for refs, half in ((pieces[:4], c), (pieces[4:], 1 - c)):
        for slot, ref in enumerate(refs):
            kj = exchanged(slot, half)
            for kf in range(1, 4):
                start = pl.multiple_of((f ^ kf) * rows + (j ^ kj) * r, 16)
                at = dst.at[pl.ds(start, r), pl.ds(pl.multiple_of(half * h, 128), h)]
                out.append((ref.at[kf - 1, :, pl.ds(first, h)], at))
    return out


def in_copies(place, refs, dst, flat):
    if len(refs) == 1:
        return [(refs[0], dst)]
    return column_copies(place, refs[0], refs[1:], dst, flat)


def out_copies(place, refs, dst, flat):
    if len(refs) == 2:
        return [(refs[0], dst)]
    return column_copies(place, refs[0], refs[2:], dst, flat)


def expand_copies(place, refs, dst, flat):
    if len(refs) == 2:
        return [(refs[1], dst)]
    return column_copies(place, refs[1], refs[2:], dst, flat, refs[0].shape[1] // 2)


def shrink_copies(place, refs, dst, flat):
    if len(refs) == 1:
        return [(refs[0], dst)]
    f, j, c = place
    own, pieces = refs[0], refs[1:]
    rows = own.shape[0]
    r = rows // 8
    out = [(own, flat)]
    for refs, half in ((pieces[:4], c), (pieces[4:], 1 - c)):
        for slot, ref in enumerate(refs):
            kj = exchanged(slot, half)
            for kf in range(1, 4):
                start = pl.multiple_of((f ^ kf) * rows + half * (rows // 2) + (j ^ kj) * r, 16)
                out.append((ref.at[kf - 1], dst.at[pl.ds(start, r), :]))
    return out


def own_part(place, pairs, dst, flat):
    if len(pairs) > 1:
        rows = flat.shape[0]
        dst[pl.ds(pl.multiple_of(place[0] * rows, 16), rows), :] = flat[...].astype(BF)


MOST = 25


def begin(pairs, sems):
    for i, (src, dst) in enumerate(pairs):
        pltpu.make_async_copy(src, dst, sems.at[i]).start()


def finish(pairs, sems):
    for i, (src, dst) in enumerate(pairs):
        pltpu.make_async_copy(src, dst, sems.at[i]).wait()


def place_of(ref):
    return ref[0], ref[1], ref[2]


def tables(length):
    lane = np.arange(128)
    angles = np.arange(length)[:, None] * (10000.0 ** (-2.0 * ((lane % HEAD) // 2) / HEAD))[None, :]
    cosine, sine = np.cos(angles), np.sin(angles)
    even = (lane % 2 == 0)[None, :]
    parts = (cosine, np.where(even, -sine, 0.0), np.where(even, 0.0, sine))
    return [jnp.asarray(part.astype(np.float32)) for part in parts]


def rotate(u, cosine, up, down):
    return u * cosine + pltpu.roll(u, 127, 1) * up + pltpu.roll(u, 1, 1) * down


def qkv_kernel(*refs, pieces):
    place_ref, x_ref, b_ref, cos_ref, up_ref, down_ref = refs[:6]
    w_refs = refs[6 : 6 + pieces]
    o_ref, w_ref, flat_ref, sems = refs[6 + pieces :]

    @pl.when(pl.program_id(0) == 0)
    def _():
        copies = in_copies(place_of(place_ref), w_refs, w_ref, flat_ref)
        begin(copies, sems)
        finish(copies, sems)
        own_part(place_of(place_ref), copies, w_ref, flat_ref)

    x = x_ref[...]
    cosine, up, down = cos_ref[...], up_ref[...], down_ref[...]
    model, width = w_ref.shape
    for col in range(0, width, 256):
        acc = dot_nn(x, w_ref[:, col : col + 256]) + b_ref[:, col : col + 256]
        for tile in range(2):
            lo = col + tile * 128
            u = acc[:, tile * 128 : (tile + 1) * 128]
            if lo < 2 * model:
                u = rotate(u, cosine, up, down)
            if lo < model:
                u = u * (1.0 / math.sqrt(HEAD))
            o_ref[:, lo : lo + 128] = u.astype(BF)


def qkv_call(place, x, weight, bias, tabs, length, block=256):
    n, model = x.shape
    per = length // block
    width = bias.shape[1]
    table = pl.BlockSpec((block, 128), lambda i, _: (i % per, 0))
    spec = pltpu.PrefetchScalarGridSpec(
        num_scalar_prefetch=1,
        grid=(n // block,),
        in_specs=[
            pl.BlockSpec((block, model), lambda i, _: (i, 0)),
            pl.BlockSpec((1, width), lambda i, _: (0, 0)),
            table,
            table,
            table,
        ]
        + [ANY] * len(weight),
        out_specs=pl.BlockSpec((block, width), lambda i, _: (i, 0)),
        scratch_shapes=[
            pltpu.VMEM((model, width), BF),
            pltpu.VMEM((model // 4, width), F32),
            pltpu.SemaphoreType.DMA((MOST,)),
        ],
    )
    return pl.pallas_call(
        functools.partial(qkv_kernel, pieces=len(weight)),
        grid_spec=spec,
        out_shape=jax.ShapeDtypeStruct((n, width), BF),
        cost_estimate=cost(2 * n * model * width, 2 * (n * model + model * width + n * width)),
        compiler_params=params(60),
        name="qkv",
    )(place, x, bias, *tabs, *weight)


def attend_kernel(len_ref, q_ref, k_ref, v_ref, o_ref, qa_ref, *, block):
    length = q_ref.shape[0]
    live = len_ref[pl.program_id(0)]
    lane = lax.broadcasted_iota(jnp.int32, (length, 128), 1)
    pos = lax.broadcasted_iota(jnp.int32, (length, 128), 0)
    k, v = k_ref[...].astype(F32), v_ref[...].astype(F32)
    keys, values = [], []
    for h in range(2):
        own = (lane // HEAD) == h
        aux = HEAD * (1 - h)
        mask = jnp.where((lane == aux) & (pos >= live), NEG_FILL, 0.0)
        keys.append(jnp.where(own, k, mask).astype(BF))
        values.append(jnp.where(own, v, 1.0).astype(BF))
    lane = lax.broadcasted_iota(jnp.int32, (block, 128), 1)
    for i in range(length // block):
        rows = slice(i * block, (i + 1) * block)
        q = q_ref[rows, :].astype(F32)
        mixed = []
        for h in range(2):
            own = (lane // HEAD) == h
            aux = HEAD * (1 - h)
            scores = dot_nt(jnp.where(own, q, jnp.where(lane == aux, 1.0, 0.0)).astype(BF), keys[h])
            top = jnp.max(scores, -1, keepdims=True)
            summed = dot_nn(jnp.exp(scores - top).astype(BF), values[h])
            mixed.append(summed / pltpu.roll(summed, HEAD, 1))
            shift = -(top + jnp.log(summed))
            hi = shift.astype(BF).astype(F32)
            mid = (shift - hi).astype(BF).astype(F32)
            extra = jnp.where(lane == aux, hi, jnp.where(lane == aux + 1, mid, shift - hi - mid))
            extra = jnp.where(lane < aux + 3, extra, jnp.where(lane == aux + 3, 1.0, 0.0))
            qa_ref[h, rows, :] = jnp.where(own, q, extra).astype(BF)
        o_ref[rows, :] = jnp.where(lane < HEAD, mixed[0], mixed[1]).astype(BF)


def attend_call(lengths, qkv, length, first, count, block=256):
    n, width = qkv.shape
    rows, pairs = n // length, width // 384
    one = lambda off: pl.BlockSpec((length, 128), lambda b, p, _: (b, off * pairs + first + p))
    spec = pltpu.PrefetchScalarGridSpec(
        num_scalar_prefetch=1,
        grid=(rows, count),
        in_specs=[one(0), one(1), one(2)],
        out_specs=[
            pl.BlockSpec((length, 128), lambda b, p, _: (b, p)),
            pl.BlockSpec((None, 2, length, 128), lambda b, p, _: (b, p, 0, 0)),
        ],
    )
    return pl.pallas_call(
        functools.partial(attend_kernel, block=block),
        grid_spec=spec,
        out_shape=[
            jax.ShapeDtypeStruct((n, count * 128), BF),
            jax.ShapeDtypeStruct((rows, 2 * count, length, 128), BF),
        ],
        cost_estimate=cost(rows * count * 32 * length * length * 128, 12 * n * count * 128, rows * count * 2 * length * length),
        compiler_params=params(60),
        name="attend",
    )(lengths, qkv, qkv, qkv)


def back_kernel(
    place_ref,
    len_ref,
    qa_ref,
    k_ref,
    v_ref,
    o_ref,
    do_ref,
    cos_ref,
    up_ref,
    down_ref,
    xt_ref,
    g_ref,
    sum_ref,
    theirs_ref,
    mine_ref,
    doa_ref,
    dqt_ref,
    acc_ref=None,
    *,
    block,
):
    length = k_ref.shape[0]
    pair, row, rows_last = pl.program_id(0), pl.program_id(1), pl.num_programs(1) - 1
    live = len_ref[row]
    lane = lax.broadcasted_iota(jnp.int32, (length, 128), 1)
    do = do_ref[...].astype(F32)
    prod = do * o_ref[...].astype(F32)
    for h in range(2):
        own = (lane // HEAD) == h
        aux = HEAD * (1 - h)
        shift = -jnp.sum(jnp.where(own, prod, 0.0), -1, keepdims=True)
        hi = shift.astype(BF).astype(F32)
        extra = jnp.where(lane == aux, hi, jnp.where(lane == aux + 1, shift - hi, 0.0))
        doa_ref[h] = jnp.where(own, do, extra).astype(BF)
    lane = lax.broadcasted_iota(jnp.int32, (block, 128), 1)
    pos = lax.broadcasted_iota(jnp.int32, (block, 128), 0)
    dk_sum = jnp.zeros((1, 128), F32)
    dv_sum = jnp.zeros((1, 128), F32)
    for i in range(length // block):
        rows = slice(i * block, (i + 1) * block)
        k, v = k_ref[rows, :].astype(F32), v_ref[rows, :].astype(F32)
        kt = k.T.astype(BF)
        dks, dvs = [], []
        for h in range(2):
            own = (lane // HEAD) == h
            aux = HEAD * (1 - h)
            mask = jnp.where((lane == aux + 3) & (pos + i * block >= live), NEG_FILL, 0.0)
            ka = jnp.where(own, k, jnp.where((lane >= aux) & (lane < aux + 3), 1.0, mask)).astype(BF)
            va = jnp.where(own, v, jnp.where((lane >= aux) & (lane < aux + 2), 1.0, 0.0)).astype(BF)
            qa, doa = qa_ref[h], doa_ref[h]
            p = jnp.exp(dot_nt(ka, qa))
            ds = (p * dot_nt(va, doa)).astype(BF)
            dvs.append(dot_nn(p.astype(BF), doa))
            dks.append(dot_nn(ds, qa))
            dqt = dot_nn(kt[h * HEAD : (h + 1) * HEAD, :], ds)
            if i == 0:
                dqt_ref[h * HEAD : (h + 1) * HEAD, :] = dqt
            else:
                dqt_ref[h * HEAD : (h + 1) * HEAD, :] += dqt
        dk = jnp.where(lane < HEAD, dks[0], dks[1])
        dk = rotate(dk, cos_ref[rows, :], -up_ref[rows, :], -down_ref[rows, :]).astype(BF)
        dv = jnp.where(lane < HEAD, dvs[0], dvs[1]).astype(BF)
        g_ref[rows, 128:256] = dk
        g_ref[rows, 256:384] = dv
        dk_sum += jnp.sum(dk.astype(F32), 0, keepdims=True)
        dv_sum += jnp.sum(dv.astype(F32), 0, keepdims=True)
    dq = rotate(dqt_ref[...].T * (1.0 / math.sqrt(HEAD)), cos_ref[...], -up_ref[...], -down_ref[...]).astype(BF)
    g_ref[:, 0:128] = dq
    sum_ref[...] = jnp.concatenate([jnp.sum(dq.astype(F32), 0, keepdims=True), dk_sum, dv_sum], -1)
    acc = dot_nn(xt_ref[...], g_ref[...])
    r = acc.shape[0] // 16

    def put(acc, ref, order):
        for slot in range(4):
            for kf in range(4):
                rows = slice((slot * 4 + kf) * r, (slot * 4 + kf + 1) * r)
                ref[order[slot], kf] = acc[rows].astype(BF)

    if acc_ref is not None:
        acc_ref[...] = jnp.where(row == 0, 0.0, acc_ref[...]) + acc

    @pl.when((pair == 0) & (row == rows_last))
    def _():
        put(acc if acc_ref is None else acc_ref[...], theirs_ref, TURNED)

    @pl.when((pair == 1) & (row == rows_last))
    def _():
        put(acc if acc_ref is None else acc_ref[...], mine_ref, (0, 1, 2, 3))


def back_call(place, lengths, seen, qkv, dattn, xt, tabs, length, span, block=256):
    attn, qa = seen
    n, width = qkv.shape
    rows, pairs = n // length, width // 384
    model = width // 3
    which = lambda p, place: jnp.where(p == 0, 1 - place[2], place[2])
    one = lambda off: pl.BlockSpec((length, 128), lambda p, b, place, _: (b, off * pairs + 2 * span + which(p, place)))
    table = pl.BlockSpec((length, 128), lambda *_: (0, 0))
    part = pl.BlockSpec((4, 4, model // 16, 384), lambda *_: (0, 0, 0, 0))
    spec = pltpu.PrefetchScalarGridSpec(
        num_scalar_prefetch=2,
        grid=(2, rows),
        in_specs=[
            pl.BlockSpec((None, 2, length, 128), lambda p, b, place, _: (b, which(p, place), 0, 0)),
            one(1),
            one(2),
            pl.BlockSpec((length, 128), lambda p, b, place, _: (b, which(p, place))),
            one(0),
            table,
            table,
            table,
            pl.BlockSpec((model, length), lambda p, b, *_: (0, b)),
        ],
        out_specs=[
            pl.BlockSpec((length, 384), lambda p, b, place, _: (b, which(p, place))),
            pl.BlockSpec((None, None, 1, 384), lambda p, b, place, _: (b, which(p, place), 0, 0)),
            part,
            part,
        ],
        scratch_shapes=[pltpu.VMEM((2, length, 128), BF), pltpu.VMEM((128, length), F32)]
        + ([pltpu.VMEM((model, 384), F32)] if rows > 1 else []),
    )
    return pl.pallas_call(
        functools.partial(back_kernel, block=block),
        grid_spec=spec,
        out_shape=[
            jax.ShapeDtypeStruct((n, 768), BF),
            jax.ShapeDtypeStruct((rows, 2, 1, 384), F32),
            jax.ShapeDtypeStruct((4, 4, model // 16, 384), BF),
            jax.ShapeDtypeStruct((4, 4, model // 16, 384), BF),
        ],
        cost_estimate=cost(rows * 80 * length * length * 128, 24 * n * 128, rows * 4 * length * length),
        compiler_params=params(60),
        name="attend_back",
    )(place, lengths, qa, qkv, qkv, attn, dattn, *tabs, xt)


def norm_forward(u):
    center = u - jnp.mean(u, -1, keepdims=True)
    inverse = lax.rsqrt(jnp.mean(center * center, -1, keepdims=True) + NORM_EPS)
    return center * inverse, inverse


def norm_backward(incoming, normed, inverse, gain):
    scaled = incoming * gain
    mean = jnp.mean(scaled, -1, keepdims=True)
    return inverse * (scaled - mean - normed * jnp.mean(scaled * normed, -1, keepdims=True))


def adder(ref):
    def add(row, value, off=0):
        ref[row : row + 1, off : off + value.shape[1]] += jnp.sum(value, 0, keepdims=True)

    return add


def turn_columns(value, place, ref):
    f, j, c = place
    turned = value.T
    r = turned.shape[0] // 16
    for fb in range(4):
        for jb in range(4):
            start = pl.multiple_of((exchanged(j ^ jb, c) * 4 + (f ^ fb)) * r, 16)
            ref[pl.ds(start, r), :] = turned[(fb * 4 + jb) * r : (fb * 4 + jb + 1) * r].astype(BF)


def turn_halves(value, place, ref, cols):
    _, j, c = place
    turned = value.T
    r = turned.shape[0] // 8
    for cb in range(2):
        for jb in range(4):
            start = pl.multiple_of(((c ^ cb) * 4 + exchanged(j ^ jb, c)) * r, 16)
            ref[pl.ds(start, r), cols] = turned[(cb * 4 + jb) * r : (cb * 4 + jb + 1) * r].astype(BF)


def turn_kernel(place_ref, x_ref, o_ref):
    turn_columns(x_ref[...].astype(F32), place_of(place_ref), o_ref)


def turn_call(place, x, block=256):
    n, model = x.shape
    spec = pltpu.PrefetchScalarGridSpec(
        num_scalar_prefetch=1,
        grid=(n // block,),
        in_specs=[pl.BlockSpec((block, model), lambda i, _: (i, 0))],
        out_specs=pl.BlockSpec((model, block), lambda i, _: (0, i)),
    )
    return pl.pallas_call(
        turn_kernel,
        grid_spec=spec,
        out_shape=jax.ShapeDtypeStruct((model, n), BF),
        cost_estimate=cost(n * model, 4 * n * model),
        compiler_params=params(16),
        name="turn",
    )(place, x)


def ffn_kernel(*refs, length, chunk, attn, side, shrink, blocks):
    place_ref, len_ref, x_ref, cot_ref, v_ref = refs[:5]
    at_refs = refs[5 : 5 + attn]
    side_refs = refs[5 + attn : 5 + attn + side]
    shrink_refs = refs[5 + attn + side : 5 + attn + side + shrink]
    outs = refs[5 + attn + side + shrink :]
    out_ref, slope_ref, yt_ref, att_ref, r1_ref, dr2_ref, dvec_ref, theirs_ref, mine_ref = outs[:9]
    wo_ref, w1_ref, w2_ref, act_ref, dzt_ref, flat_o, flat_1, flat_2, sem_o, sem_1, sem_2 = outs[9:]
    step = pl.program_id(0)
    block, model = x_ref.shape
    ff = w1_ref.shape[1]
    per = length // block
    live = len_ref[jnp.minimum(step, blocks - 1) // per]
    place = place_of(place_ref)
    vec = lambda i: v_ref[i : i + 1, :]

    @pl.when(step == 0)
    def _():
        first = out_copies(place, side_refs, wo_ref, flat_o)
        second = expand_copies(place, side_refs, w1_ref, flat_1)
        third = shrink_copies(place, shrink_refs, w2_ref, flat_2)
        begin(first, sem_o)
        begin(second, sem_1)
        begin(third, sem_2)
        dvec_ref[...] = jnp.zeros_like(dvec_ref)
        finish(first, sem_o)
        own_part(place, first, wo_ref, flat_o)
        finish(second, sem_1)
        own_part(place, second, w1_ref, flat_1)
        finish(third, sem_2)
        own_part(place, third, w2_ref, flat_2)

    @pl.when(step < blocks)
    def _():
        here = pl.ds(pl.multiple_of(step * block, block), block)
        at = jnp.concatenate([ref[...] for ref in at_refs], -1)
        turn_columns(at.astype(F32), place, att_ref)
        r1 = x_ref[...].astype(F32) + (dot_nn(at, wo_ref[...]) + vec(7))
        r1_ref[...] = r1
        n1, _ = norm_forward(r1)
        y1 = n1 * vec(0) + vec(2)
        y1b = y1.astype(BF)
        turn_columns(y1, place, yt_ref)
        z = jnp.zeros((block, model), F32)
        for lo in range(0, ff, chunk):
            cols = slice(lo, lo + chunk)
            bias = v_ref[9 + lo // model : 10 + lo // model, lo % model : lo % model + chunk]
            pre = dot_nn(y1b, w1_ref[:, cols]) + bias
            phi = 0.5 * (1.0 + lax.erf(pre * ROOT_HALF))
            act = (pre * phi).astype(BF)
            act_ref[here, cols] = act
            slope_ref[:, cols] = (phi + pre * (jnp.exp(-0.5 * pre * pre) * INV_ROOT_TAU)).astype(BF)
            z = z + dot_nn(act, w2_ref[cols, :])
        r2 = y1 + (z + vec(8))
        n2, i2 = norm_forward(r2)
        out_ref[...] = (n2 * vec(1) + vec(3)).astype(BF)
        pos = lax.broadcasted_iota(jnp.int32, (block, model), 0) + (step % per) * block
        e = jnp.where(pos < live, cot_ref[...].astype(F32), 0.0)
        dr2 = norm_backward(e, n2, i2, vec(1))
        dr2_ref[...] = dr2
        turn_halves(dr2, place, dzt_ref, here)
        add = adder(dvec_ref)
        add(1, e * n2)
        add(3, e)
        add(8, dr2.astype(BF).astype(F32))

    @pl.when(step >= blocks)
    def _():
        kf = step - blocks
        width = ff // 4
        r = model // 8
        cols = pl.ds(pl.multiple_of((place[0] ^ kf) * width, 128), width)
        acc = dot_nn(dzt_ref[...], act_ref[:, cols])
        for slot in range(4):
            mine_ref[slot] = acc[slot * r : (slot + 1) * r].astype(BF)
            theirs_ref[TURNED[slot]] = acc[(4 + slot) * r : (5 + slot) * r].astype(BF)


def ffn_call(place, lengths, x, attn, cot, side, shrink, vec, length, block=256, chunk=768):
    n, model = x.shape
    ff = 4 * model
    blocks = n // block
    tok = pl.BlockSpec((block, model), lambda i, *_: (jnp.minimum(i, blocks - 1), 0))
    wide = pl.BlockSpec((block, ff), lambda i, *_: (jnp.minimum(i, blocks - 1), 0))
    small = pl.BlockSpec((13, model), lambda i, *_: (0, 0))
    turned = pl.BlockSpec((model, block), lambda i, *_: (0, jnp.minimum(i, blocks - 1)))
    grad = pl.BlockSpec((4, None, model // 8, ff // 4), lambda i, *_: (0, jnp.maximum(i - blocks, 0), 0, 0))
    spec = pltpu.PrefetchScalarGridSpec(
        num_scalar_prefetch=2,
        grid=(blocks + 4,),
        in_specs=[tok, tok, small]
        + [pl.BlockSpec((block, a.shape[1]), lambda i, *_: (jnp.minimum(i, blocks - 1), 0)) for a in attn]
        + [ANY] * (len(side) + len(shrink)),
        out_specs=[tok, wide, turned, turned, tok, tok, small, grad, grad],
        scratch_shapes=[
            pltpu.VMEM((model, model), BF),
            pltpu.VMEM((model, ff), BF),
            pltpu.VMEM((ff, model), BF),
            pltpu.VMEM((n, ff), BF),
            pltpu.VMEM((model, n), BF),
            pltpu.VMEM((model // 4, model), F32),
            pltpu.VMEM((model // 4, ff), F32),
            pltpu.VMEM((ff // 4, model), F32),
        ]
        + [pltpu.SemaphoreType.DMA((MOST,))] * 3,
    )
    s = lambda w, t: jax.ShapeDtypeStruct((n, w), t)
    flip = jax.ShapeDtypeStruct((model, n), BF)
    parts = jax.ShapeDtypeStruct((4, 4, model // 8, ff // 4), BF)
    return pl.pallas_call(
        functools.partial(
            ffn_kernel, length=length, chunk=chunk, attn=len(attn), side=len(side), shrink=len(shrink), blocks=blocks
        ),
        grid_spec=spec,
        out_shape=[
            s(model, BF),
            s(ff, BF),
            flip,
            flip,
            s(model, F32),
            s(model, F32),
            jax.ShapeDtypeStruct((13, model), F32),
            parts,
            parts,
        ],
        cost_estimate=cost(
            2 * n * (2 * model * model + 6 * model * ff), n * (model * 20 + ff * 4) + model * ff * 4, n * ff * 2
        ),
        compiler_params=params(60),
        name="ffn",
    )(place, lengths, x, cot, vec, *attn, *side, *shrink)


def ffn_back_kernel(*refs, chunk, side, shrink):
    place_ref, dr2_ref, slope_ref, r1_ref, v_ref = refs[:5]
    side_refs = refs[5 : 5 + side]
    shrink_refs = refs[5 + side : 5 + side + shrink]
    outs = refs[5 + side + shrink :]
    dpre_ref, dr1_ref, da_ref, dat_ref, dvec_ref = outs[:5]
    wo_ref, w1_ref, w2_ref, flat_o, flat_1, flat_2, sem_o, sem_1, sem_2 = outs[5:]
    step = pl.program_id(0)
    block, model = dr2_ref.shape
    ff = w1_ref.shape[1]
    place = place_of(place_ref)
    vec = lambda i: v_ref[i : i + 1, :]

    @pl.when(step == 0)
    def _():
        first = out_copies(place, side_refs, wo_ref, flat_o)
        second = expand_copies(place, side_refs, w1_ref, flat_1)
        third = shrink_copies(place, shrink_refs, w2_ref, flat_2)
        begin(third, sem_2)
        begin(second, sem_1)
        begin(first, sem_o)
        dvec_ref[...] = jnp.zeros_like(dvec_ref)
        finish(third, sem_2)
        own_part(place, third, w2_ref, flat_2)
        finish(second, sem_1)
        own_part(place, second, w1_ref, flat_1)
        finish(first, sem_o)
        own_part(place, first, wo_ref, flat_o)

    add = adder(dvec_ref)
    dy = dr2_ref[...]
    dz = dy.astype(BF)
    for lo in range(0, ff, chunk):
        cols = slice(lo, lo + chunk)
        dpre = (dot_nt(dz, w2_ref[cols, :]) * slope_ref[:, cols].astype(F32)).astype(BF)
        dpre_ref[:, cols] = dpre
        add(9 + lo // model, dpre.astype(F32), lo % model)
        dy = dy + dot_nt(dpre, w1_ref[:, cols])
    n1, i1 = norm_forward(r1_ref[...])
    add(0, dy * n1)
    add(2, dy)
    dr1 = norm_backward(dy, n1, i1, vec(0))
    dr1_ref[...] = dr1
    da = dr1.astype(BF)
    da_ref[...] = da
    add(7, da.astype(F32))
    dat_ref[...] = dot_nt(da, wo_ref[...]).astype(BF)


def ffn_back_call(place, dr2, slope, r1, side, shrink, vec, block=256, chunk=768):
    n, model = dr2.shape
    ff = 4 * model
    tok = pl.BlockSpec((block, model), lambda i, *_: (i, 0))
    wide = pl.BlockSpec((block, ff), lambda i, *_: (i, 0))
    small = pl.BlockSpec((13, model), lambda i, *_: (0, 0))
    spec = pltpu.PrefetchScalarGridSpec(
        num_scalar_prefetch=1,
        grid=(n // block,),
        in_specs=[tok, wide, tok, small] + [ANY] * (len(side) + len(shrink)),
        out_specs=[wide, tok, tok, tok, small],
        scratch_shapes=[
            pltpu.VMEM((model, model), BF),
            pltpu.VMEM((model, ff), BF),
            pltpu.VMEM((ff, model), BF),
            pltpu.VMEM((model // 4, model), F32),
            pltpu.VMEM((model // 4, ff), F32),
            pltpu.VMEM((ff // 4, model), F32),
        ]
        + [pltpu.SemaphoreType.DMA((MOST,))] * 3,
    )
    s = lambda w, t: jax.ShapeDtypeStruct((n, w), t)
    return pl.pallas_call(
        functools.partial(ffn_back_kernel, chunk=chunk, side=len(side), shrink=len(shrink)),
        grid_spec=spec,
        out_shape=[s(ff, BF), s(model, F32), s(model, BF), s(model, BF), jax.ShapeDtypeStruct((13, model), F32)],
        cost_estimate=cost(2 * n * (model * model + 2 * model * ff), n * (model * 18 + ff * 4) + model * ff * 4),
        compiler_params=params(60),
        name="ffn_back",
    )(place, dr2, slope, r1, vec, *side, *shrink)


def side_grad_kernel(place_ref, yt_ref, att_ref, dpre_ref, da_ref, theirs_ref, mine_ref, *, steps):
    step = pl.program_id(0)
    r = yt_ref.shape[0] // 16

    def put(acc, ref, order):
        for slot in range(4):
            for kf in range(4):
                rows = slice((slot * 4 + kf) * r, (slot * 4 + kf + 1) * r)
                ref[order[slot], kf, :, : acc.shape[1]] = acc[rows].astype(BF)

    for first, ref, order in ((0, theirs_ref, TURNED), (steps, mine_ref, (0, 1, 2, 3))):

        @pl.when((step >= first) & (step < first + steps - 1))
        def _(ref=ref, order=order):
            put(dot_nn(yt_ref[...], dpre_ref[...]), ref, order)

        @pl.when(step == first + steps - 1)
        def _(ref=ref, order=order):
            put(dot_nn(att_ref[...], da_ref[...]), ref, order)


def side_grad_call(place, yt, att, dpre, da, block=768):
    model, n = yt.shape
    half = dpre.shape[1] // 2
    steps = half // block + 1
    which = lambda i, place: jnp.where(i < steps, 1 - place[2], place[2])
    turned = pl.BlockSpec((model, n), lambda i, _: (0, 0))
    width = half + model // 2
    out = lambda first: pl.BlockSpec(
        (4, 4, model // 16, block), lambda i, _: (0, 0, 0, jnp.clip(i - first, 0, steps - 1))
    )
    spec = pltpu.PrefetchScalarGridSpec(
        num_scalar_prefetch=1,
        grid=(2 * steps,),
        in_specs=[
            turned,
            turned,
            pl.BlockSpec(
                (n, block), lambda i, place: (0, which(i, place) * (steps - 1) + jnp.minimum(i % steps, steps - 2))
            ),
            pl.BlockSpec((n, model // 2), lambda i, place: (0, which(i, place))),
        ],
        out_specs=[out(0), out(steps)],
    )
    return pl.pallas_call(
        functools.partial(side_grad_kernel, steps=steps),
        grid_spec=spec,
        out_shape=[jax.ShapeDtypeStruct((4, 4, model // 16, width), BF)] * 2,
        cost_estimate=cost(4 * n * model * width, 4 * (n * model + n * width + model * width)),
        compiler_params=params(60),
        name="side_grad",
    )(place, yt, att, dpre, da)


def token_kernel(*refs, pieces, parts):
    place_ref, dr1_ref = refs[:2]
    g_refs = refs[2 : 2 + parts]
    w_refs = refs[2 + parts : 2 + parts + pieces]
    o_ref, w_ref, flat_ref, sems = refs[2 + parts + pieces :]
    model = w_ref.shape[0]

    @pl.when(pl.program_id(0) == 0)
    def _():
        copies = in_copies(place_of(place_ref), w_refs, w_ref, flat_ref)
        begin(copies, sems)
        finish(copies, sems)
        own_part(place_of(place_ref), copies, w_ref, flat_ref)

    total = dr1_ref[...]
    for t in range(3):
        tiles = [ref[:, lo + t * 128 : lo + (t + 1) * 128] for ref in g_refs for lo in range(0, ref.shape[1], 384)]
        total = total + dot_nt(jnp.concatenate(tiles, -1), w_ref[:, t * model : (t + 1) * model])
    o_ref[...] = total.astype(BF)


def token_call(place, dr1, grads, weight, block=256):
    n, model = dr1.shape
    tok = lambda w: pl.BlockSpec((block, w), lambda i, _: (i, 0))
    spec = pltpu.PrefetchScalarGridSpec(
        num_scalar_prefetch=1,
        grid=(n // block,),
        in_specs=[tok(model)] + [tok(g.shape[1]) for g in grads] + [ANY] * len(weight),
        out_specs=tok(model),
        scratch_shapes=[
            pltpu.VMEM((model, 3 * model), BF),
            pltpu.VMEM((model // 4, 3 * model), F32),
            pltpu.SemaphoreType.DMA((MOST,)),
        ],
    )
    return pl.pallas_call(
        functools.partial(token_kernel, pieces=len(weight), parts=len(grads)),
        grid_spec=spec,
        out_shape=jax.ShapeDtypeStruct((n, model), BF),
        cost_estimate=cost(6 * n * model * model, n * model * 12 + 6 * model * model),
        compiler_params=params(60),
        name="token_gradient",
    )(place, dr1, *grads, *weight)


def picked(refs, count, extra):
    at = 0
    for i in range(count):
        width = refs[i].shape[-1]
        yield refs[i], (refs[count + i] if i < count - extra else None), slice(at, at + width)
        at += width


def add_first_kernel(*refs, count, extra):
    out = refs[-1]
    for mine, recv, cols in picked(refs, count, extra):
        total = mine[...].astype(F32)
        if recv is not None:
            total = total + recv[...].astype(F32)
        out[:, :, :, cols] = total.astype(BF)


def add_first(mine, recv):
    shapes = [m.shape for m in mine]
    r, width = shapes[0][2], sum(s[3] for s in shapes)
    block = lambda w: pl.BlockSpec((2, 2, r, w), lambda k: (1, k, 0, 0))
    return pl.pallas_call(
        functools.partial(add_first_kernel, count=len(mine), extra=len(mine) - len(recv)),
        grid=(2,),
        in_specs=[block(s[3]) for s in shapes + shapes[: len(recv)]],
        out_specs=pl.BlockSpec((2, 2, r, width), lambda k: (0, k, 0, 0)),
        out_shape=jax.ShapeDtypeStruct((2, 4, r, width), BF),
        cost_estimate=cost(8 * r * width, 48 * r * width),
        compiler_params=params(16),
        name="add_first",
    )(*mine, *recv)


def add_second_kernel(*refs, count, extra):
    got, out = refs[-2:]
    for mine, recv, cols in picked(refs, count, extra):
        total = mine[...].astype(F32) + got[:, :, cols].astype(F32)
        if recv is not None:
            total = total + recv[...].astype(F32)
        out[:, :, cols] = total.astype(BF)


def add_second(mine, recv, got):
    shapes = [m.shape for m in mine]
    _, _, r, width = got.shape
    block = lambda w: pl.BlockSpec((None, 4, r, w), lambda k: (1, 0, 0, 0))
    return pl.pallas_call(
        functools.partial(add_second_kernel, count=len(mine), extra=len(mine) - len(recv)),
        grid=(1,),
        in_specs=[block(s[3]) for s in shapes + shapes[: len(recv)]] + [block(width)],
        out_specs=pl.BlockSpec((4, r, width), lambda k: (0, 0, 0)),
        out_shape=jax.ShapeDtypeStruct((4, r, width), BF),
        cost_estimate=cost(12 * r * width, 32 * r * width),
        compiler_params=params(16),
        name="add_second",
    )(*mine, *recv, got)


def add_z_kernel(place_ref, *refs, count, extra, split):
    ins = 2 * count - extra + 2
    got, last = refs[ins - 2 : ins]
    outs = refs[ins:]
    f = place_ref[0]
    for mine, recv, cols in picked(refs, count, extra):
        for kf in range(4):
            total = mine[kf].astype(F32) + got[kf, :, cols].astype(F32) + last[kf, :, cols].astype(F32)
            if recv is not None:
                total = total + recv[kf].astype(F32)
            if split:
                outs[kf][:, cols] = total.astype(BF)
            else:
                outs[0][f ^ kf, :, cols] = total.astype(BF)


def add_z(place, mine, recv, got, last, split):
    shapes = [m.shape for m in mine]
    _, _, r, width = got.shape
    block = lambda w: pl.BlockSpec((None, 4, r, w), lambda *_: (0, 0, 0, 0))
    if split:
        outs = [pl.BlockSpec((r, width), lambda *_: (0, 0))] * 4
        shape = [jax.ShapeDtypeStruct((r, width), BF)] * 4
    else:
        outs = pl.BlockSpec((4, r, width), lambda *_: (0, 0, 0))
        shape = jax.ShapeDtypeStruct((4, r, width), BF)
    spec = pltpu.PrefetchScalarGridSpec(
        num_scalar_prefetch=1,
        grid=(1,),
        in_specs=[block(s[3]) for s in shapes + shapes[: len(recv)]]
        + [block(width), pl.BlockSpec((4, r, width), lambda *_: (0, 0, 0))],
        out_specs=outs,
    )
    return pl.pallas_call(
        functools.partial(add_z_kernel, count=len(mine), extra=len(mine) - len(recv), split=split),
        grid_spec=spec,
        out_shape=shape,
        cost_estimate=cost(16 * r * width, 40 * r * width),
        compiler_params=params(20),
        name="add_z",
    )(place, *mine, *recv, got, last)


def over_z_sum(parts):
    return lax.psum_scatter(parts, "fsdp", scatter_dimension=0)


def add_all_kernel(*refs):
    total = refs[0][...].astype(F32)
    for ref in refs[1:-1]:
        total = total + ref[...].astype(F32)
    refs[-1][...] = total.astype(BF)


def add_all(*parts):
    return pl.pallas_call(
        add_all_kernel,
        out_shape=jax.ShapeDtypeStruct(parts[0].shape, BF),
        cost_estimate=cost(4 * parts[0].size, 10 * parts[0].size),
        compiler_params=params(8),
        name="add_all",
    )(*parts)


def send_z(own, one, two, three):
    return own, cross(one, 1), cross(two, 2), cross(three, 3)


def over_chips(total):
    return total, swap(total, 2), swap(total, 4), swap(total, 6)


def both_cores(chips):
    return (*chips, *(swap_core(part) for part in chips))


def vector_parts_kernel(place_ref, one_ref, two_ref, *refs):
    sums, (theirs_ref, mine_ref) = refs[:-2], refs[-2:]
    f, j, c = place_of(place_ref)
    rest = one_ref[...] + two_ref[...]
    heads = []
    for t in range(3):
        cols = slice(t * 128, (t + 1) * 128)
        tiles = [jnp.sum(ref[:, pair, :, cols], 0) for ref in sums for pair in range(2)]
        heads.append(jnp.concatenate(tiles, -1))
    value = jnp.concatenate([rest[:4], *heads, rest[7:]], 0)
    theirs_ref[...] = jnp.zeros_like(theirs_ref)
    mine_ref[...] = jnp.zeros_like(mine_ref)
    rows, model = value.shape
    width = model // 16
    for fb in range(4):
        for jb in range(4):
            lo = (fb * 4 + jb) * width
            part = value[:, lo : lo + width].astype(BF)
            mine_ref[exchanged(j ^ jb, c), f ^ fb, :rows, :width] = part
            theirs_ref[exchanged(j ^ jb, 1 - c), f ^ fb, :rows, :width] = part


def vector_parts(place, one, two, sums, r):
    whole = lambda a: pl.BlockSpec(a.shape, lambda *_, k=a.ndim: (0,) * k)
    spec = pltpu.PrefetchScalarGridSpec(
        num_scalar_prefetch=1,
        grid=(1,),
        in_specs=[whole(a) for a in (one, two, *sums)],
        out_specs=[pl.BlockSpec((4, 4, r, 128), lambda *_: (0, 0, 0, 0))] * 2,
    )
    return pl.pallas_call(
        vector_parts_kernel,
        grid_spec=spec,
        out_shape=[jax.ShapeDtypeStruct((4, 4, r, 128), BF)] * 2,
        compiler_params=params(8),
        name="vector_parts",
    )(place, one, two, *sums)


def adam_update(master, moment, square, gradient, rate, decay):
    momentum = BETA_ONE * moment + (1.0 - BETA_ONE) * gradient
    squares = BETA_TWO * square + (1.0 - BETA_TWO) * gradient * gradient
    corrected = momentum / (1.0 - BETA_ONE**STEP)
    spread = jnp.sqrt(squares / (1.0 - BETA_TWO**STEP))
    return (master - rate * (corrected / (spread + ADAM_EPS) + decay * master), momentum, squares)


def adam_block(state, outs, g, rate):
    w, m, s = (ref[...] for ref in state)
    for ref, value in zip(outs, adam_update(w, m, s, g, rate, WEIGHT_DECAY)):
        ref[...] = value


def adam_side_kernel(*refs, weights, moves, rates):
    state, grad, outs = refs[: 3 * weights], refs[3 * weights], refs[3 * weights + 1 : 6 * weights + 1]
    flats = refs[6 * weights + 1 :]
    step = pl.program_id(0)
    rows = state[0].shape[0]

    @pl.when(step == 0)
    def _():
        r = grad.shape[1]
        for weight, src, width in moves:
            for d in range(8):
                to = slice((d % 2) * width, (d % 2 + 1) * width)
                flats[weight][d // 2 * r : (d // 2 + 1) * r, to] = grad[d, :, src : src + width]

    here = pl.ds(pl.multiple_of(step * rows, rows), rows)
    for i in range(weights):
        cut = slice(3 * i, 3 * i + 3)
        adam_block(state[cut], outs[cut], flats[i][here, :].astype(F32), rates[i])


def adam_side_call(states, grad, moves, rates, steps=6):
    rows = states[0][0].shape[0] // steps
    block = lambda a: pl.BlockSpec((rows, a.shape[1]), lambda i: (i, 0))
    flat = [a for state in states for a in state]
    size = sum(a.size for a in flat)
    return pl.pallas_call(
        functools.partial(adam_side_kernel, weights=len(states), moves=tuple(moves), rates=tuple(rates)),
        grid=(steps,),
        in_specs=[block(a) for a in flat] + [pl.BlockSpec(grad.shape, lambda i: (0, 0, 0))],
        out_specs=[block(a) for a in flat],
        scratch_shapes=[pltpu.VMEM(state[0].shape, BF) for state in states],
        out_shape=[jax.ShapeDtypeStruct(a.shape, F32) for a in flat],
        cost_estimate=cost(size * 4, size * 9),
        compiler_params=params(60),
        name="adam_side",
    )(*flat, grad)


def adam_in_kernel(*refs, moves, rate):
    place_ref, state, grads, outs, flat = refs[0], refs[1:4], refs[4:12], refs[12:15], refs[15]
    _, j, c = place_of(place_ref)
    step = pl.program_id(0)
    rows = state[0].shape[0]

    @pl.when(step == 0)
    def _():
        for i, ref in enumerate(grads):
            half = c if i < 4 else 1 - c
            r = ref.shape[0]
            here = pl.ds(pl.multiple_of((j ^ (i % 4)) * r, 16), r)
            for src, to, stride in moves:
                cols = pl.ds(pl.multiple_of(to + half * stride, 128), 128)
                flat[here, cols] = ref[:, src : src + 128]

    here = pl.ds(pl.multiple_of(step * rows, rows), rows)
    adam_block(state, outs, flat[here, :].astype(F32), rate)


def adam_in_call(place, state, grads, moves, rate, steps=6):
    rows = state[0].shape[0] // steps
    block = pl.BlockSpec((rows, state[0].shape[1]), lambda i, _: (i, 0))
    spec = pltpu.PrefetchScalarGridSpec(
        num_scalar_prefetch=1,
        grid=(steps,),
        in_specs=[block] * 3 + [pl.BlockSpec(g.shape, lambda i, _: (0, 0)) for g in grads],
        out_specs=[block] * 3,
        scratch_shapes=[pltpu.VMEM(state[0].shape, BF)],
    )
    return pl.pallas_call(
        functools.partial(adam_in_kernel, moves=tuple(moves), rate=rate),
        grid_spec=spec,
        out_shape=[jax.ShapeDtypeStruct(state[0].shape, F32)] * 3,
        cost_estimate=cost(state[0].size * 12, state[0].size * 28),
        compiler_params=params(60),
        name="adam_in",
    )(place, *state, *grads)


def adam_turned_kernel(*refs, rate):
    state, grad, outs, (flat_ref, g_ref) = refs[:3], refs[3], refs[4:7], refs[7:]
    step = pl.program_id(0)
    rows = state[0].shape[0]

    @pl.when(step == 0)
    def _():
        r = grad.shape[1]
        for d in range(8):
            at = (d % 2) * 4 + d // 2
            flat_ref[at * r : (at + 1) * r, :] = grad[d].astype(F32)
        g_ref[...] = flat_ref[...].T

    adam_block(state, outs, g_ref[pl.ds(pl.multiple_of(step * rows, rows), rows), :], rate)


def adam_turned_call(state, grad, rate, steps=8):
    total, cols = state[0].shape
    block = pl.BlockSpec((total // steps, cols), lambda i: (i, 0))
    return pl.pallas_call(
        functools.partial(adam_turned_kernel, rate=rate),
        grid=(steps,),
        in_specs=[block] * 3 + [pl.BlockSpec(grad.shape, lambda i: (0, 0, 0))],
        out_specs=[block] * 3,
        scratch_shapes=[pltpu.VMEM((cols, total), F32), pltpu.VMEM((total, cols), F32)],
        out_shape=[jax.ShapeDtypeStruct(state[0].shape, F32)] * 3,
        cost_estimate=cost(total * cols * 12, total * cols * 28),
        compiler_params=params(60),
        name="adam_turned",
    )(*state, grad)


def vector_rows(rest, sums):
    heads = jnp.concatenate([jnp.sum(s, 0) for s in sums], 0).reshape(-1, 3, 128)
    heads = heads.transpose(1, 0, 2).reshape(3, -1)
    return jnp.concatenate([rest[:4], heads, rest[7:]], 0)


def local(
    tokens,
    cotangent,
    lengths,
    inward_weight,
    inward_moment,
    inward_square,
    outward_weight,
    outward_moment,
    outward_square,
    expand_weight,
    expand_moment,
    expand_square,
    shrink_weight,
    shrink_moment,
    shrink_square,
    vectors,
    vector_moment,
    vector_square,
    sliced,
):
    _, length, model = tokens.shape
    x, cot = tokens.reshape(-1, model), cotangent.reshape(-1, model)
    tabs = tables(length)
    ff = 4 * model
    pairs = model // 128
    inward = (inward_weight, inward_moment, inward_square)
    outward = (outward_weight, outward_moment, outward_square)
    expand = (expand_weight, expand_moment, expand_square)
    shrink = (shrink_weight, shrink_moment, shrink_square)
    vector = (vectors, vector_moment, vector_square)
    rate_d, rate_o, rate_f = 1.0 / math.sqrt(model), 1.0 / math.sqrt(OUT_FAN), 1.0 / math.sqrt(ff)
    f, d = lax.axis_index("fsdp"), lax.axis_index("dp")
    j, c = d // 2, d % 2
    place = jnp.stack([f, j, c]).astype(jnp.int32) if sliced else jnp.zeros((3,), jnp.int32)
    spans = [(0, 2), (2, 2), (4, 2)]

    if not sliced:
        low = [w.astype(BF) for w in (inward_weight, outward_weight, expand_weight, shrink_weight, vectors)]
        whole = [lax.all_gather(w, "fsdp", axis=0, tiled=True) for w in low[:4]]
        in_pieces, side_pieces, shrink_pieces = (whole[0],), (whole[1], whole[2]), (whole[3],)
        vec = lax.all_gather(low[4], "fsdp", axis=1, tiled=True).astype(F32)
        xt = turn_call(place, x)
        qkv = qkv_call(place, x, in_pieces, vec[4:7].reshape(1, -1), tabs, length)
        seen = [attend_call(lengths, qkv, length, *span) for span in spans]
        out, slope, yt, att, r1, dr2, vec_two, far, near = ffn_call(
            place, lengths, x, [a for a, _ in seen], cot, side_pieces, shrink_pieces, vec, length
        )
        order = jnp.array(TURNED)
        shrink_grad = jnp.concatenate([near, far[order]]).transpose(1, 3, 0, 2).reshape(ff, model)
        dpre, dr1, da, dattn, vec_one = ffn_back_call(place, dr2, slope, r1, side_pieces, shrink_pieces, vec)
        far, near = side_grad_call(place, yt, att, dpre, da)
        both = jnp.stack([near, far[order]]).transpose(2, 1, 3, 0, 4).reshape(model, 2, -1)
        expand_grad = both[:, :, : ff // 2].reshape(model, ff)
        outward_grad = both[:, :, ff // 2 :].reshape(model, model)
        backs = [back_call(place, lengths, seen[i], qkv, dattn, xt, tabs, length, i) for i in range(len(spans))]
        token_gradient = token_call(place, dr1, [b[0] for b in backs], in_pieces)
        parts = jnp.stack([part for _, _, far, near in backs for part in (near, far[order])])
        parts = parts.transpose(2, 1, 3, 0, 4).reshape(model, pairs, 3, 128)
        inward_grad = parts.transpose(0, 2, 1, 3).reshape(model, 3 * model)

        def reduced(g, axis=0):
            return lax.psum(lax.psum_scatter(g, "fsdp", scatter_dimension=axis, tiled=True).astype(F32), "dp")

        inward_new = adam_update(*inward, reduced(inward_grad), rate_d, WEIGHT_DECAY)
        outward_new = adam_update(*outward, reduced(outward_grad), rate_o, WEIGHT_DECAY)
        expand_new = adam_update(*expand, reduced(expand_grad), rate_d, WEIGHT_DECAY)
        shrink_new = adam_update(*shrink, reduced(shrink_grad), rate_f, WEIGHT_DECAY)
        vec_sum = reduced(vector_rows(vec_one + vec_two, [b[1] for b in backs]), 1)
    else:
        shard = model // 4
        r = shard // 4

        def columns(w):
            half = w.shape[1] // 2
            return lax.dynamic_slice(w, (j * r, c * half), (r, half))

        def rows(w):
            r = w.shape[0] // 8
            return lax.dynamic_slice(w, ((c * 4 + j) * r, 0), (r, w.shape[1]))

        part_in = columns(inward_weight).astype(BF)
        part_side = jnp.concatenate([columns(outward_weight), columns(expand_weight)], -1).astype(BF)
        part_shrink = rows(shrink_weight).astype(BF)
        low_vec = vectors.astype(BF)
        z_in = after(jnp.stack(over_z(part_in)), part_side, part_shrink, low_vec)
        first_in, second_in = swap_first(z_in), swap_second(z_in)
        z_side = over_z(after(part_side, z_in))
        first_in, second_in = after((first_in, second_in))
        third_in = swap_second(after(first_in, second_in))
        z_vec = over_z(after(low_vec, first_in))
        xt = turn_call(place, after(x, first_in))
        third_in = after(third_in, xt)
        in_pieces = (inward_weight, *both_cores((z_in, second_in, first_in, third_in)))
        by = (low_vec, *z_vec)
        ordered = []
        for at in range(4):
            k = f ^ at
            ordered.append(jnp.where(k == 0, by[0], jnp.where(k == 1, by[1], jnp.where(k == 2, by[2], by[3]))))
        vec = jnp.concatenate(ordered, 1).astype(F32)
        z_side = jnp.stack(after(z_side, third_in))
        first_side, second_side = swap_first(z_side), swap_second(z_side)
        z_shrink = over_z(after(part_shrink, z_side))
        qkv = qkv_call(place, x, after(in_pieces, z_side), vec[4:7].reshape(1, -1), tabs, length)
        first_side, second_side = after((first_side, second_side), qkv)
        third_side = swap_second(first_side)
        side_near = (z_side, second_side, first_side)
        side_far = tuple(swap_core(part) for part in side_near)
        seen = [attend_call(lengths, after(qkv, first_side, second_side), length, *spans[0])]
        third_side = after(third_side, seen[0])
        z_shrink = jnp.stack(after(z_shrink, third_side))
        first_shrink, second_shrink = swap_first(z_shrink), swap_second(z_shrink)
        side_pieces = (outward_weight, expand_weight, *side_near, third_side, *side_far, swap_core(third_side))
        seen.append(attend_call(lengths, after(qkv, third_side, z_shrink), length, *spans[1]))
        first_shrink, second_shrink = after((first_shrink, second_shrink), seen[1])
        third_shrink = swap_second(after(first_shrink, second_shrink))
        shrink_near = (z_shrink, second_shrink, first_shrink)
        shrink_far = tuple(swap_core(part) for part in shrink_near)
        seen.append(attend_call(lengths, after(qkv, first_shrink, second_shrink), length, *spans[2]))
        third_shrink = after(third_shrink, seen[2])
        shrink_pieces = (shrink_weight, *shrink_near, third_shrink, *shrink_far, swap_core(third_shrink))

        out, slope, yt, att, r1, dr2, vec_two, theirs_s, mine_s = ffn_call(
            place, lengths, x, [a for a, _ in seen], cot, side_pieces, shrink_pieces, vec, length
        )
        recv_s = swap_core(theirs_s)
        dpre, dr1, da, dattn, vec_one = ffn_back_call(place, dr2, slope, r1, side_pieces, shrink_pieces, vec)

        def back(span, *wait):
            return back_call(place, lengths, seen[span], qkv, after(dattn, *wait), xt, tabs, length, span)

        recv_s = after(recv_s, dattn)
        to_s = add_first([mine_s], [recv_s])
        got_s = swap_first(to_s)
        theirs_d, mine_d = side_grad_call(place, yt, att, after(dpre, to_s), da)
        got_s = after(got_s, theirs_d)
        on_s = add_second([mine_s], [recv_s], got_s)
        last_s = swap_second(on_s)
        recv_d = swap_core(after(theirs_d, on_s))
        g0, sum0, theirs_0, mine_0 = back(0, on_s)
        last_s, recv_d = after((last_s, recv_d), g0)
        z_s = add_z(place, [mine_s], [recv_s], got_s, last_s, False)
        part_s = over_z_sum(z_s)
        to_d = add_first([mine_d], [after(recv_d, z_s)])
        got_d = swap_first(to_d)
        recv_0 = swap_core(after(theirs_0, to_d))
        g1, sum1, theirs_1, mine_1 = back(1, to_d)
        got_d, part_s, recv_0 = after((got_d, part_s, recv_0), g1)
        on_d = add_second([mine_d], [recv_d], got_d)
        last_d = swap_second(on_d)
        recv_1 = swap_core(after(theirs_1, on_d))
        sum_s = lax.all_gather(after(part_s, on_d), "dp")
        g2, sum2, theirs_2, mine_2 = back(2, on_d)
        last_d, recv_1, theirs_2, sum_s = after((last_d, recv_1, theirs_2, sum_s), g2)
        recv_2 = swap_core(theirs_2)
        vec_one, vec_two = after((vec_one, vec_two), last_d)
        theirs_v, mine_v = vector_parts(place, vec_one, vec_two, [sum0, sum1, sum2], r)
        mine_e = [mine_0, mine_1, mine_2, mine_v]
        recv_e = [recv_0, recv_1, after(recv_2, theirs_v), swap_core(theirs_v)]
        to_e = add_first(mine_e, recv_e)
        got_e = swap_first(to_e)
        z_d = add_z(place, [mine_d], [recv_d], got_d, after(last_d, to_e), False)
        part_d = over_z_sum(z_d)
        token_gradient = token_call(place, after(dr1, z_d), [g0, g1, g2], in_pieces)
        got_e = after(got_e, token_gradient)
        on_e = add_second(mine_e, recv_e, got_e)
        last_e = swap_second(on_e)
        sum_d = lax.all_gather(after(part_d, on_e), "dp")
        shrink_new = adam_turned_call((after(shrink[0], on_e), *shrink[1:]), sum_s, rate_f)
        last_e = after(last_e, shrink_new[0])
        z_e = send_z(*add_z(place, mine_e, recv_e, got_e, last_e, True))
        moves = [(0, ff // 2, model // 2), (1, 0, ff // 2)]
        sum_e = over_chips(add_all(*z_e))
        side_states = [(after(outward[0], sum_e[0]), *outward[1:]), expand]
        side_new = adam_side_call(side_states, sum_d, moves, [rate_o, rate_d])
        outward_new, expand_new = side_new[:3], side_new[3:]
        sum_e = after(sum_e, side_new[0])
        width = 3 * model // 2
        picks = [part[: vectors.shape[0], width : width + r] for part in sum_e]
        ordered = []
        for at in range(4):
            k = j ^ at
            ordered.append(
                jnp.where(k == 0, picks[0], jnp.where(k == 1, picks[1], jnp.where(k == 2, picks[2], picks[3])))
            )
        vec_sum = jnp.concatenate(ordered, 1).astype(F32)
        moves = []
        for span in range(3):
            for t in range(3):
                moves.append((span * 384 + t * 128, t * model + span * 256, 128))
        inward_new = adam_in_call(place, inward, both_cores(sum_e), moves, rate_d)
    vector_new = adam_update(*vector, vec_sum, 0.5, 0.0)
    return (
        out.reshape(tokens.shape),
        token_gradient.reshape(tokens.shape),
        *inward_new,
        *outward_new,
        *expand_new,
        *shrink_new,
        *vector_new,
    )


def solution(mesh):
    both = P(("dp", "fsdp"), None, None)
    in_specs = (both, both, P(("dp", "fsdp"))) + (P("fsdp", None),) * 12 + (P(None, "fsdp"),) * 3
    out_specs = (both, both) + (P("fsdp", None),) * 12 + (P(None, "fsdp"),) * 3
    sliced = mesh.shape["dp"] == 8 and mesh.shape["fsdp"] == 4
    step = functools.partial(local, sliced=sliced)
    return jax.shard_map(step, mesh=mesh, in_specs=in_specs, out_specs=out_specs, check_vma=False)
```

```python
import functools
import math

import jax
import jax.numpy as jnp
import numpy as np
from jax import lax
from jax.experimental import pallas as pl
from jax.experimental.pallas import tpu as pltpu
from jax.sharding import PartitionSpec as P

BF = jnp.bfloat16
F32 = jnp.float32
HEAD = 64
STEP = 10
OUT_FAN = 3
BETA_ONE = 0.5
BETA_TWO = 0.5
ADAM_EPS = 1e-08
WEIGHT_DECAY = 0.01
NORM_EPS = 1e-12
NEG_FILL = -1000000000.0
ROOT_HALF = 0.7071067811865476
INV_ROOT_TAU = 0.3989422804014327
ANY = pl.BlockSpec(memory_space=pl.ANY)


def dot_nn(a, b):
    return lax.dot_general(a, b, (((1,), (0,)), ((), ())), preferred_element_type=F32)


def dot_nt(a, b):
    return lax.dot_general(a, b, (((1,), (1,)), ((), ())), preferred_element_type=F32)


def dot_tn(a, b):
    return lax.dot_general(a, b, (((0,), (0,)), ((), ())), preferred_element_type=F32)


def params():
    return pltpu.CompilerParams(vmem_limit_bytes=64 * 1024 * 1024)


def cost(flops, moved, trans=0):
    return pl.CostEstimate(flops=int(flops), bytes_accessed=int(moved), transcendentals=int(trans))


def swap(x, even, odd=None):
    odd = even if odd is None else odd
    return lax.ppermute(x, "dp", [(i, i ^ (odd if i % 2 else even)) for i in range(8)])


def swap_core(x):
    return swap(x, 1)


def swap_first(x):
    return swap(x, 4, 2)


def swap_second(x):
    return swap(x, 2, 4)


def cross(x, bit):
    return lax.ppermute(x, "fsdp", [(i, i ^ bit) for i in range(4)])


def over_z(part):
    return tuple(cross(part, k) for k in (1, 2, 3))


def after(x, *others):
    return lax.optimization_barrier((x, *others))[0]


TURNED = (0, 2, 1, 3)


def exchanged(k, c):
    return jnp.where(c == 0, k, (k & 1) * 2 + (k >> 1))


def column_copies(place, own, pieces, dst, flat, first=0, staged=True):
    f, j, c = place
    rows, cols = own.shape
    r, h = rows // 4, cols // 2
    out = [(own, flat)]
    for refs, half in ((pieces[:4], c), (pieces[4:], 1 - c)):
        for slot, ref in enumerate(refs):
            kj = exchanged(slot, half) if staged else slot
            for kf in range(1, 4):
                start = pl.multiple_of((f ^ kf) * rows + (j ^ kj) * r, 16)
                at = dst.at[pl.ds(start, r), pl.ds(pl.multiple_of(half * h, 128), h)]
                out.append((ref.at[kf - 1, :, pl.ds(first, h)], at))
    return out


def in_copies(place, refs, dst, flat):
    if len(refs) == 1:
        return [(refs[0], dst)]
    return column_copies(place, refs[0], refs[1:], dst, flat, staged=False)


def out_copies(place, refs, dst, flat):
    if len(refs) == 2:
        return [(refs[0], dst)]
    return column_copies(place, refs[0], refs[2:], dst, flat)


def expand_copies(place, refs, dst, flat):
    if len(refs) == 2:
        return [(refs[1], dst)]
    return column_copies(place, refs[1], refs[2:], dst, flat, refs[0].shape[1] // 2)


def shrink_copies(place, refs, dst, flat):
    if len(refs) == 1:
        return [(refs[0], dst)]
    f, j, c = place
    own, pieces = refs[0], refs[1:]
    rows = own.shape[0]
    r = rows // 8
    out = [(own, flat)]
    for refs, half in ((pieces[:4], c), (pieces[4:], 1 - c)):
        for slot, ref in enumerate(refs):
            kj = exchanged(slot, half)
            for kf in range(1, 4):
                start = pl.multiple_of((f ^ kf) * rows + half * (rows // 2) + (j ^ kj) * r, 16)
                out.append((ref.at[kf - 1], dst.at[pl.ds(start, r), :]))
    return out


def own_part(place, pairs, dst, flat):
    if len(pairs) > 1:
        rows = flat.shape[0]
        dst[pl.ds(pl.multiple_of(place[0] * rows, 16), rows), :] = flat[...].astype(BF)


MOST = 25


def begin(pairs, sems):
    for i, (src, dst) in enumerate(pairs):
        pltpu.make_async_copy(src, dst, sems.at[i]).start()


def finish(pairs, sems):
    for i, (src, dst) in enumerate(pairs):
        pltpu.make_async_copy(src, dst, sems.at[i]).wait()


def place_of(ref):
    return ref[0], ref[1], ref[2]


def tables(length):
    lane = np.arange(128)
    angles = np.arange(length)[:, None] * (10000.0 ** (-2.0 * ((lane % HEAD) // 2) / HEAD))[None, :]
    cosine, sine = np.cos(angles), np.sin(angles)
    even = (lane % 2 == 0)[None, :]
    parts = (cosine, np.where(even, -sine, 0.0), np.where(even, 0.0, sine))
    return [jnp.asarray(part.astype(np.float32)) for part in parts]


def rotate(u, cosine, up, down):
    return u * cosine + pltpu.roll(u, 127, 1) * up + pltpu.roll(u, 1, 1) * down


def turn_columns(value, place, ref):
    f, j, c = place
    turned = value.T
    r = turned.shape[0] // 16
    for fb in range(4):
        for jb in range(4):
            start = pl.multiple_of((exchanged(j ^ jb, c) * 4 + (f ^ fb)) * r, 16)
            ref[pl.ds(start, r), :] = turned[(fb * 4 + jb) * r : (fb * 4 + jb + 1) * r].astype(BF)


def qkv_kernel(*refs, pieces):
    place_ref, x_ref, b_ref, cos_ref, up_ref, down_ref = refs[:6]
    w_refs = refs[6 : 6 + pieces]
    o_ref, xt_ref, w_ref, flat_ref, sems = refs[6 + pieces :]

    @pl.when(pl.program_id(0) == 0)
    def _():
        copies = in_copies(place_of(place_ref), w_refs, w_ref, flat_ref)
        begin(copies, sems)
        finish(copies, sems)
        own_part(place_of(place_ref), copies, w_ref, flat_ref)

    x = x_ref[...]
    turn_columns(x.astype(F32), place_of(place_ref), xt_ref)
    cosine, up, down = cos_ref[...], up_ref[...], down_ref[...]
    model, width = w_ref.shape
    for col in range(0, width, 256):
        acc = dot_nn(x, w_ref[:, col : col + 256]) + b_ref[:, col : col + 256]
        for tile in range(2):
            lo = col + tile * 128
            u = acc[:, tile * 128 : (tile + 1) * 128]
            if lo < 2 * model:
                u = rotate(u, cosine, up, down)
            if lo < model:
                u = u * (1.0 / math.sqrt(HEAD))
            o_ref[:, lo : lo + 128] = u.astype(BF)


def qkv_call(place, x, weight, bias, tabs, length, block=256):
    n, model = x.shape
    per = length // block
    width = bias.shape[1]
    table = pl.BlockSpec((block, 128), lambda i, _: (i % per, 0))
    spec = pltpu.PrefetchScalarGridSpec(
        num_scalar_prefetch=1,
        grid=(n // block,),
        in_specs=[
            pl.BlockSpec((block, model), lambda i, _: (i, 0)),
            pl.BlockSpec((1, width), lambda i, _: (0, 0)),
            table,
            table,
            table,
        ]
        + [ANY] * len(weight),
        out_specs=[
            pl.BlockSpec((block, width), lambda i, _: (i, 0)),
            pl.BlockSpec((model, block), lambda i, _: (0, i)),
        ],
        scratch_shapes=[
            pltpu.VMEM((model, width), BF),
            pltpu.VMEM((model // 4, width), F32),
            pltpu.SemaphoreType.DMA((MOST,)),
        ],
    )
    return pl.pallas_call(
        functools.partial(qkv_kernel, pieces=len(weight)),
        grid_spec=spec,
        out_shape=[jax.ShapeDtypeStruct((n, width), BF), jax.ShapeDtypeStruct((model, n), BF)],
        cost_estimate=cost(2 * n * model * width, 2 * (n * model + model * width + n * width)),
        compiler_params=params(),
        name="qkv",
    )(place, x, bias, *tabs, *weight)


def attend_kernel(len_ref, q_ref, k_ref, v_ref, o_ref, qa_ref, *, block):
    length = q_ref.shape[0]
    live = len_ref[pl.program_id(0)]
    lane = lax.broadcasted_iota(jnp.int32, (length, 128), 1)
    pos = lax.broadcasted_iota(jnp.int32, (length, 128), 0)
    k, vt = k_ref[...].astype(F32), v_ref[...].astype(F32).T
    keys, values = [], []
    for h in range(2):
        own = (lane // HEAD) == h
        aux = HEAD * (1 - h)
        mask = jnp.where((lane == aux) & (pos >= live), NEG_FILL, 0.0)
        keys.append(jnp.where(own, k, mask).astype(BF))
        values.append(jnp.concatenate([vt[h * HEAD : (h + 1) * HEAD], jnp.ones((16, length), F32)], 0).astype(BF))
    lane = lax.broadcasted_iota(jnp.int32, (block, 128), 1)
    for i in range(length // block):
        rows = slice(i * block, (i + 1) * block)
        q = q_ref[rows, :].astype(F32)
        mixed, stats = [], []
        for h in range(2):
            own = (lane // HEAD) == h
            aux = HEAD * (1 - h)
            scores = dot_nt(keys[h], jnp.where(own, q, jnp.where(lane == aux, 1.0, 0.0)).astype(BF))
            top = jnp.max(scores, 0, keepdims=True)
            summed = dot_nn(values[h], jnp.exp(scores - top).astype(BF))
            total = summed[HEAD : HEAD + 1]
            mixed.append(summed[:HEAD] / total)
            shift = -(top + jnp.log(total))
            hi = shift.astype(BF).astype(F32)
            mid = (shift - hi).astype(BF).astype(F32)
            one = jnp.ones_like(hi)
            stats.append(jnp.concatenate([hi, mid, shift - hi - mid, one, jnp.zeros((HEAD - 4, block), F32)], 0))
        o_ref[rows, :] = jnp.concatenate(mixed, 0).T.astype(BF)
        extra = jnp.concatenate([stats[1], stats[0]], 0).T
        for h in range(2):
            qa_ref[h, rows, :] = jnp.where((lane // HEAD) == h, q, extra).astype(BF)


def attend_call(lengths, qkv, length, first, count, block=1024):
    n, width = qkv.shape
    rows, pairs = n // length, width // 384
    one = lambda off: pl.BlockSpec((length, 128), lambda b, p, _: (b, off * pairs + first + p))
    spec = pltpu.PrefetchScalarGridSpec(
        num_scalar_prefetch=1,
        grid=(rows, count),
        in_specs=[one(0), one(1), one(2)],
        out_specs=[
            pl.BlockSpec((length, 128), lambda b, p, _: (b, p)),
            pl.BlockSpec((None, 2, length, 128), lambda b, p, _: (b, p, 0, 0)),
        ],
    )
    return pl.pallas_call(
        functools.partial(attend_kernel, block=block),
        grid_spec=spec,
        out_shape=[
            jax.ShapeDtypeStruct((n, count * 128), BF),
            jax.ShapeDtypeStruct((rows, 2 * count, length, 128), BF),
        ],
        cost_estimate=cost(rows * count * 32 * length * length * 128, 12 * n * count * 128, rows * count * 2 * length * length),
        compiler_params=params(),
        name="attend",
    )(lengths, qkv, qkv, qkv)


def back_kernel(
    place_ref,
    len_ref,
    qa_ref,
    k_ref,
    v_ref,
    o_ref,
    do_ref,
    cos_ref,
    up_ref,
    down_ref,
    xt_ref,
    g_ref,
    sum_ref,
    theirs_ref,
    mine_ref,
    doa_ref,
    dqt_ref,
    acc_ref=None,
    *,
    block,
):
    length = k_ref.shape[0]
    pair, row, rows_last = pl.program_id(0), pl.program_id(1), pl.num_programs(1) - 1
    live = len_ref[row]
    lane = lax.broadcasted_iota(jnp.int32, (length, 128), 1)
    do = do_ref[...].astype(F32)
    prod = do * o_ref[...].astype(F32)
    for h in range(2):
        own = (lane // HEAD) == h
        aux = HEAD * (1 - h)
        shift = -jnp.sum(jnp.where(own, prod, 0.0), -1, keepdims=True)
        hi = shift.astype(BF).astype(F32)
        extra = jnp.where(lane == aux, hi, jnp.where(lane == aux + 1, shift - hi, 0.0))
        doa_ref[h] = jnp.where(own, do, extra).astype(BF)
    lane = lax.broadcasted_iota(jnp.int32, (block, 128), 1)
    pos = lax.broadcasted_iota(jnp.int32, (block, 128), 0)
    dk_sum = jnp.zeros((1, 128), F32)
    dv_sum = jnp.zeros((1, 128), F32)
    for i in range(length // block):
        rows = slice(i * block, (i + 1) * block)
        k, v = k_ref[rows, :].astype(F32), v_ref[rows, :].astype(F32)
        kt = k.T.astype(BF)
        dks, dvs = [], []
        for h in range(2):
            own = (lane // HEAD) == h
            aux = HEAD * (1 - h)
            mask = jnp.where((lane == aux + 3) & (pos + i * block >= live), NEG_FILL, 0.0)
            ka = jnp.where(own, k, jnp.where((lane >= aux) & (lane < aux + 3), 1.0, mask)).astype(BF)
            va = jnp.where(own, v, jnp.where((lane >= aux) & (lane < aux + 2), 1.0, 0.0)).astype(BF)
            qa, doa = qa_ref[h], doa_ref[h]
            p = jnp.exp(dot_nt(ka, qa))
            ds = (p * dot_nt(va, doa)).astype(BF)
            dvs.append(dot_nn(p.astype(BF), doa))
            dks.append(dot_nn(ds, qa))
            dqt = dot_nn(kt[h * HEAD : (h + 1) * HEAD, :], ds)
            if i == 0:
                dqt_ref[h * HEAD : (h + 1) * HEAD, :] = dqt
            else:
                dqt_ref[h * HEAD : (h + 1) * HEAD, :] += dqt
        dk = jnp.where(lane < HEAD, dks[0], dks[1])
        dk = rotate(dk, cos_ref[rows, :], -up_ref[rows, :], -down_ref[rows, :]).astype(BF)
        dv = jnp.where(lane < HEAD, dvs[0], dvs[1]).astype(BF)
        g_ref[rows, 128:256] = dk
        g_ref[rows, 256:384] = dv
        dk_sum += jnp.sum(dk.astype(F32), 0, keepdims=True)
        dv_sum += jnp.sum(dv.astype(F32), 0, keepdims=True)
    dq = rotate(dqt_ref[...].T * (1.0 / math.sqrt(HEAD)), cos_ref[...], -up_ref[...], -down_ref[...]).astype(BF)
    g_ref[:, 0:128] = dq
    sum_ref[...] = jnp.concatenate([jnp.sum(dq.astype(F32), 0, keepdims=True), dk_sum, dv_sum], -1)
    acc = dot_nn(xt_ref[...], g_ref[...])
    r = acc.shape[0] // 16

    def put(acc, ref, order):
        for slot in range(4):
            for kf in range(4):
                rows = slice((slot * 4 + kf) * r, (slot * 4 + kf + 1) * r)
                ref[order[slot], kf] = acc[rows].astype(BF)

    if acc_ref is not None:
        acc_ref[...] = jnp.where(row == 0, 0.0, acc_ref[...]) + acc

    @pl.when((pair == 0) & (row == rows_last))
    def _():
        put(acc if acc_ref is None else acc_ref[...], theirs_ref, TURNED)

    @pl.when((pair == 1) & (row == rows_last))
    def _():
        put(acc if acc_ref is None else acc_ref[...], mine_ref, (0, 1, 2, 3))


def back_call(place, lengths, seen, qkv, dattn, xt, tabs, length, span, block=256):
    attn, qa = seen
    n, width = qkv.shape
    rows, pairs = n // length, width // 384
    model = width // 3
    which = lambda p, place: jnp.where(p == 0, 1 - place[2], place[2])
    one = lambda off: pl.BlockSpec((length, 128), lambda p, b, place, _: (b, off * pairs + 2 * span + which(p, place)))
    table = pl.BlockSpec((length, 128), lambda *_: (0, 0))
    part = pl.BlockSpec((4, 4, model // 16, 384), lambda *_: (0, 0, 0, 0))
    spec = pltpu.PrefetchScalarGridSpec(
        num_scalar_prefetch=2,
        grid=(2, rows),
        in_specs=[
            pl.BlockSpec((None, 2, length, 128), lambda p, b, place, _: (b, which(p, place), 0, 0)),
            one(1),
            one(2),
            pl.BlockSpec((length, 128), lambda p, b, place, _: (b, which(p, place))),
            one(0),
            table,
            table,
            table,
            pl.BlockSpec((model, length), lambda p, b, *_: (0, b)),
        ],
        out_specs=[
            pl.BlockSpec((length, 384), lambda p, b, place, _: (b, which(p, place))),
            pl.BlockSpec((None, None, 1, 384), lambda p, b, place, _: (b, which(p, place), 0, 0)),
            part,
            part,
        ],
        scratch_shapes=[pltpu.VMEM((2, length, 128), BF), pltpu.VMEM((128, length), F32)]
        + ([pltpu.VMEM((model, 384), F32)] if rows > 1 else []),
    )
    return pl.pallas_call(
        functools.partial(back_kernel, block=block),
        grid_spec=spec,
        out_shape=[
            jax.ShapeDtypeStruct((n, 768), BF),
            jax.ShapeDtypeStruct((rows, 2, 1, 384), F32),
            jax.ShapeDtypeStruct((4, 4, model // 16, 384), BF),
            jax.ShapeDtypeStruct((4, 4, model // 16, 384), BF),
        ],
        cost_estimate=cost(rows * 80 * length * length * 128, 24 * n * 128, rows * 4 * length * length),
        compiler_params=params(),
        name="attend_back",
    )(place, lengths, qa, qkv, qkv, attn, dattn, *tabs, xt)


def norm_forward(u):
    center = u - jnp.mean(u, -1, keepdims=True)
    inverse = lax.rsqrt(jnp.mean(center * center, -1, keepdims=True) + NORM_EPS)
    return center * inverse, inverse


def norm_backward(incoming, normed, inverse, gain):
    scaled = incoming * gain
    mean = jnp.mean(scaled, -1, keepdims=True)
    return inverse * (scaled - mean - normed * jnp.mean(scaled * normed, -1, keepdims=True))


def adder(ref):
    def add(row, value, off=0):
        ref[row : row + 1, off : off + value.shape[1]] += jnp.sum(value, 0, keepdims=True)

    return add


def turn_halves(value, place, ref, cols):
    _, j, c = place
    turned = value.T
    r = turned.shape[0] // 8
    for cb in range(2):
        for jb in range(4):
            start = pl.multiple_of(((c ^ cb) * 4 + exchanged(j ^ jb, c)) * r, 16)
            ref[pl.ds(start, r), cols] = turned[(cb * 4 + jb) * r : (cb * 4 + jb + 1) * r].astype(BF)


def ffn_kernel(*refs, length, chunk, attn, side, shrink, blocks):
    place_ref, len_ref, x_ref, cot_ref, v_ref = refs[:5]
    at_refs = refs[5 : 5 + attn]
    side_refs = refs[5 + attn : 5 + attn + side]
    shrink_refs = refs[5 + attn + side : 5 + attn + side + shrink]
    outs = refs[5 + attn + side + shrink :]
    out_ref, slope_ref, yt_ref, att_ref, r1_ref, dr2_ref, dvec_ref, theirs_ref, mine_ref = outs[:9]
    wo_ref, w1_ref, w2_ref, act_ref, dzt_ref, flat_o, flat_1, flat_2, sem_o, sem_1, sem_2 = outs[9:]
    step = pl.program_id(0)
    block, model = x_ref.shape
    ff = w1_ref.shape[1]
    per = length // block
    live = len_ref[jnp.minimum(step, blocks - 1) // per]
    place = place_of(place_ref)
    vec = lambda i: v_ref[i : i + 1, :]

    @pl.when(step == 0)
    def _():
        first = out_copies(place, side_refs, wo_ref, flat_o)
        second = expand_copies(place, side_refs, w1_ref, flat_1)
        third = shrink_copies(place, shrink_refs, w2_ref, flat_2)
        begin(first, sem_o)
        begin(second, sem_1)
        begin(third, sem_2)
        dvec_ref[...] = jnp.zeros_like(dvec_ref)
        finish(first, sem_o)
        own_part(place, first, wo_ref, flat_o)
        finish(second, sem_1)
        own_part(place, second, w1_ref, flat_1)
        finish(third, sem_2)
        own_part(place, third, w2_ref, flat_2)

    @pl.when(step < blocks)
    def _():
        here = pl.ds(pl.multiple_of(step * block, block), block)
        at = jnp.concatenate([ref[...] for ref in at_refs], -1)
        turn_columns(at.astype(F32), place, att_ref)
        r1 = x_ref[...].astype(F32) + (dot_nn(at, wo_ref[...]) + vec(7))
        r1_ref[...] = r1
        n1, _ = norm_forward(r1)
        y1 = n1 * vec(0) + vec(2)
        y1b = y1.astype(BF)
        turn_columns(y1, place, yt_ref)
        z = jnp.zeros((block, model), F32)
        for lo in range(0, ff, chunk):
            cols = slice(lo, lo + chunk)
            bias = v_ref[9 + lo // model : 10 + lo // model, lo % model : lo % model + chunk]
            pre = dot_nn(y1b, w1_ref[:, cols]) + bias
            phi = 0.5 * (1.0 + lax.erf(pre * ROOT_HALF))
            act = (pre * phi).astype(BF)
            act_ref[here, cols] = act
            slope_ref[:, cols] = (phi + pre * (jnp.exp(-0.5 * pre * pre) * INV_ROOT_TAU)).astype(BF)
            z = z + dot_nn(act, w2_ref[cols, :])
        r2 = y1 + (z + vec(8))
        n2, i2 = norm_forward(r2)
        out_ref[...] = (n2 * vec(1) + vec(3)).astype(BF)
        pos = lax.broadcasted_iota(jnp.int32, (block, model), 0) + (step % per) * block
        e = jnp.where(pos < live, cot_ref[...].astype(F32), 0.0)
        dr2 = norm_backward(e, n2, i2, vec(1))
        dr2_ref[...] = dr2
        turn_halves(dr2, place, dzt_ref, here)
        add = adder(dvec_ref)
        add(1, e * n2)
        add(3, e)
        add(8, dr2.astype(BF).astype(F32))

    @pl.when(step >= blocks)
    def _():
        kf = step - blocks
        width = ff // 4
        r = model // 8
        cols = pl.ds(pl.multiple_of((place[0] ^ kf) * width, 128), width)
        acc = dot_nn(dzt_ref[...], act_ref[:, cols])
        for slot in range(4):
            mine_ref[slot] = acc[slot * r : (slot + 1) * r].astype(BF)
            theirs_ref[TURNED[slot]] = acc[(4 + slot) * r : (5 + slot) * r].astype(BF)


def ffn_call(place, lengths, x, attn, cot, side, shrink, vec, length, block=256, chunk=768):
    n, model = x.shape
    ff = 4 * model
    blocks = n // block
    tok = pl.BlockSpec((block, model), lambda i, *_: (jnp.minimum(i, blocks - 1), 0))
    wide = pl.BlockSpec((block, ff), lambda i, *_: (jnp.minimum(i, blocks - 1), 0))
    small = pl.BlockSpec((13, model), lambda i, *_: (0, 0))
    turned = pl.BlockSpec((model, block), lambda i, *_: (0, jnp.minimum(i, blocks - 1)))
    grad = pl.BlockSpec((4, None, model // 8, ff // 4), lambda i, *_: (0, jnp.maximum(i - blocks, 0), 0, 0))
    spec = pltpu.PrefetchScalarGridSpec(
        num_scalar_prefetch=2,
        grid=(blocks + 4,),
        in_specs=[tok, tok, small]
        + [pl.BlockSpec((block, a.shape[1]), lambda i, *_: (jnp.minimum(i, blocks - 1), 0)) for a in attn]
        + [ANY] * (len(side) + len(shrink)),
        out_specs=[tok, wide, turned, turned, tok, tok, small, grad, grad],
        scratch_shapes=[
            pltpu.VMEM((model, model), BF),
            pltpu.VMEM((model, ff), BF),
            pltpu.VMEM((ff, model), BF),
            pltpu.VMEM((n, ff), BF),
            pltpu.VMEM((model, n), BF),
            pltpu.VMEM((model // 4, model), F32),
            pltpu.VMEM((model // 4, ff), F32),
            pltpu.VMEM((ff // 4, model), F32),
        ]
        + [pltpu.SemaphoreType.DMA((MOST,))] * 3,
    )
    s = lambda w, t: jax.ShapeDtypeStruct((n, w), t)
    flip = jax.ShapeDtypeStruct((model, n), BF)
    parts = jax.ShapeDtypeStruct((4, 4, model // 8, ff // 4), BF)
    return pl.pallas_call(
        functools.partial(
            ffn_kernel, length=length, chunk=chunk, attn=len(attn), side=len(side), shrink=len(shrink), blocks=blocks
        ),
        grid_spec=spec,
        out_shape=[
            s(model, BF),
            s(ff, BF),
            flip,
            flip,
            s(model, F32),
            s(model, F32),
            jax.ShapeDtypeStruct((13, model), F32),
            parts,
            parts,
        ],
        cost_estimate=cost(
            2 * n * (2 * model * model + 6 * model * ff), n * (model * 20 + ff * 4) + model * ff * 4, n * ff * 2
        ),
        compiler_params=params(),
        name="ffn",
    )(place, lengths, x, cot, vec, *attn, *side, *shrink)


def ffn_back_kernel(*refs, chunk, side, shrink):
    place_ref, dr2_ref, slope_ref, r1_ref, v_ref = refs[:5]
    side_refs = refs[5 : 5 + side]
    shrink_refs = refs[5 + side : 5 + side + shrink]
    outs = refs[5 + side + shrink :]
    dpre_ref, dr1_ref, da_ref, dat_ref, dvec_ref = outs[:5]
    wo_ref, w1_ref, w2_ref, flat_o, flat_1, flat_2, sem_o, sem_1, sem_2 = outs[5:]
    step = pl.program_id(0)
    block, model = dr2_ref.shape
    ff = w1_ref.shape[1]
    place = place_of(place_ref)
    vec = lambda i: v_ref[i : i + 1, :]

    @pl.when(step == 0)
    def _():
        first = out_copies(place, side_refs, wo_ref, flat_o)
        second = expand_copies(place, side_refs, w1_ref, flat_1)
        third = shrink_copies(place, shrink_refs, w2_ref, flat_2)
        begin(third, sem_2)
        begin(second, sem_1)
        begin(first, sem_o)
        dvec_ref[...] = jnp.zeros_like(dvec_ref)
        finish(third, sem_2)
        own_part(place, third, w2_ref, flat_2)
        finish(second, sem_1)
        own_part(place, second, w1_ref, flat_1)
        finish(first, sem_o)
        own_part(place, first, wo_ref, flat_o)

    add = adder(dvec_ref)
    dy = dr2_ref[...]
    dz = dy.astype(BF)
    for lo in range(0, ff, chunk):
        cols = slice(lo, lo + chunk)
        dpre = (dot_nt(dz, w2_ref[cols, :]) * slope_ref[:, cols].astype(F32)).astype(BF)
        dpre_ref[:, cols] = dpre
        add(9 + lo // model, dpre.astype(F32), lo % model)
        dy = dy + dot_nt(dpre, w1_ref[:, cols])
    n1, i1 = norm_forward(r1_ref[...])
    add(0, dy * n1)
    add(2, dy)
    dr1 = norm_backward(dy, n1, i1, vec(0))
    dr1_ref[...] = dr1
    da = dr1.astype(BF)
    da_ref[...] = da
    add(7, da.astype(F32))
    dat_ref[...] = dot_nt(da, wo_ref[...]).astype(BF)


def ffn_back_call(place, dr2, slope, r1, side, shrink, vec, block=256, chunk=768):
    n, model = dr2.shape
    ff = 4 * model
    tok = pl.BlockSpec((block, model), lambda i, *_: (i, 0))
    wide = pl.BlockSpec((block, ff), lambda i, *_: (i, 0))
    small = pl.BlockSpec((13, model), lambda i, *_: (0, 0))
    spec = pltpu.PrefetchScalarGridSpec(
        num_scalar_prefetch=1,
        grid=(n // block,),
        in_specs=[tok, wide, tok, small] + [ANY] * (len(side) + len(shrink)),
        out_specs=[wide, tok, tok, tok, small],
        scratch_shapes=[
            pltpu.VMEM((model, model), BF),
            pltpu.VMEM((model, ff), BF),
            pltpu.VMEM((ff, model), BF),
            pltpu.VMEM((model // 4, model), F32),
            pltpu.VMEM((model // 4, ff), F32),
            pltpu.VMEM((ff // 4, model), F32),
        ]
        + [pltpu.SemaphoreType.DMA((MOST,))] * 3,
    )
    s = lambda w, t: jax.ShapeDtypeStruct((n, w), t)
    return pl.pallas_call(
        functools.partial(ffn_back_kernel, chunk=chunk, side=len(side), shrink=len(shrink)),
        grid_spec=spec,
        out_shape=[s(ff, BF), s(model, F32), s(model, BF), s(model, BF), jax.ShapeDtypeStruct((13, model), F32)],
        cost_estimate=cost(2 * n * (model * model + 2 * model * ff), n * (model * 18 + ff * 4) + model * ff * 4),
        compiler_params=params(),
        name="ffn_back",
    )(place, dr2, slope, r1, vec, *side, *shrink)


def side_grad_kernel(place_ref, yt_ref, att_ref, dpre_ref, da_ref, theirs_ref, mine_ref, *, steps):
    step = pl.program_id(0)
    r = yt_ref.shape[0] // 16

    def put(acc, ref, order):
        for slot in range(4):
            for kf in range(4):
                rows = slice((slot * 4 + kf) * r, (slot * 4 + kf + 1) * r)
                ref[order[slot], kf, :, : acc.shape[1]] = acc[rows].astype(BF)

    for first, ref, order in ((0, theirs_ref, TURNED), (steps, mine_ref, (0, 1, 2, 3))):

        @pl.when((step >= first) & (step < first + steps - 1))
        def _(ref=ref, order=order):
            put(dot_nn(yt_ref[...], dpre_ref[...]), ref, order)

        @pl.when(step == first + steps - 1)
        def _(ref=ref, order=order):
            put(dot_nn(att_ref[...], da_ref[...]), ref, order)


def side_grad_call(place, yt, att, dpre, da, block=768):
    model, n = yt.shape
    half = dpre.shape[1] // 2
    steps = half // block + 1
    which = lambda i, place: jnp.where(i < steps, 1 - place[2], place[2])
    turned = pl.BlockSpec((model, n), lambda i, _: (0, 0))
    width = half + model // 2
    out = lambda first: pl.BlockSpec(
        (4, 4, model // 16, block), lambda i, _: (0, 0, 0, jnp.clip(i - first, 0, steps - 1))
    )
    spec = pltpu.PrefetchScalarGridSpec(
        num_scalar_prefetch=1,
        grid=(2 * steps,),
        in_specs=[
            turned,
            turned,
            pl.BlockSpec(
                (n, block), lambda i, place: (0, which(i, place) * (steps - 1) + jnp.minimum(i % steps, steps - 2))
            ),
            pl.BlockSpec((n, model // 2), lambda i, place: (0, which(i, place))),
        ],
        out_specs=[out(0), out(steps)],
    )
    return pl.pallas_call(
        functools.partial(side_grad_kernel, steps=steps),
        grid_spec=spec,
        out_shape=[jax.ShapeDtypeStruct((4, 4, model // 16, width), BF)] * 2,
        cost_estimate=cost(4 * n * model * width, 4 * (n * model + n * width + model * width)),
        compiler_params=params(),
        name="side_grad",
    )(place, yt, att, dpre, da)


def token_kernel(*refs, pieces, parts):
    place_ref, dr1_ref = refs[:2]
    g_refs = refs[2 : 2 + parts]
    w_refs = refs[2 + parts : 2 + parts + pieces]
    o_ref, w_ref, flat_ref, sems = refs[2 + parts + pieces :]
    model = w_ref.shape[0]

    @pl.when(pl.program_id(0) == 0)
    def _():
        copies = in_copies(place_of(place_ref), w_refs, w_ref, flat_ref)
        begin(copies, sems)
        finish(copies, sems)
        own_part(place_of(place_ref), copies, w_ref, flat_ref)

    total = dr1_ref[...]
    for t in range(3):
        tiles = [ref[:, lo + t * 128 : lo + (t + 1) * 128] for ref in g_refs for lo in range(0, ref.shape[1], 384)]
        total = total + dot_nt(jnp.concatenate(tiles, -1), w_ref[:, t * model : (t + 1) * model])
    o_ref[...] = total.astype(BF)


def token_call(place, dr1, grads, weight, block=256):
    n, model = dr1.shape
    tok = lambda w: pl.BlockSpec((block, w), lambda i, _: (i, 0))
    spec = pltpu.PrefetchScalarGridSpec(
        num_scalar_prefetch=1,
        grid=(n // block,),
        in_specs=[tok(model)] + [tok(g.shape[1]) for g in grads] + [ANY] * len(weight),
        out_specs=tok(model),
        scratch_shapes=[
            pltpu.VMEM((model, 3 * model), BF),
            pltpu.VMEM((model // 4, 3 * model), F32),
            pltpu.SemaphoreType.DMA((MOST,)),
        ],
    )
    return pl.pallas_call(
        functools.partial(token_kernel, pieces=len(weight), parts=len(grads)),
        grid_spec=spec,
        out_shape=jax.ShapeDtypeStruct((n, model), BF),
        cost_estimate=cost(6 * n * model * model, n * model * 12 + 6 * model * model),
        compiler_params=params(),
        name="token_gradient",
    )(place, dr1, *grads, *weight)


def picked(refs, count, extra):
    at = 0
    for i in range(count):
        width = refs[i].shape[-1]
        yield refs[i], (refs[count + i] if i < count - extra else None), slice(at, at + width)
        at += width


def add_first_kernel(*refs, count, extra):
    out = refs[-1]
    for mine, recv, cols in picked(refs, count, extra):
        total = mine[...].astype(F32)
        if recv is not None:
            total = total + recv[...].astype(F32)
        out[:, :, :, cols] = total.astype(BF)


def add_first(mine, recv):
    shapes = [m.shape for m in mine]
    r, width = shapes[0][2], sum(s[3] for s in shapes)
    block = lambda w: pl.BlockSpec((2, 2, r, w), lambda k: (1, k, 0, 0))
    return pl.pallas_call(
        functools.partial(add_first_kernel, count=len(mine), extra=len(mine) - len(recv)),
        grid=(2,),
        in_specs=[block(s[3]) for s in shapes + shapes[: len(recv)]],
        out_specs=pl.BlockSpec((2, 2, r, width), lambda k: (0, k, 0, 0)),
        out_shape=jax.ShapeDtypeStruct((2, 4, r, width), BF),
        cost_estimate=cost(8 * r * width, 48 * r * width),
        compiler_params=params(),
        name="add_first",
    )(*mine, *recv)


def add_second_kernel(*refs, count, extra):
    got, out = refs[-2:]
    for mine, recv, cols in picked(refs, count, extra):
        total = mine[...].astype(F32) + got[:, :, cols].astype(F32)
        if recv is not None:
            total = total + recv[...].astype(F32)
        out[:, :, cols] = total.astype(BF)


def add_second(mine, recv, got):
    shapes = [m.shape for m in mine]
    _, _, r, width = got.shape
    block = lambda w: pl.BlockSpec((None, 4, r, w), lambda k: (1, 0, 0, 0))
    return pl.pallas_call(
        functools.partial(add_second_kernel, count=len(mine), extra=len(mine) - len(recv)),
        grid=(1,),
        in_specs=[block(s[3]) for s in shapes + shapes[: len(recv)]] + [block(width)],
        out_specs=pl.BlockSpec((4, r, width), lambda k: (0, 0, 0)),
        out_shape=jax.ShapeDtypeStruct((4, r, width), BF),
        cost_estimate=cost(12 * r * width, 32 * r * width),
        compiler_params=params(),
        name="add_second",
    )(*mine, *recv, got)


def add_z_kernel(place_ref, *refs, count, extra, split):
    ins = 2 * count - extra + 2
    got, last = refs[ins - 2 : ins]
    outs = refs[ins:]
    f = place_ref[0]
    for mine, recv, cols in picked(refs, count, extra):
        for kf in range(4):
            total = mine[kf].astype(F32) + got[kf, :, cols].astype(F32) + last[kf, :, cols].astype(F32)
            if recv is not None:
                total = total + recv[kf].astype(F32)
            if split:
                outs[kf][:, cols] = total.astype(BF)
            else:
                outs[0][f ^ kf, :, cols] = total.astype(BF)


def add_z(place, mine, recv, got, last, split):
    shapes = [m.shape for m in mine]
    _, _, r, width = got.shape
    block = lambda w: pl.BlockSpec((None, 4, r, w), lambda *_: (0, 0, 0, 0))
    if split:
        outs = [pl.BlockSpec((r, width), lambda *_: (0, 0))] * 4
        shape = [jax.ShapeDtypeStruct((r, width), BF)] * 4
    else:
        outs = pl.BlockSpec((4, r, width), lambda *_: (0, 0, 0))
        shape = jax.ShapeDtypeStruct((4, r, width), BF)
    spec = pltpu.PrefetchScalarGridSpec(
        num_scalar_prefetch=1,
        grid=(1,),
        in_specs=[block(s[3]) for s in shapes + shapes[: len(recv)]]
        + [block(width), pl.BlockSpec((4, r, width), lambda *_: (0, 0, 0))],
        out_specs=outs,
    )
    return pl.pallas_call(
        functools.partial(add_z_kernel, count=len(mine), extra=len(mine) - len(recv), split=split),
        grid_spec=spec,
        out_shape=shape,
        cost_estimate=cost(16 * r * width, 40 * r * width),
        compiler_params=params(),
        name="add_z",
    )(place, *mine, *recv, got, last)


def add_all_kernel(*refs):
    total = refs[0][...].astype(F32)
    for ref in refs[1:-1]:
        total = total + ref[...].astype(F32)
    refs[-1][...] = total.astype(BF)


def add_all(*parts):
    return pl.pallas_call(
        add_all_kernel,
        out_shape=jax.ShapeDtypeStruct(parts[0].shape, BF),
        cost_estimate=cost(4 * parts[0].size, 10 * parts[0].size),
        compiler_params=params(),
        name="add_all",
    )(*parts)


def send_z(own, one, two, three):
    return own, cross(one, 1), cross(two, 2), cross(three, 3)


def over_chips(total):
    return total, swap(total, 2), swap(total, 4), swap(total, 6)


def both_cores(chips):
    return (*chips, *(swap_core(part) for part in chips))


def vector_parts_kernel(place_ref, one_ref, two_ref, *refs):
    sums, (theirs_ref, mine_ref) = refs[:-2], refs[-2:]
    f, j, c = place_of(place_ref)
    rest = one_ref[...] + two_ref[...]
    heads = []
    for t in range(3):
        cols = slice(t * 128, (t + 1) * 128)
        tiles = [jnp.sum(ref[:, pair, :, cols], 0) for ref in sums for pair in range(2)]
        heads.append(jnp.concatenate(tiles, -1))
    value = jnp.concatenate([rest[:4], *heads, rest[7:]], 0)
    theirs_ref[...] = jnp.zeros_like(theirs_ref)
    mine_ref[...] = jnp.zeros_like(mine_ref)
    rows, model = value.shape
    width = model // 16
    for fb in range(4):
        for jb in range(4):
            lo = (fb * 4 + jb) * width
            part = value[:, lo : lo + width].astype(BF)
            mine_ref[exchanged(j ^ jb, c), f ^ fb, :rows, :width] = part
            theirs_ref[exchanged(j ^ jb, 1 - c), f ^ fb, :rows, :width] = part


def vector_parts(place, one, two, sums, r):
    whole = lambda a: pl.BlockSpec(a.shape, lambda *_, k=a.ndim: (0,) * k)
    spec = pltpu.PrefetchScalarGridSpec(
        num_scalar_prefetch=1,
        grid=(1,),
        in_specs=[whole(a) for a in (one, two, *sums)],
        out_specs=[pl.BlockSpec((4, 4, r, 128), lambda *_: (0, 0, 0, 0))] * 2,
    )
    return pl.pallas_call(
        vector_parts_kernel,
        grid_spec=spec,
        out_shape=[jax.ShapeDtypeStruct((4, 4, r, 128), BF)] * 2,
        compiler_params=params(),
        name="vector_parts",
    )(place, one, two, *sums)


def adam_update(master, moment, square, gradient, rate, decay):
    momentum = BETA_ONE * moment + (1.0 - BETA_ONE) * gradient
    squares = BETA_TWO * square + (1.0 - BETA_TWO) * gradient * gradient
    corrected = momentum / (1.0 - BETA_ONE**STEP)
    spread = jnp.sqrt(squares / (1.0 - BETA_TWO**STEP))
    return (master - rate * (corrected / (spread + ADAM_EPS) + decay * master), momentum, squares)


def adam_block(state, outs, g, rate):
    w, m, s = (ref[...] for ref in state)
    for ref, value in zip(outs, adam_update(w, m, s, g, rate, WEIGHT_DECAY)):
        ref[...] = value


def adam_side_kernel(*refs, weights, moves, rates):
    state, grad, outs = refs[: 3 * weights], refs[3 * weights], refs[3 * weights + 1 : 6 * weights + 1]
    flats = refs[6 * weights + 1 :]
    step = pl.program_id(0)
    rows = state[0].shape[0]

    @pl.when(step == 0)
    def _():
        r = grad.shape[1]
        for weight, src, width in moves:
            for d in range(8):
                to = slice((d % 2) * width, (d % 2 + 1) * width)
                flats[weight][d // 2 * r : (d // 2 + 1) * r, to] = grad[d, :, src : src + width]

    here = pl.ds(pl.multiple_of(step * rows, rows), rows)
    for i in range(weights):
        cut = slice(3 * i, 3 * i + 3)
        adam_block(state[cut], outs[cut], flats[i][here, :].astype(F32), rates[i])


def adam_side_call(states, grad, moves, rates, steps=2):
    rows = states[0][0].shape[0] // steps
    block = lambda a: pl.BlockSpec((rows, a.shape[1]), lambda i: (i, 0))
    flat = [a for state in states for a in state]
    size = sum(a.size for a in flat)
    return pl.pallas_call(
        functools.partial(adam_side_kernel, weights=len(states), moves=tuple(moves), rates=tuple(rates)),
        grid=(steps,),
        in_specs=[block(a) for a in flat] + [pl.BlockSpec(grad.shape, lambda i: (0, 0, 0))],
        out_specs=[block(a) for a in flat],
        scratch_shapes=[pltpu.VMEM(state[0].shape, BF) for state in states],
        out_shape=[jax.ShapeDtypeStruct(a.shape, F32) for a in flat],
        cost_estimate=cost(size * 4, size * 9),
        compiler_params=params(),
        name="adam_side",
    )(*flat, grad)


def adam_in_kernel(*refs, moves, rate):
    place_ref, state, grads, outs, flat = refs[0], refs[1:4], refs[4:12], refs[12:15], refs[15]
    _, j, c = place_of(place_ref)
    step = pl.program_id(0)
    rows = state[0].shape[0]

    @pl.when(step == 0)
    def _():
        for i, ref in enumerate(grads):
            half = c if i < 4 else 1 - c
            r = ref.shape[0]
            here = pl.ds(pl.multiple_of((j ^ (i % 4)) * r, 16), r)
            for src, to, stride in moves:
                cols = pl.ds(pl.multiple_of(to + half * stride, 128), 128)
                flat[here, cols] = ref[:, src : src + 128]

    here = pl.ds(pl.multiple_of(step * rows, rows), rows)
    adam_block(state, outs, flat[here, :].astype(F32), rate)


def adam_in_call(place, state, grads, moves, rate, steps=2):
    rows = state[0].shape[0] // steps
    block = pl.BlockSpec((rows, state[0].shape[1]), lambda i, _: (i, 0))
    spec = pltpu.PrefetchScalarGridSpec(
        num_scalar_prefetch=1,
        grid=(steps,),
        in_specs=[block] * 3 + [pl.BlockSpec(g.shape, lambda i, _: (0, 0)) for g in grads],
        out_specs=[block] * 3,
        scratch_shapes=[pltpu.VMEM(state[0].shape, BF)],
    )
    return pl.pallas_call(
        functools.partial(adam_in_kernel, moves=tuple(moves), rate=rate),
        grid_spec=spec,
        out_shape=[jax.ShapeDtypeStruct(state[0].shape, F32)] * 3,
        cost_estimate=cost(state[0].size * 12, state[0].size * 28),
        compiler_params=params(),
        name="adam_in",
    )(place, *state, *grads)


def adam_turned_kernel(*refs, rate):
    state, grad, outs, (flat_ref, g_ref) = refs[:3], refs[3], refs[4:7], refs[7:]
    step = pl.program_id(0)
    rows = state[0].shape[0]

    @pl.when(step == 0)
    def _():
        r = grad.shape[1]
        for d in range(8):
            at = (d % 2) * 4 + d // 2
            flat_ref[at * r : (at + 1) * r, :] = grad[d].astype(F32)
        g_ref[...] = flat_ref[...].T

    adam_block(state, outs, g_ref[pl.ds(pl.multiple_of(step * rows, rows), rows), :], rate)


def adam_turned_call(state, grad, rate, steps=2):
    total, cols = state[0].shape
    block = pl.BlockSpec((total // steps, cols), lambda i: (i, 0))
    return pl.pallas_call(
        functools.partial(adam_turned_kernel, rate=rate),
        grid=(steps,),
        in_specs=[block] * 3 + [pl.BlockSpec(grad.shape, lambda i: (0, 0, 0))],
        out_specs=[block] * 3,
        scratch_shapes=[pltpu.VMEM((cols, total), F32), pltpu.VMEM((total, cols), F32)],
        out_shape=[jax.ShapeDtypeStruct(state[0].shape, F32)] * 3,
        cost_estimate=cost(total * cols * 12, total * cols * 28),
        compiler_params=params(),
        name="adam_turned",
    )(*state, grad)


def vector_rows(rest, sums):
    heads = jnp.concatenate([jnp.sum(s, 0) for s in sums], 0).reshape(-1, 3, 128)
    heads = heads.transpose(1, 0, 2).reshape(3, -1)
    return jnp.concatenate([rest[:4], heads, rest[7:]], 0)


def local(
    tokens,
    cotangent,
    lengths,
    inward_weight,
    inward_moment,
    inward_square,
    outward_weight,
    outward_moment,
    outward_square,
    expand_weight,
    expand_moment,
    expand_square,
    shrink_weight,
    shrink_moment,
    shrink_square,
    vectors,
    vector_moment,
    vector_square,
    sliced,
):
    _, length, model = tokens.shape
    x, cot = tokens.reshape(-1, model), cotangent.reshape(-1, model)
    tabs = tables(length)
    ff = 4 * model
    pairs = model // 128
    inward = (inward_weight, inward_moment, inward_square)
    outward = (outward_weight, outward_moment, outward_square)
    expand = (expand_weight, expand_moment, expand_square)
    shrink = (shrink_weight, shrink_moment, shrink_square)
    vector = (vectors, vector_moment, vector_square)
    rate_d, rate_o, rate_f = 1.0 / math.sqrt(model), 1.0 / math.sqrt(OUT_FAN), 1.0 / math.sqrt(ff)
    f, d = lax.axis_index("fsdp"), lax.axis_index("dp")
    j, c = d // 2, d % 2
    place = jnp.stack([f, j, c]).astype(jnp.int32) if sliced else jnp.zeros((3,), jnp.int32)
    spans = [(0, 2), (2, 2), (4, 2)]

    if not sliced:
        low = [w.astype(BF) for w in (inward_weight, outward_weight, expand_weight, shrink_weight, vectors)]
        whole = [lax.all_gather(w, "fsdp", axis=0, tiled=True) for w in low[:4]]
        in_pieces, side_pieces, shrink_pieces = (whole[0],), (whole[1], whole[2]), (whole[3],)
        vec = lax.all_gather(low[4], "fsdp", axis=1, tiled=True).astype(F32)
        qkv, xt = qkv_call(place, x, in_pieces, vec[4:7].reshape(1, -1), tabs, length)
        seen = [attend_call(lengths, qkv, length, *span) for span in spans]
        out, slope, yt, att, r1, dr2, vec_two, far, near = ffn_call(
            place, lengths, x, [a for a, _ in seen], cot, side_pieces, shrink_pieces, vec, length
        )
        order = jnp.array(TURNED)
        shrink_grad = jnp.concatenate([near, far[order]]).transpose(1, 3, 0, 2).reshape(ff, model)
        dpre, dr1, da, dattn, vec_one = ffn_back_call(place, dr2, slope, r1, side_pieces, shrink_pieces, vec)
        far, near = side_grad_call(place, yt, att, dpre, da)
        both = jnp.stack([near, far[order]]).transpose(2, 1, 3, 0, 4).reshape(model, 2, -1)
        expand_grad = both[:, :, : ff // 2].reshape(model, ff)
        outward_grad = both[:, :, ff // 2 :].reshape(model, model)
        backs = [back_call(place, lengths, seen[i], qkv, dattn, xt, tabs, length, i) for i in range(len(spans))]
        token_gradient = token_call(place, dr1, [b[0] for b in backs], in_pieces)
        parts = jnp.stack([part for _, _, far, near in backs for part in (near, far[order])])
        parts = parts.transpose(2, 1, 3, 0, 4).reshape(model, pairs, 3, 128)
        inward_grad = parts.transpose(0, 2, 1, 3).reshape(model, 3 * model)

        def reduced(g, axis=0):
            return lax.psum(lax.psum_scatter(g, "fsdp", scatter_dimension=axis, tiled=True).astype(F32), "dp")

        inward_new = adam_update(*inward, reduced(inward_grad), rate_d, WEIGHT_DECAY)
        outward_new = adam_update(*outward, reduced(outward_grad), rate_o, WEIGHT_DECAY)
        expand_new = adam_update(*expand, reduced(expand_grad), rate_d, WEIGHT_DECAY)
        shrink_new = adam_update(*shrink, reduced(shrink_grad), rate_f, WEIGHT_DECAY)
        vec_sum = reduced(vector_rows(vec_one + vec_two, [b[1] for b in backs]), 1)
    else:
        shard = model // 4
        r = shard // 4

        def columns(w):
            half = w.shape[1] // 2
            return lax.dynamic_slice(w, (j * r, c * half), (r, half))

        def rows(w):
            r = w.shape[0] // 8
            return lax.dynamic_slice(w, ((c * 4 + j) * r, 0), (r, w.shape[1]))

        low_vec = vectors.astype(BF)
        third = r + r // 3
        beside = jnp.pad(low_vec.reshape(-1, third), ((0, r - 3 * vectors.shape[0]), (0, 128 - third)))
        part_in = jnp.concatenate([columns(inward_weight).astype(BF), beside], -1)
        part_side = jnp.concatenate([columns(outward_weight), columns(expand_weight)], -1).astype(BF)
        part_shrink = rows(shrink_weight).astype(BF)
        z_in = after(jnp.stack(over_z(part_in)), part_side, part_shrink)
        chips_in, z_side = after((over_chips(z_in), over_z(after(part_side, z_in))))
        in_pieces = (inward_weight, *both_cores(chips_in))
        by = z_in[:, : 3 * vectors.shape[0], part_in.shape[1] - 128 : part_in.shape[1] - 128 + third]
        by = (low_vec, *by.reshape(3, vectors.shape[0], shard))
        ordered = []
        for at in range(4):
            k = f ^ at
            ordered.append(jnp.where(k == 0, by[0], jnp.where(k == 1, by[1], jnp.where(k == 2, by[2], by[3]))))
        vec = jnp.concatenate(ordered, 1).astype(F32)
        z_side = jnp.stack(z_side)
        first_side, second_side = swap_first(z_side), swap_second(z_side)
        z_shrink = over_z(after(part_shrink, z_side))
        qkv, xt = qkv_call(place, x, after(in_pieces, z_side, vec), vec[4:7].reshape(1, -1), tabs, length)
        first_side, second_side, z_shrink = after((first_side, second_side, z_shrink), qkv)
        third_side = swap_second(first_side)
        side_near = (z_side, second_side, first_side)
        side_far = tuple(swap_core(part) for part in side_near)
        z_shrink = jnp.stack(z_shrink)
        first_shrink, second_shrink = swap_first(z_shrink), swap_second(z_shrink)
        seen = [attend_call(lengths, after(qkv, first_side, z_shrink), length, *spans[0])]
        third_side, side_far, first_shrink, second_shrink = after(
            (third_side, side_far, first_shrink, second_shrink), seen[0]
        )
        third_shrink = swap_second(first_shrink)
        shrink_near = (z_shrink, second_shrink, first_shrink)
        shrink_far = tuple(swap_core(part) for part in shrink_near)
        side_pieces = (outward_weight, expand_weight, *side_near, third_side, *side_far, swap_core(third_side))
        seen.append(attend_call(lengths, after(qkv, third_side, first_shrink), length, *spans[1]))
        third_shrink, shrink_far = after((third_shrink, shrink_far), seen[1])
        shrink_pieces = (shrink_weight, *shrink_near, third_shrink, *shrink_far, swap_core(third_shrink))
        seen.append(attend_call(lengths, after(qkv, third_shrink), length, *spans[2]))

        out, slope, yt, att, r1, dr2, vec_two, theirs_s, mine_s = ffn_call(
            place, lengths, x, [a for a, _ in seen], cot, side_pieces, shrink_pieces, vec, length
        )
        recv_s = swap_core(theirs_s)
        dpre, dr1, da, dattn, vec_one = ffn_back_call(place, dr2, slope, r1, side_pieces, shrink_pieces, vec)

        def back(span, *wait):
            return back_call(place, lengths, seen[span], qkv, after(dattn, *wait), xt, tabs, length, span)

        recv_s = after(recv_s, dattn)
        to_s = add_first([mine_s], [recv_s])
        got_s = swap_first(to_s)
        theirs_d, mine_d = side_grad_call(place, yt, att, after(dpre, to_s), da)
        got_s = after(got_s, theirs_d)
        on_s = add_second([mine_s], [recv_s], got_s)
        last_s = swap_second(on_s)
        recv_d = swap_core(after(theirs_d, on_s))
        g0, sum0, theirs_0, mine_0 = back(0, on_s)
        last_s, recv_d = after((last_s, recv_d), g0)
        z_s = add_z(place, [mine_s], [recv_s], got_s, last_s, False)
        part_s = lax.psum_scatter(z_s, "fsdp", scatter_dimension=0)
        to_d = add_first([mine_d], [after(recv_d, z_s)])
        got_d = swap_first(to_d)
        recv_0 = swap_core(after(theirs_0, to_d))
        g1, sum1, theirs_1, mine_1 = back(1, to_d)
        got_d, recv_0 = after((got_d, recv_0), g1)
        on_d = add_second([mine_d], [recv_d], got_d)
        last_d = swap_second(on_d)
        recv_1 = swap_core(after(theirs_1, on_d))
        g2, sum2, theirs_2, mine_2 = back(2, on_d)
        last_d, recv_1, theirs_2, part_s = after((last_d, recv_1, theirs_2, part_s), g2)
        sum_s = lax.all_gather(part_s, "dp")
        recv_2 = swap_core(theirs_2)
        vec_one, vec_two = after((vec_one, vec_two), last_d)
        theirs_v, mine_v = vector_parts(place, vec_one, vec_two, [sum0, sum1, sum2], r)
        mine_e = [mine_0, mine_1, mine_2, mine_v]
        recv_e = [recv_0, recv_1, after(recv_2, theirs_v), swap_core(theirs_v)]
        to_e = add_first(mine_e, recv_e)
        got_e = swap_first(to_e)
        z_d = send_z(*add_z(place, [mine_d], [recv_d], got_d, after(last_d, to_e), True))
        token_gradient = token_call(place, after(dr1, z_d[0]), [g0, g1, g2], in_pieces)
        got_e, z_d = after((got_e, z_d), token_gradient)
        on_e = add_second(mine_e, recv_e, got_e)
        last_e = swap_second(on_e)
        sum_d = lax.all_gather(add_all(*after(z_d, on_e)), "dp")
        shrink_new = adam_turned_call((after(shrink[0], on_e), *shrink[1:]), sum_s, rate_f)
        last_e = after(last_e, shrink_new[0])
        z_e = send_z(*add_z(place, mine_e, recv_e, got_e, last_e, True))
        moves = [(0, ff // 2, model // 2), (1, 0, ff // 2)]
        sum_e = over_chips(add_all(*z_e))
        side_states = [(after(outward[0], sum_e[0]), *outward[1:]), expand]
        side_new = adam_side_call(side_states, sum_d, moves, [rate_o, rate_d])
        outward_new, expand_new = side_new[:3], side_new[3:]
        sum_e = after(sum_e, side_new[0])
        width = 3 * model // 2
        picks = [part[: vectors.shape[0], width : width + r] for part in sum_e]
        ordered = []
        for at in range(4):
            k = j ^ at
            ordered.append(
                jnp.where(k == 0, picks[0], jnp.where(k == 1, picks[1], jnp.where(k == 2, picks[2], picks[3])))
            )
        vec_sum = jnp.concatenate(ordered, 1).astype(F32)
        moves = []
        for span in range(3):
            for t in range(3):
                moves.append((span * 384 + t * 128, t * model + span * 256, 128))
        inward_new = adam_in_call(place, inward, both_cores(sum_e), moves, rate_d)
    vector_new = adam_update(*vector, vec_sum, 0.5, 0.0)
    return (
        out.reshape(tokens.shape),
        token_gradient.reshape(tokens.shape),
        *inward_new,
        *outward_new,
        *expand_new,
        *shrink_new,
        *vector_new,
    )


def solution(mesh):
    both = P(("dp", "fsdp"), None, None)
    in_specs = (both, both, P(("dp", "fsdp"))) + (P("fsdp", None),) * 12 + (P(None, "fsdp"),) * 3
    out_specs = (both, both) + (P("fsdp", None),) * 12 + (P(None, "fsdp"),) * 3
    sliced = mesh.shape["dp"] == 8 and mesh.shape["fsdp"] == 4
    step = functools.partial(local, sliced=sliced)
    return jax.shard_map(step, mesh=mesh, in_specs=in_specs, out_specs=out_specs, check_vma=False)
```

```python
import functools
import math

import jax
import jax.numpy as jnp
import numpy as np
from jax import lax
from jax.experimental import pallas as pl
from jax.experimental.pallas import tpu as pltpu
from jax.sharding import PartitionSpec as P

BF = jnp.bfloat16
F32 = jnp.float32
HEAD = 64
STEP = 10
OUT_FAN = 3
BETA_ONE = 0.5
BETA_TWO = 0.5
ADAM_EPS = 1e-08
WEIGHT_DECAY = 0.01
NORM_EPS = 1e-12
NEG_FILL = -1000000000.0
ROOT_HALF = 0.7071067811865476
INV_ROOT_TAU = 0.3989422804014327
ANY = pl.BlockSpec(memory_space=pl.ANY)


def dot_nn(a, b):
    return lax.dot_general(a, b, (((1,), (0,)), ((), ())), preferred_element_type=F32)


def dot_nt(a, b):
    return lax.dot_general(a, b, (((1,), (1,)), ((), ())), preferred_element_type=F32)


def dot_tn(a, b):
    return lax.dot_general(a, b, (((0,), (0,)), ((), ())), preferred_element_type=F32)


def params():
    return pltpu.CompilerParams(vmem_limit_bytes=64 * 1024 * 1024)


def cost(flops, moved, trans=0):
    return pl.CostEstimate(flops=int(flops), bytes_accessed=int(moved), transcendentals=int(trans))


def swap(x, even, odd=None):
    odd = even if odd is None else odd
    return lax.ppermute(x, "dp", [(i, i ^ (odd if i % 2 else even)) for i in range(8)])


def swap_core(x):
    return swap(x, 1)


def swap_first(x):
    return swap(x, 4, 2)


def swap_second(x):
    return swap(x, 2, 4)


def cross(x, bit):
    return lax.ppermute(x, "fsdp", [(i, i ^ bit) for i in range(4)])


def over_z(part):
    return tuple(cross(part, k) for k in (1, 2, 3))


def after(x, *others):
    return lax.optimization_barrier((x, *others))[0]


TURNED = (0, 2, 1, 3)


def exchanged(k, c):
    return jnp.where(c == 0, k, (k & 1) * 2 + (k >> 1))


def column_copies(place, own, pieces, dst, flat, first=0, staged=True):
    f, j, c = place
    rows, cols = own.shape
    r, h = rows // 4, cols // 2
    out = [(own, flat)]
    for refs, half in ((pieces[:4], c), (pieces[4:], 1 - c)):
        for slot, ref in enumerate(refs):
            kj = exchanged(slot, half) if staged else slot
            for kf in range(1, 4):
                start = pl.multiple_of((f ^ kf) * rows + (j ^ kj) * r, 16)
                at = dst.at[pl.ds(start, r), pl.ds(pl.multiple_of(half * h, 128), h)]
                out.append((ref.at[kf - 1, :, pl.ds(first, h)], at))
    return out


def in_copies(place, refs, dst, flat):
    if len(refs) == 1:
        return [(refs[0], dst)]
    return column_copies(place, refs[0], refs[1:], dst, flat, staged=False)


def out_copies(place, refs, dst, flat):
    if len(refs) == 2:
        return [(refs[0], dst)]
    return column_copies(place, refs[0], refs[2:], dst, flat)


def expand_copies(place, refs, dst, flat):
    if len(refs) == 2:
        return [(refs[1], dst)]
    return column_copies(place, refs[1], refs[2:], dst, flat, refs[0].shape[1] // 2)


def shrink_copies(place, refs, dst, flat):
    if len(refs) == 1:
        return [(refs[0], dst)]
    f, j, c = place
    own, pieces = refs[0], refs[1:]
    rows = own.shape[0]
    r = rows // 8
    out = [(own, flat)]
    for refs, half in ((pieces[:4], c), (pieces[4:], 1 - c)):
        for slot, ref in enumerate(refs):
            kj = exchanged(slot, half)
            for kf in range(1, 4):
                start = pl.multiple_of((f ^ kf) * rows + half * (rows // 2) + (j ^ kj) * r, 16)
                out.append((ref.at[kf - 1], dst.at[pl.ds(start, r), :]))
    return out


def own_part(place, pairs, dst, flat):
    if len(pairs) > 1:
        rows = flat.shape[0]
        dst[pl.ds(pl.multiple_of(place[0] * rows, 16), rows), :] = flat[...].astype(BF)


MOST = 25


def begin(pairs, sems):
    for i, (src, dst) in enumerate(pairs):
        pltpu.make_async_copy(src, dst, sems.at[i]).start()


def finish(pairs, sems):
    for i, (src, dst) in enumerate(pairs):
        pltpu.make_async_copy(src, dst, sems.at[i]).wait()


def place_finder(sliced):
    def place():
        f, d = lax.axis_index("fsdp"), lax.axis_index("dp")
        if not sliced:
            f, d = f * 0, d * 0
        return f, d >> 1, d & 1

    return place


def tables(length):
    lane = np.arange(128)
    angles = np.arange(length)[:, None] * (10000.0 ** (-2.0 * ((lane % HEAD) // 2) / HEAD))[None, :]
    cosine, sine = np.cos(angles), np.sin(angles)
    even = (lane % 2 == 0)[None, :]
    parts = (cosine, np.where(even, -sine, 0.0), np.where(even, 0.0, sine))
    return [jnp.asarray(part.astype(np.float32)) for part in parts]


def rotate(u, cosine, up, down):
    return u * cosine + pltpu.roll(u, 127, 1) * up + pltpu.roll(u, 1, 1) * down


def turn_columns(value, place, ref):
    f, j, c = place
    turned = value.T
    r = turned.shape[0] // 16
    for fb in range(4):
        for jb in range(4):
            start = pl.multiple_of((exchanged(j ^ jb, c) * 4 + (f ^ fb)) * r, 16)
            ref[pl.ds(start, r), :] = turned[(fb * 4 + jb) * r : (fb * 4 + jb + 1) * r].astype(BF)


def qkv_kernel(*refs, place, pieces):
    x_ref, b_ref, cos_ref, up_ref, down_ref = refs[:5]
    w_refs = refs[5 : 5 + pieces]
    o_ref, xt_ref, w_ref, flat_ref, sems = refs[5 + pieces :]

    @pl.when(pl.program_id(0) == 0)
    def _():
        copies = in_copies(place(), w_refs, w_ref, flat_ref)
        begin(copies, sems)
        finish(copies, sems)
        own_part(place(), copies, w_ref, flat_ref)

    x = x_ref[...]
    turn_columns(x.astype(F32), place(), xt_ref)
    cosine, up, down = cos_ref[...], up_ref[...], down_ref[...]
    model, width = w_ref.shape
    for col in range(0, width, 256):
        acc = dot_nn(x, w_ref[:, col : col + 256]) + b_ref[:, col : col + 256]
        for tile in range(2):
            lo = col + tile * 128
            u = acc[:, tile * 128 : (tile + 1) * 128]
            if lo < 2 * model:
                u = rotate(u, cosine, up, down)
            if lo < model:
                u = u * (1.0 / math.sqrt(HEAD))
            o_ref[:, lo : lo + 128] = u.astype(BF)


def qkv_call(place, x, weight, bias, tabs, length, block=256):
    n, model = x.shape
    per = length // block
    width = bias.shape[1]
    table = pl.BlockSpec((block, 128), lambda i: (i % per, 0))
    spec = pltpu.PrefetchScalarGridSpec(
        num_scalar_prefetch=0,
        grid=(n // block,),
        in_specs=[
            pl.BlockSpec((block, model), lambda i: (i, 0)),
            pl.BlockSpec((1, width), lambda i: (0, 0)),
            table,
            table,
            table,
        ]
        + [ANY] * len(weight),
        out_specs=[
            pl.BlockSpec((block, width), lambda i: (i, 0)),
            pl.BlockSpec((model, block), lambda i: (0, i)),
        ],
        scratch_shapes=[
            pltpu.VMEM((model, width), BF),
            pltpu.VMEM((model // 4, width), F32),
            pltpu.SemaphoreType.DMA((MOST,)),
        ],
    )
    return pl.pallas_call(
        functools.partial(qkv_kernel, place=place, pieces=len(weight)),
        grid_spec=spec,
        out_shape=[jax.ShapeDtypeStruct((n, width), BF), jax.ShapeDtypeStruct((model, n), BF)],
        cost_estimate=cost(2 * n * model * width, 2 * (n * model + model * width + n * width)),
        compiler_params=params(),
        name="qkv",
    )(x, bias, *tabs, *weight)


def attend_kernel(live_ref, q_ref, k_ref, v_ref, o_ref, qa_ref, *, block):
    length = q_ref.shape[0]
    live = live_ref[...]
    lane = lax.broadcasted_iota(jnp.int32, (length, 128), 1)
    pos = lax.broadcasted_iota(jnp.int32, (length, 128), 0)
    k, vt = k_ref[...].astype(F32), v_ref[...].astype(F32).T
    keys, values = [], []
    for h in range(2):
        own = (lane // HEAD) == h
        aux = HEAD * (1 - h)
        mask = jnp.where((lane == aux) & (pos >= live), NEG_FILL, 0.0)
        keys.append(jnp.where(own, k, mask).astype(BF))
        values.append(jnp.concatenate([vt[h * HEAD : (h + 1) * HEAD], jnp.ones((16, length), F32)], 0).astype(BF))
    lane = lax.broadcasted_iota(jnp.int32, (block, 128), 1)
    for i in range(length // block):
        rows = slice(i * block, (i + 1) * block)
        q = q_ref[rows, :].astype(F32)
        mixed, stats = [], []
        for h in range(2):
            own = (lane // HEAD) == h
            aux = HEAD * (1 - h)
            scores = dot_nt(keys[h], jnp.where(own, q, jnp.where(lane == aux, 1.0, 0.0)).astype(BF))
            top = jnp.max(scores, 0, keepdims=True)
            summed = dot_nn(values[h], jnp.exp(scores - top).astype(BF))
            total = summed[HEAD : HEAD + 1]
            mixed.append(summed[:HEAD] / total)
            shift = -(top + jnp.log(total))
            hi = shift.astype(BF).astype(F32)
            mid = (shift - hi).astype(BF).astype(F32)
            one = jnp.ones_like(hi)
            stats.append(jnp.concatenate([hi, mid, shift - hi - mid, one, jnp.zeros((HEAD - 4, block), F32)], 0))
        o_ref[rows, :] = jnp.concatenate(mixed, 0).T.astype(BF)
        extra = jnp.concatenate([stats[1], stats[0]], 0).T
        for h in range(2):
            qa_ref[h, rows, :] = jnp.where((lane // HEAD) == h, q, extra).astype(BF)


def attend_call(lengths, qkv, length, first, count, block=1024):
    n, width = qkv.shape
    rows, pairs = n // length, width // 384
    one = lambda off: pl.BlockSpec((length, 128), lambda b, p: (b, off * pairs + first + p))
    spec = pltpu.PrefetchScalarGridSpec(
        num_scalar_prefetch=0,
        grid=(rows, count),
        in_specs=[pl.BlockSpec((None, 1, 128), lambda b, p: (b, 0, 0)), one(0), one(1), one(2)],
        out_specs=[
            pl.BlockSpec((length, 128), lambda b, p: (b, p)),
            pl.BlockSpec((None, 2, length, 128), lambda b, p: (b, p, 0, 0)),
        ],
    )
    return pl.pallas_call(
        functools.partial(attend_kernel, block=block),
        grid_spec=spec,
        out_shape=[
            jax.ShapeDtypeStruct((n, count * 128), BF),
            jax.ShapeDtypeStruct((rows, 2 * count, length, 128), BF),
        ],
        cost_estimate=cost(rows * count * 32 * length * length * 128, 12 * n * count * 128, rows * count * 2 * length * length),
        compiler_params=params(),
        name="attend",
    )(lengths, qkv, qkv, qkv)


def back_kernel(
    live_ref,
    qa_ref,
    k_ref,
    v_ref,
    o_ref,
    do_ref,
    cos_ref,
    up_ref,
    down_ref,
    xt_ref,
    g_ref,
    sum_ref,
    theirs_ref,
    mine_ref,
    doa_ref,
    dqt_ref,
    acc_ref=None,
    *,
    block,
):
    length = k_ref.shape[0]
    pair, row, rows_last = pl.program_id(0), pl.program_id(1), pl.num_programs(1) - 1
    live = live_ref[...]
    lane = lax.broadcasted_iota(jnp.int32, (length, 128), 1)
    do = do_ref[...].astype(F32)
    prod = do * o_ref[...].astype(F32)
    for h in range(2):
        own = (lane // HEAD) == h
        aux = HEAD * (1 - h)
        shift = -jnp.sum(jnp.where(own, prod, 0.0), -1, keepdims=True)
        hi = shift.astype(BF).astype(F32)
        extra = jnp.where(lane == aux, hi, jnp.where(lane == aux + 1, shift - hi, 0.0))
        doa_ref[h] = jnp.where(own, do, extra).astype(BF)
    lane = lax.broadcasted_iota(jnp.int32, (block, 128), 1)
    pos = lax.broadcasted_iota(jnp.int32, (block, 128), 0)
    dk_sum = jnp.zeros((1, 128), F32)
    dv_sum = jnp.zeros((1, 128), F32)
    for i in range(length // block):
        rows = slice(i * block, (i + 1) * block)
        k, v = k_ref[rows, :].astype(F32), v_ref[rows, :].astype(F32)
        kt = k.T.astype(BF)
        dks, dvs = [], []
        for h in range(2):
            own = (lane // HEAD) == h
            aux = HEAD * (1 - h)
            mask = jnp.where((lane == aux + 3) & (pos + i * block >= live), NEG_FILL, 0.0)
            ka = jnp.where(own, k, jnp.where((lane >= aux) & (lane < aux + 3), 1.0, mask)).astype(BF)
            va = jnp.where(own, v, jnp.where((lane >= aux) & (lane < aux + 2), 1.0, 0.0)).astype(BF)
            qa, doa = qa_ref[h], doa_ref[h]
            p = jnp.exp(dot_nt(ka, qa))
            ds = (p * dot_nt(va, doa)).astype(BF)
            dvs.append(dot_nn(p.astype(BF), doa))
            dks.append(dot_nn(ds, qa))
            dqt = dot_nn(kt[h * HEAD : (h + 1) * HEAD, :], ds)
            if i == 0:
                dqt_ref[h * HEAD : (h + 1) * HEAD, :] = dqt
            else:
                dqt_ref[h * HEAD : (h + 1) * HEAD, :] += dqt
        dk = jnp.where(lane < HEAD, dks[0], dks[1])
        dk = rotate(dk, cos_ref[rows, :], -up_ref[rows, :], -down_ref[rows, :]).astype(BF)
        dv = jnp.where(lane < HEAD, dvs[0], dvs[1]).astype(BF)
        g_ref[rows, 128:256] = dk
        g_ref[rows, 256:384] = dv
        dk_sum += jnp.sum(dk.astype(F32), 0, keepdims=True)
        dv_sum += jnp.sum(dv.astype(F32), 0, keepdims=True)
    dq = rotate(dqt_ref[...].T * (1.0 / math.sqrt(HEAD)), cos_ref[...], -up_ref[...], -down_ref[...]).astype(BF)
    g_ref[:, 0:128] = dq
    sum_ref[...] = jnp.concatenate([jnp.sum(dq.astype(F32), 0, keepdims=True), dk_sum, dv_sum], -1)
    acc = dot_nn(xt_ref[...], g_ref[...])
    r = acc.shape[0] // 16

    def put(acc, ref, order):
        for slot in range(4):
            for kf in range(4):
                rows = slice((slot * 4 + kf) * r, (slot * 4 + kf + 1) * r)
                ref[order[slot], kf] = acc[rows].astype(BF)

    if acc_ref is not None:
        acc_ref[...] = jnp.where(row == 0, 0.0, acc_ref[...]) + acc

    @pl.when((pair == 0) & (row == rows_last))
    def _():
        put(acc if acc_ref is None else acc_ref[...], theirs_ref, TURNED)

    @pl.when((pair == 1) & (row == rows_last))
    def _():
        put(acc if acc_ref is None else acc_ref[...], mine_ref, (0, 1, 2, 3))


def back_call(place, lengths, seen, qkv, dattn, xt, tabs, length, span, block=256):
    attn, qa = seen
    n, width = qkv.shape
    rows, pairs = n // length, width // 384
    model = width // 3
    which = lambda p: jnp.where(p == 0, 1 - place()[2], place()[2])
    one = lambda off: pl.BlockSpec((length, 128), lambda p, b: (b, off * pairs + 2 * span + which(p)))
    table = pl.BlockSpec((length, 128), lambda *_: (0, 0))
    part = pl.BlockSpec((4, 4, model // 16, 384), lambda *_: (0, 0, 0, 0))
    spec = pltpu.PrefetchScalarGridSpec(
        num_scalar_prefetch=0,
        grid=(2, rows),
        in_specs=[
            pl.BlockSpec((None, 1, 128), lambda p, b: (b, 0, 0)),
            pl.BlockSpec((None, 2, length, 128), lambda p, b: (b, which(p), 0, 0)),
            one(1),
            one(2),
            pl.BlockSpec((length, 128), lambda p, b: (b, which(p))),
            one(0),
            table,
            table,
            table,
            pl.BlockSpec((model, length), lambda p, b, *_: (0, b)),
        ],
        out_specs=[
            pl.BlockSpec((length, 384), lambda p, b: (b, which(p))),
            pl.BlockSpec((None, None, 1, 384), lambda p, b: (b, which(p), 0, 0)),
            part,
            part,
        ],
        scratch_shapes=[pltpu.VMEM((2, length, 128), BF), pltpu.VMEM((128, length), F32)]
        + ([pltpu.VMEM((model, 384), F32)] if rows > 1 else []),
    )
    return pl.pallas_call(
        functools.partial(back_kernel, block=block),
        grid_spec=spec,
        out_shape=[
            jax.ShapeDtypeStruct((n, 768), BF),
            jax.ShapeDtypeStruct((rows, 2, 1, 384), F32),
            jax.ShapeDtypeStruct((4, 4, model // 16, 384), BF),
            jax.ShapeDtypeStruct((4, 4, model // 16, 384), BF),
        ],
        cost_estimate=cost(rows * 80 * length * length * 128, 24 * n * 128, rows * 4 * length * length),
        compiler_params=params(),
        name="attend_back",
    )(lengths, qa, qkv, qkv, attn, dattn, *tabs, xt)


def norm_forward(u):
    center = u - jnp.mean(u, -1, keepdims=True)
    inverse = lax.rsqrt(jnp.mean(center * center, -1, keepdims=True) + NORM_EPS)
    return center * inverse, inverse


def norm_backward(incoming, normed, inverse, gain):
    scaled = incoming * gain
    mean = jnp.mean(scaled, -1, keepdims=True)
    return inverse * (scaled - mean - normed * jnp.mean(scaled * normed, -1, keepdims=True))


def adder(ref):
    def add(row, value, off=0):
        ref[row : row + 1, off : off + value.shape[1]] += jnp.sum(value, 0, keepdims=True)

    return add


def turn_halves(value, place, ref, cols):
    _, j, c = place
    turned = value.T
    r = turned.shape[0] // 8
    for cb in range(2):
        for jb in range(4):
            start = pl.multiple_of(((c ^ cb) * 4 + exchanged(j ^ jb, c)) * r, 16)
            ref[pl.ds(start, r), cols] = turned[(cb * 4 + jb) * r : (cb * 4 + jb + 1) * r].astype(BF)


def ffn_kernel(*refs, place, length, chunk, attn, side, shrink, blocks):
    live_ref, x_ref, cot_ref, v_ref = refs[:4]
    at_refs = refs[4 : 4 + attn]
    side_refs = refs[4 + attn : 4 + attn + side]
    shrink_refs = refs[4 + attn + side : 4 + attn + side + shrink]
    outs = refs[4 + attn + side + shrink :]
    out_ref, yt_ref, att_ref, dpre_ref, dr1_ref, da_ref, dat_ref, dvec_ref, theirs_ref, mine_ref = outs[:10]
    wo_ref, w1_ref, w2_ref, act_ref, dzt_ref, slope_ref, flat_o, flat_1, flat_2, sem_o, sem_1, sem_2 = outs[10:]
    step = pl.program_id(0)
    block, model = x_ref.shape
    ff = w1_ref.shape[1]
    per = length // block
    live = live_ref[:, :1]
    place = place()
    vec = lambda i: v_ref[i : i + 1, :]

    @pl.when(step == 0)
    def _():
        first = out_copies(place, side_refs, wo_ref, flat_o)
        second = expand_copies(place, side_refs, w1_ref, flat_1)
        third = shrink_copies(place, shrink_refs, w2_ref, flat_2)
        begin(first, sem_o)
        begin(second, sem_1)
        begin(third, sem_2)
        dvec_ref[...] = jnp.zeros_like(dvec_ref)
        finish(first, sem_o)
        own_part(place, first, wo_ref, flat_o)
        finish(second, sem_1)
        own_part(place, second, w1_ref, flat_1)
        finish(third, sem_2)
        own_part(place, third, w2_ref, flat_2)

    @pl.when(step < blocks)
    def _():
        here = pl.ds(pl.multiple_of(step * block, block), block)
        add = adder(dvec_ref)
        at = jnp.concatenate([ref[...] for ref in at_refs], -1)
        turn_columns(at.astype(F32), place, att_ref)
        r1 = x_ref[...].astype(F32) + (dot_nn(at, wo_ref[...]) + vec(7))
        n1, i1 = norm_forward(r1)
        y1 = n1 * vec(0) + vec(2)
        y1b = y1.astype(BF)
        turn_columns(y1, place, yt_ref)
        z = jnp.zeros((block, model), F32)
        for lo in range(0, ff, chunk):
            cols = slice(lo, lo + chunk)
            bias = v_ref[9 + lo // model : 10 + lo // model, lo % model : lo % model + chunk]
            pre = dot_nn(y1b, w1_ref[:, cols]) + bias
            phi = 0.5 * (1.0 + lax.erf(pre * ROOT_HALF))
            act = (pre * phi).astype(BF)
            act_ref[here, cols] = act
            slope_ref[:, cols] = phi + pre * (jnp.exp(-0.5 * pre * pre) * INV_ROOT_TAU)
            z = z + dot_nn(act, w2_ref[cols, :])
        r2 = y1 + (z + vec(8))
        n2, i2 = norm_forward(r2)
        out_ref[...] = (n2 * vec(1) + vec(3)).astype(BF)
        pos = lax.broadcasted_iota(jnp.int32, (block, model), 0) + (step % per) * block
        e = jnp.where(pos < live, cot_ref[...].astype(F32), 0.0)
        dy = norm_backward(e, n2, i2, vec(1))
        turn_halves(dy, place, dzt_ref, here)
        dz = dy.astype(BF)
        add(1, e * n2)
        add(3, e)
        add(8, dz.astype(F32))
        for lo in range(0, ff, chunk):
            cols = slice(lo, lo + chunk)
            dpre = (dot_nt(dz, w2_ref[cols, :]) * slope_ref[:, cols]).astype(BF)
            dpre_ref[:, cols] = dpre
            add(9 + lo // model, dpre.astype(F32), lo % model)
            dy = dy + dot_nt(dpre, w1_ref[:, cols])
        add(0, dy * n1)
        add(2, dy)
        dr1 = norm_backward(dy, n1, i1, vec(0))
        dr1_ref[...] = dr1
        da = dr1.astype(BF)
        da_ref[...] = da
        add(7, da.astype(F32))
        dat_ref[...] = dot_nt(da, wo_ref[...]).astype(BF)

    @pl.when(step >= blocks)
    def _():
        kf = step - blocks
        width = ff // 4
        r = model // 8
        cols = pl.ds(pl.multiple_of((place[0] ^ kf) * width, 128), width)
        acc = dot_nn(dzt_ref[...], act_ref[:, cols])
        for slot in range(4):
            mine_ref[slot] = acc[slot * r : (slot + 1) * r].astype(BF)
            theirs_ref[TURNED[slot]] = acc[(4 + slot) * r : (5 + slot) * r].astype(BF)


def ffn_call(place, lengths, x, attn, cot, side, shrink, vec, length, block=256, chunk=768):
    n, model = x.shape
    ff = 4 * model
    blocks = n // block
    at = lambda i: jnp.minimum(i, blocks - 1)
    tok = pl.BlockSpec((block, model), lambda i, *_: (at(i), 0))
    wide = pl.BlockSpec((block, ff), lambda i, *_: (at(i), 0))
    small = pl.BlockSpec((13, model), lambda i, *_: (0, 0))
    turned = pl.BlockSpec((model, block), lambda i, *_: (0, at(i)))
    grad = pl.BlockSpec((4, None, model // 8, ff // 4), lambda i, *_: (0, jnp.maximum(i - blocks, 0), 0, 0))
    spec = pltpu.PrefetchScalarGridSpec(
        num_scalar_prefetch=0,
        grid=(blocks + 4,),
        in_specs=[pl.BlockSpec((None, 1, 128), lambda i: (at(i) // (length // block), 0, 0)), tok, tok, small]
        + [pl.BlockSpec((block, a.shape[1]), lambda i, *_: (at(i), 0)) for a in attn]
        + [ANY] * (len(side) + len(shrink)),
        out_specs=[tok, turned, turned, wide, tok, tok, tok, small, grad, grad],
        scratch_shapes=[
            pltpu.VMEM((model, model), BF),
            pltpu.VMEM((model, ff), BF),
            pltpu.VMEM((ff, model), BF),
            pltpu.VMEM((n, ff), BF),
            pltpu.VMEM((model, n), BF),
            pltpu.VMEM((block, ff), F32),
            pltpu.VMEM((model // 4, model), F32),
            pltpu.VMEM((model // 4, ff), F32),
            pltpu.VMEM((ff // 4, model), F32),
        ]
        + [pltpu.SemaphoreType.DMA((MOST,))] * 3,
    )
    s = lambda w, t: jax.ShapeDtypeStruct((n, w), t)
    flip = jax.ShapeDtypeStruct((model, n), BF)
    parts = jax.ShapeDtypeStruct((4, 4, model // 8, ff // 4), BF)
    return pl.pallas_call(
        functools.partial(
            ffn_kernel, place=place, length=length, chunk=chunk, attn=len(attn), side=len(side), shrink=len(shrink), blocks=blocks
        ),
        grid_spec=spec,
        out_shape=[
            s(model, BF),
            flip,
            flip,
            s(ff, BF),
            s(model, F32),
            s(model, BF),
            s(model, BF),
            jax.ShapeDtypeStruct((13, model), F32),
            parts,
            parts,
        ],
        cost_estimate=cost(
            2 * n * (3 * model * model + 10 * model * ff), n * (model * 20 + ff * 4) + model * ff * 4, n * ff * 2
        ),
        compiler_params=params(),
        name="ffn",
    )(lengths, x, cot, vec, *attn, *side, *shrink)


def side_grad_kernel(yt_ref, att_ref, dpre_ref, da_ref, theirs_ref, mine_ref, *, steps):
    step = pl.program_id(0)
    r = yt_ref.shape[0] // 16

    def put(acc, ref, order):
        for slot in range(4):
            for kf in range(4):
                rows = slice((slot * 4 + kf) * r, (slot * 4 + kf + 1) * r)
                ref[order[slot], kf, :, : acc.shape[1]] = acc[rows].astype(BF)

    for first, ref, order in ((0, theirs_ref, TURNED), (steps, mine_ref, (0, 1, 2, 3))):

        @pl.when((step >= first) & (step < first + steps - 1))
        def _(ref=ref, order=order):
            put(dot_nn(yt_ref[...], dpre_ref[...]), ref, order)

        @pl.when(step == first + steps - 1)
        def _(ref=ref, order=order):
            put(dot_nn(att_ref[...], da_ref[...]), ref, order)


def side_grad_call(place, yt, att, dpre, da, block=768):
    model, n = yt.shape
    half = dpre.shape[1] // 2
    steps = half // block + 1
    which = lambda i: jnp.where(i < steps, 1 - place()[2], place()[2])
    turned = pl.BlockSpec((model, n), lambda i: (0, 0))
    width = half + model // 2
    out = lambda first: pl.BlockSpec(
        (4, 4, model // 16, block), lambda i: (0, 0, 0, jnp.clip(i - first, 0, steps - 1))
    )
    spec = pltpu.PrefetchScalarGridSpec(
        num_scalar_prefetch=0,
        grid=(2 * steps,),
        in_specs=[
            turned,
            turned,
            pl.BlockSpec(
                (n, block), lambda i: (0, which(i) * (steps - 1) + jnp.minimum(i % steps, steps - 2))
            ),
            pl.BlockSpec((n, model // 2), lambda i: (0, which(i))),
        ],
        out_specs=[out(0), out(steps)],
    )
    return pl.pallas_call(
        functools.partial(side_grad_kernel, steps=steps),
        grid_spec=spec,
        out_shape=[jax.ShapeDtypeStruct((4, 4, model // 16, width), BF)] * 2,
        cost_estimate=cost(4 * n * model * width, 4 * (n * model + n * width + model * width)),
        compiler_params=params(),
        name="side_grad",
    )(yt, att, dpre, da)


def token_kernel(*refs, place, pieces, parts):
    dr1_ref = refs[0]
    g_refs = refs[1 : 1 + parts]
    w_refs = refs[1 + parts : 1 + parts + pieces]
    o_ref, w_ref, flat_ref, sems = refs[1 + parts + pieces :]
    model = w_ref.shape[0]

    @pl.when(pl.program_id(0) == 0)
    def _():
        copies = in_copies(place(), w_refs, w_ref, flat_ref)
        begin(copies, sems)
        finish(copies, sems)
        own_part(place(), copies, w_ref, flat_ref)

    total = dr1_ref[...]
    for t in range(3):
        tiles = [ref[:, lo + t * 128 : lo + (t + 1) * 128] for ref in g_refs for lo in range(0, ref.shape[1], 384)]
        total = total + dot_nt(jnp.concatenate(tiles, -1), w_ref[:, t * model : (t + 1) * model])
    o_ref[...] = total.astype(BF)


def token_call(place, dr1, grads, weight, block=256):
    n, model = dr1.shape
    tok = lambda w: pl.BlockSpec((block, w), lambda i: (i, 0))
    spec = pltpu.PrefetchScalarGridSpec(
        num_scalar_prefetch=0,
        grid=(n // block,),
        in_specs=[tok(model)] + [tok(g.shape[1]) for g in grads] + [ANY] * len(weight),
        out_specs=tok(model),
        scratch_shapes=[
            pltpu.VMEM((model, 3 * model), BF),
            pltpu.VMEM((model // 4, 3 * model), F32),
            pltpu.SemaphoreType.DMA((MOST,)),
        ],
    )
    return pl.pallas_call(
        functools.partial(token_kernel, place=place, pieces=len(weight), parts=len(grads)),
        grid_spec=spec,
        out_shape=jax.ShapeDtypeStruct((n, model), BF),
        cost_estimate=cost(6 * n * model * model, n * model * 12 + 6 * model * model),
        compiler_params=params(),
        name="token_gradient",
    )(dr1, *grads, *weight)


def sums_kernel(*refs, place, jobs):
    f, step = place()[0], pl.program_id(0)
    at = 0
    outs = refs[sum(mine + recv + got for _, mine, recv, got in jobs) :]
    for kind, mine, recv, got in jobs:
        mines = refs[at : at + mine]
        recvs = refs[at + mine : at + mine + recv]
        gots = refs[at + mine + recv : at + mine + recv + got]
        at += mine + recv + got
        lo = 0
        for i, ref in enumerate(mines):
            cols = slice(lo, lo + ref.shape[-1])
            lo += ref.shape[-1]
            total = ref[...].astype(F32)
            if i < recv:
                total = total + recvs[i][...].astype(F32)
            for other in gots:
                total = total + other[:, :, cols].astype(F32)
            total = total.astype(BF)
            if kind == "own":
                for k in range(2):
                    outs[0][k ^ (f & 1), :, cols] = total[k]
            elif kind == "split":
                for k in range(4):

                    @pl.when(step == k // 2)
                    def _(k=k, total=total, cols=cols, out=outs[k]):
                        out[:, cols] = total[k % 2]

            else:
                outs[0][..., cols] = total
        outs = outs[4 if kind == "split" else 1 :]


def sums_call(place, *jobs):
    arrays, specs, shapes, outs, heads = [], [], [], [], []
    for kind, mine, recv, got in jobs:
        r, width = mine[0].shape[2], sum(m.shape[3] for m in mine)
        slot = {"first": 1, "second": 1, "own": 0, "split": 0}[kind]
        lead = 2 if kind == "first" else None
        block = lambda a, slot=slot, lead=lead: pl.BlockSpec(
            (lead, 2) + a.shape[2:], lambda k, slot=slot: (slot, k, 0, 0)
        )
        half = lambda a: pl.BlockSpec((2,) + a.shape[1:], lambda k: (k, 0, 0))
        arrays += [*mine, *recv, *got]
        specs += [block(a) if a.ndim == 4 else half(a) for a in (*mine, *recv, *got)]
        heads.append((kind, len(mine), len(recv), len(got)))
        if kind == "first":
            shapes.append(jax.ShapeDtypeStruct((2, 4, r, width), BF))
            outs.append(pl.BlockSpec((2, 2, r, width), lambda k: (0, k, 0, 0)))
        elif kind == "split":
            shapes += [jax.ShapeDtypeStruct((r, width), BF)] * 4
            outs += [pl.BlockSpec((r, width), lambda k: (0, 0))] * 4
        else:
            shapes.append(jax.ShapeDtypeStruct((4, r, width), BF))
            turn = kind == "own"
            outs.append(
                pl.BlockSpec((2, r, width), lambda k, t=turn: (k ^ (place()[0] >> 1) if t else k, 0, 0))
            )
    spec = pltpu.PrefetchScalarGridSpec(num_scalar_prefetch=0, grid=(2,), in_specs=specs, out_specs=outs)
    moved = sum(a.size for a in arrays)
    return pl.pallas_call(
        functools.partial(sums_kernel, place=place, jobs=tuple(heads)),
        grid_spec=spec,
        out_shape=shapes,
        cost_estimate=cost(moved, 2 * moved),
        compiler_params=params(),
        name="sums",
    )(*arrays)


def plus(*parts):
    total = parts[0].astype(F32)
    for part in parts[1:]:
        total = total + part.astype(F32)
    return total.astype(BF)


def send_z(own, one, two, three):
    return own, cross(one, 1), cross(two, 2), cross(three, 3)


def over_chips(total):
    return total, swap(total, 2), swap(total, 4), swap(total, 6)


def both_cores(chips):
    return (*chips, *(swap_core(part) for part in chips))


def vector_parts_kernel(rest_ref, *refs, place):
    sums, mine_ref = refs[:-1], refs[-1]
    f, j, c = place()
    rest = rest_ref[...]
    heads = []
    for t in range(3):
        cols = slice(t * 128, (t + 1) * 128)
        tiles = [jnp.sum(ref[:, pair, :, cols], 0) for ref in sums for pair in range(2)]
        heads.append(jnp.concatenate(tiles, -1))
    value = jnp.concatenate([rest[:4], *heads, rest[7:]], 0)
    mine_ref[...] = jnp.zeros_like(mine_ref)
    rows, model = value.shape
    width = model // 16
    for fb in range(4):
        for jb in range(4):
            lo = (fb * 4 + jb) * width
            part = value[:, lo : lo + width].astype(BF)
            mine_ref[exchanged(j ^ jb, c), f ^ fb, :rows, :width] = part


def vector_parts(place, rest, sums, r):
    whole = lambda a: pl.BlockSpec(a.shape, lambda *_, k=a.ndim: (0,) * k)
    spec = pltpu.PrefetchScalarGridSpec(
        num_scalar_prefetch=0,
        grid=(1,),
        in_specs=[whole(a) for a in (rest, *sums)],
        out_specs=pl.BlockSpec((4, 4, r, 128), lambda *_: (0, 0, 0, 0)),
    )
    return pl.pallas_call(
        functools.partial(vector_parts_kernel, place=place),
        grid_spec=spec,
        out_shape=jax.ShapeDtypeStruct((4, 4, r, 128), BF),
        compiler_params=params(),
        name="vector_parts",
    )(rest, *sums)


def adam_update(master, moment, square, gradient, rate, decay):
    momentum = BETA_ONE * moment + (1.0 - BETA_ONE) * gradient
    squares = BETA_TWO * square + (1.0 - BETA_TWO) * gradient * gradient
    corrected = momentum / (1.0 - BETA_ONE**STEP)
    spread = jnp.sqrt(squares / (1.0 - BETA_TWO**STEP))
    return (master - rate * (corrected / (spread + ADAM_EPS) + decay * master), momentum, squares)


def adam_block(state, outs, g, rate):
    w, m, s = (ref[...] for ref in state)
    for ref, value in zip(outs, adam_update(w, m, s, g, rate, WEIGHT_DECAY)):
        ref[...] = value


def adam_side_kernel(*refs, weights, moves, rates):
    state, grad, outs = refs[: 3 * weights], refs[3 * weights], refs[3 * weights + 1 : 6 * weights + 1]
    flats = refs[6 * weights + 1 :]
    step = pl.program_id(0)
    rows = state[0].shape[0]

    @pl.when(step == 0)
    def _():
        r = grad.shape[1]
        for weight, src, width in moves:
            for d in range(8):
                to = slice((d % 2) * width, (d % 2 + 1) * width)
                flats[weight][d // 2 * r : (d // 2 + 1) * r, to] = grad[d, :, src : src + width]

    here = pl.ds(pl.multiple_of(step * rows, rows), rows)
    for i in range(weights):
        cut = slice(3 * i, 3 * i + 3)
        adam_block(state[cut], outs[cut], flats[i][here, :].astype(F32), rates[i])


def adam_side_call(states, grad, moves, rates, steps=2):
    rows = states[0][0].shape[0] // steps
    block = lambda a: pl.BlockSpec((rows, a.shape[1]), lambda i: (i, 0))
    flat = [a for state in states for a in state]
    size = sum(a.size for a in flat)
    return pl.pallas_call(
        functools.partial(adam_side_kernel, weights=len(states), moves=tuple(moves), rates=tuple(rates)),
        grid=(steps,),
        in_specs=[block(a) for a in flat] + [pl.BlockSpec(grad.shape, lambda i: (0, 0, 0))],
        out_specs=[block(a) for a in flat],
        scratch_shapes=[pltpu.VMEM(state[0].shape, BF) for state in states],
        out_shape=[jax.ShapeDtypeStruct(a.shape, F32) for a in flat],
        cost_estimate=cost(size * 4, size * 9),
        compiler_params=params(),
        name="adam_side",
    )(*flat, grad)


def adam_in_kernel(*refs, place, moves, rate, first):
    state, vector, grads, outs, vector_outs = refs[:3], refs[3:6], refs[6:14], refs[14:17], refs[17:20]
    flat, vector_flat = refs[20:]
    _, j, c = place()
    step = pl.program_id(0)
    rows = state[0].shape[0]

    @pl.when(step == 0)
    def _():
        for i, ref in enumerate(grads):
            half = c if i < 4 else 1 - c
            r = ref.shape[0]
            here = pl.ds(pl.multiple_of((j ^ (i % 4)) * r, 16), r)
            for src, to, stride in moves:
                cols = pl.ds(pl.multiple_of(to + half * stride, 128), 128)
                flat[here, cols] = ref[:, src : src + 128]
        count, width = vector_flat.shape
        width = width // 4
        both = lambda k: grads[k][:, first : first + 128].astype(F32) + grads[k + 4][:, first : first + 128].astype(F32)
        parts = [both(k) for k in range(4)]
        for at in range(4):
            k = j ^ at
            part = jnp.where(k == 0, parts[0], jnp.where(k == 1, parts[1], jnp.where(k == 2, parts[2], parts[3])))
            vector_flat[:, at * width : (at + 1) * width] = part[:count, :width]
        w, m, s = (ref[...] for ref in vector)
        for ref, value in zip(vector_outs, adam_update(w, m, s, vector_flat[...], 0.5, 0.0)):
            ref[...] = value

    here = pl.ds(pl.multiple_of(step * rows, rows), rows)
    adam_block(state, outs, flat[here, :].astype(F32), rate)


def adam_in_call(place, state, vector, grads, moves, rate, first, steps=2):
    rows = state[0].shape[0] // steps
    block = pl.BlockSpec((rows, state[0].shape[1]), lambda i: (i, 0))
    small = pl.BlockSpec(vector[0].shape, lambda i: (0, 0))
    return pl.pallas_call(
        functools.partial(adam_in_kernel, place=place, moves=tuple(moves), rate=rate, first=first),
        grid=(steps,),
        in_specs=[block] * 3 + [small] * 3 + [pl.BlockSpec(g.shape, lambda i: (0, 0)) for g in grads],
        out_specs=[block] * 3 + [small] * 3,
        scratch_shapes=[pltpu.VMEM(state[0].shape, BF), pltpu.VMEM(vector[0].shape, F32)],
        out_shape=[jax.ShapeDtypeStruct(state[0].shape, F32)] * 3 + [jax.ShapeDtypeStruct(vector[0].shape, F32)] * 3,
        cost_estimate=cost(state[0].size * 12, state[0].size * 28),
        compiler_params=params(),
        name="adam_in",
    )(*state, *vector, *grads)


def adam_turned_kernel(*refs, rate):
    state, grad, outs, (flat_ref, g_ref) = refs[:3], refs[3], refs[4:7], refs[7:]
    step = pl.program_id(0)
    rows = state[0].shape[0]

    @pl.when(step == 0)
    def _():
        r = grad.shape[1]
        for d in range(8):
            at = (d % 2) * 4 + d // 2
            flat_ref[at * r : (at + 1) * r, :] = grad[d].astype(F32)
        g_ref[...] = flat_ref[...].T

    adam_block(state, outs, g_ref[pl.ds(pl.multiple_of(step * rows, rows), rows), :], rate)


def adam_turned_call(state, grad, rate, steps=2):
    total, cols = state[0].shape
    block = pl.BlockSpec((total // steps, cols), lambda i: (i, 0))
    return pl.pallas_call(
        functools.partial(adam_turned_kernel, rate=rate),
        grid=(steps,),
        in_specs=[block] * 3 + [pl.BlockSpec(grad.shape, lambda i: (0, 0, 0))],
        out_specs=[block] * 3,
        scratch_shapes=[pltpu.VMEM((cols, total), F32), pltpu.VMEM((total, cols), F32)],
        out_shape=[jax.ShapeDtypeStruct(state[0].shape, F32)] * 3,
        cost_estimate=cost(total * cols * 12, total * cols * 28),
        compiler_params=params(),
        name="adam_turned",
    )(*state, grad)


def vector_rows(rest, sums):
    heads = jnp.concatenate([jnp.sum(s, 0) for s in sums], 0).reshape(-1, 3, 128)
    heads = heads.transpose(1, 0, 2).reshape(3, -1)
    return jnp.concatenate([rest[:4], heads, rest[7:]], 0)


def local(
    tokens,
    cotangent,
    lengths,
    inward_weight,
    inward_moment,
    inward_square,
    outward_weight,
    outward_moment,
    outward_square,
    expand_weight,
    expand_moment,
    expand_square,
    shrink_weight,
    shrink_moment,
    shrink_square,
    vectors,
    vector_moment,
    vector_square,
    sliced,
):
    _, length, model = tokens.shape
    x, cot = tokens.reshape(-1, model), cotangent.reshape(-1, model)
    tabs = tables(length)
    ff = 4 * model
    pairs = model // 128
    inward = (inward_weight, inward_moment, inward_square)
    outward = (outward_weight, outward_moment, outward_square)
    expand = (expand_weight, expand_moment, expand_square)
    shrink = (shrink_weight, shrink_moment, shrink_square)
    vector = (vectors, vector_moment, vector_square)
    rate_d, rate_o, rate_f = 1.0 / math.sqrt(model), 1.0 / math.sqrt(OUT_FAN), 1.0 / math.sqrt(ff)
    f, d = lax.axis_index("fsdp"), lax.axis_index("dp")
    j, c = d // 2, d % 2
    place = place_finder(sliced)
    lengths = jnp.broadcast_to(lengths[:, None, None], (lengths.shape[0], 1, 128))
    spans = [(0, 2), (2, 2), (4, 2)]

    if not sliced:
        low = [w.astype(BF) for w in (inward_weight, outward_weight, expand_weight, shrink_weight, vectors)]
        whole = [lax.all_gather(w, "fsdp", axis=0, tiled=True) for w in low[:4]]
        in_pieces, side_pieces, shrink_pieces = (whole[0],), (whole[1], whole[2]), (whole[3],)
        vec = lax.all_gather(low[4], "fsdp", axis=1, tiled=True).astype(F32)
        qkv, xt = qkv_call(place, x, in_pieces, vec[4:7].reshape(1, -1), tabs, length)
        seen = [attend_call(lengths, qkv, length, *span) for span in spans]
        out, yt, att, dpre, dr1, da, dattn, vec_rest, far, near = ffn_call(
            place, lengths, x, [a for a, _ in seen], cot, side_pieces, shrink_pieces, vec, length
        )
        order = jnp.array(TURNED)
        shrink_grad = jnp.concatenate([near, far[order]]).transpose(1, 3, 0, 2).reshape(ff, model)
        far, near = side_grad_call(place, yt, att, dpre, da)
        both = jnp.stack([near, far[order]]).transpose(2, 1, 3, 0, 4).reshape(model, 2, -1)
        expand_grad = both[:, :, : ff // 2].reshape(model, ff)
        outward_grad = both[:, :, ff // 2 :].reshape(model, model)
        backs = [back_call(place, lengths, seen[i], qkv, dattn, xt, tabs, length, i) for i in range(len(spans))]
        token_gradient = token_call(place, dr1, [b[0] for b in backs], in_pieces)
        parts = jnp.stack([part for _, _, far, near in backs for part in (near, far[order])])
        parts = parts.transpose(2, 1, 3, 0, 4).reshape(model, pairs, 3, 128)
        inward_grad = parts.transpose(0, 2, 1, 3).reshape(model, 3 * model)

        def reduced(g, axis=0):
            return lax.psum(lax.psum_scatter(g, "fsdp", scatter_dimension=axis, tiled=True).astype(F32), "dp")

        inward_new = adam_update(*inward, reduced(inward_grad), rate_d, WEIGHT_DECAY)
        outward_new = adam_update(*outward, reduced(outward_grad), rate_o, WEIGHT_DECAY)
        expand_new = adam_update(*expand, reduced(expand_grad), rate_d, WEIGHT_DECAY)
        shrink_new = adam_update(*shrink, reduced(shrink_grad), rate_f, WEIGHT_DECAY)
        vec_sum = reduced(vector_rows(vec_rest, [b[1] for b in backs]), 1)
        vector_new = adam_update(*vector, vec_sum, 0.5, 0.0)
    else:
        shard = model // 4
        r = shard // 4

        def columns(w):
            half = w.shape[1] // 2
            return lax.dynamic_slice(w, (j * r, c * half), (r, half))

        def rows(w):
            r = w.shape[0] // 8
            return lax.dynamic_slice(w, ((c * 4 + j) * r, 0), (r, w.shape[1]))

        low_vec = vectors.astype(BF)
        third = r + r // 3
        beside = jnp.pad(low_vec.reshape(-1, third), ((0, r - 3 * vectors.shape[0]), (0, 128 - third)))
        part_in = jnp.concatenate([columns(inward_weight).astype(BF), beside], -1)
        part_side = jnp.concatenate([columns(outward_weight), columns(expand_weight)], -1).astype(BF)
        part_shrink = rows(shrink_weight).astype(BF)
        z_in = after(jnp.stack(over_z(part_in)), part_side, part_shrink)
        chips_in, z_side = after((over_chips(z_in), over_z(after(part_side, z_in))))
        in_pieces = (inward_weight, *both_cores(chips_in))
        by = z_in[:, : 3 * vectors.shape[0], part_in.shape[1] - 128 : part_in.shape[1] - 128 + third]
        by = (low_vec, *by.reshape(3, vectors.shape[0], shard))
        ordered = []
        for at in range(4):
            k = f ^ at
            ordered.append(jnp.where(k == 0, by[0], jnp.where(k == 1, by[1], jnp.where(k == 2, by[2], by[3]))))
        vec = jnp.concatenate(ordered, 1).astype(F32)
        z_side = jnp.stack(z_side)
        first_side, second_side = swap_first(z_side), swap_second(z_side)
        qkv, xt = qkv_call(place, x, after(in_pieces, z_side, vec), vec[4:7].reshape(1, -1), tabs, length)
        first_side, second_side = after((first_side, second_side), qkv)
        third_side = swap_second(first_side)
        z_shrink = over_z(after(part_shrink, first_side))
        far_z_side = swap_core(after(z_side, qkv))
        seen = [attend_call(lengths, after(qkv, first_side), length, *spans[0])]
        third_side, far_z_side, z_shrink = after((third_side, far_z_side, z_shrink), seen[0])
        z_shrink = jnp.stack(z_shrink)
        first_shrink, second_shrink = swap_first(z_shrink), swap_second(z_shrink)
        far_side = tuple(swap_core(part) for part in after((second_side, first_side, third_side), z_shrink))
        seen.append(attend_call(lengths, after(qkv, third_side, z_shrink), length, *spans[1]))
        first_shrink, second_shrink, far_side = after((first_shrink, second_shrink, far_side), seen[1])
        third_shrink = swap_second(first_shrink)
        shrink_near = (z_shrink, second_shrink, first_shrink)
        shrink_far = tuple(swap_core(part) for part in shrink_near)
        side_pieces = (outward_weight, expand_weight, z_side, second_side, first_side, third_side, far_z_side, *far_side)
        seen.append(attend_call(lengths, after(qkv, first_shrink), length, *spans[2]))
        third_shrink, shrink_far = after((third_shrink, shrink_far), seen[2])
        shrink_pieces = (shrink_weight, *shrink_near, third_shrink, *shrink_far, swap_core(third_shrink))

        out, yt, att, dpre, dr1, da, dattn, vec_rest, theirs_s, mine_s = ffn_call(
            place, lengths, x, [a for a, _ in seen], cot, side_pieces, shrink_pieces, vec, length
        )

        def back(span, *wait):
            return back_call(place, lengths, seen[span], qkv, after(dattn, *wait), xt, tabs, length, span)

        recv_s = swap_core(theirs_s)
        theirs_d, mine_d = side_grad_call(place, yt, att, dpre, da)
        recv_s = after(recv_s, theirs_d)
        to_s = sums_call(place, ("first", [mine_s], [recv_s], []))[0]
        got_s = swap_first(to_s)
        recv_d = swap_core(after(theirs_d, to_s))
        g0, sum0, theirs_0, mine_0 = back(0, to_s)
        got_s, recv_d = after((got_s, recv_d), g0)
        on_s, to_d = sums_call(place, ("second", [mine_s], [recv_s], [got_s]), ("first", [mine_d], [recv_d], []))
        last_s, got_d = swap_second(on_s), swap_first(to_d)
        recv_0 = swap_core(after(theirs_0, to_d))
        g1, sum1, theirs_1, mine_1 = back(1, to_d)
        got_d, last_s, recv_0 = after((got_d, last_s, recv_0), g1)
        on_d, z_s = sums_call(
            place, ("second", [mine_d], [recv_d], [got_d]), ("own", [mine_s], [recv_s], [got_s, last_s])
        )
        last_d = swap_second(on_d)
        recv_1 = swap_core(after(theirs_1, on_d))
        part_s = lax.psum_scatter(z_s, "fsdp", scatter_dimension=0)
        g2, sum2, theirs_2, mine_2 = back(2, on_d)
        last_d, recv_1, theirs_2, part_s = after((last_d, recv_1, theirs_2, part_s), g2)
        sum_s = lax.all_gather(part_s, "dp")
        recv_2 = swap_core(theirs_2)
        mine_v = vector_parts(place, after(vec_rest, last_d), [sum0, sum1, sum2], r)
        mine_e = [mine_0, mine_1, mine_2, mine_v]
        recv_e = [recv_0, recv_1, after(recv_2, mine_v)]
        to_e = sums_call(place, ("first", mine_e, recv_e, []))[0]
        got_e = swap_first(to_e)
        z_d = send_z(*sums_call(place, ("split", [mine_d], [recv_d], [got_d, after(last_d, to_e)])))
        token_gradient = token_call(place, after(dr1, z_d[0]), [g0, g1, g2], in_pieces)
        got_e, z_d = after((got_e, z_d), token_gradient)
        on_e = sums_call(place, ("second", mine_e, recv_e, [got_e]))[0]
        last_e = swap_second(on_e)
        sum_d = lax.all_gather(plus(*after(z_d, on_e)), "dp")
        shrink_new = adam_turned_call((after(shrink[0], on_e), *shrink[1:]), sum_s, rate_f)
        last_e = after(last_e, shrink_new[0])
        z_e = send_z(*sums_call(place, ("split", mine_e, recv_e, [got_e, last_e])))
        moves = [(0, ff // 2, model // 2), (1, 0, ff // 2)]
        sum_e = over_chips(plus(*z_e))
        side_states = [(after(outward[0], sum_e[0]), *outward[1:]), expand]
        side_new = adam_side_call(side_states, sum_d, moves, [rate_o, rate_d])
        outward_new, expand_new = side_new[:3], side_new[3:]
        sum_e = both_cores(after(sum_e, side_new[0]))
        moves = []
        for span in range(3):
            for t in range(3):
                moves.append((span * 384 + t * 128, t * model + span * 256, 128))
        both_new = adam_in_call(place, inward, vector, sum_e, moves, rate_d, 3 * model // 2)
        inward_new, vector_new = both_new[:3], both_new[3:]
    return (
        out.reshape(tokens.shape),
        token_gradient.reshape(tokens.shape),
        *inward_new,
        *outward_new,
        *expand_new,
        *shrink_new,
        *vector_new,
    )


def solution(mesh):
    both = P(("dp", "fsdp"), None, None)
    in_specs = (both, both, P(("dp", "fsdp"))) + (P("fsdp", None),) * 12 + (P(None, "fsdp"),) * 3
    out_specs = (both, both) + (P("fsdp", None),) * 12 + (P(None, "fsdp"),) * 3
    sliced = mesh.shape["dp"] == 8 and mesh.shape["fsdp"] == 4
    step = functools.partial(local, sliced=sliced)
    return jax.shard_map(step, mesh=mesh, in_specs=in_specs, out_specs=out_specs, check_vma=False)
```

```python
import functools
import math

import jax
import jax.numpy as jnp
import numpy as np
from jax import lax
from jax.experimental import pallas as pl
from jax.experimental.pallas import tpu as pltpu
from jax.sharding import PartitionSpec as P

BF = jnp.bfloat16
F32 = jnp.float32
HEAD = 64
STEP = 10
OUT_FAN = 3
BETA_ONE = 0.5
BETA_TWO = 0.5
ADAM_EPS = 1e-08
WEIGHT_DECAY = 0.01
NORM_EPS = 1e-12
NEG_FILL = -1000000000.0
ROOT_HALF = 0.7071067811865476
INV_ROOT_TAU = 0.3989422804014327
ANY = pl.BlockSpec(memory_space=pl.ANY)


def dot_nn(a, b):
    return lax.dot_general(a, b, (((1,), (0,)), ((), ())), preferred_element_type=F32)


def dot_nt(a, b):
    return lax.dot_general(a, b, (((1,), (1,)), ((), ())), preferred_element_type=F32)


def dot_tn(a, b):
    return lax.dot_general(a, b, (((0,), (0,)), ((), ())), preferred_element_type=F32)


def params():
    return pltpu.CompilerParams(vmem_limit_bytes=64 * 1024 * 1024)


def cost(flops, moved, trans=0):
    return pl.CostEstimate(flops=int(flops), bytes_accessed=int(moved), transcendentals=int(trans))


def swap(x, even, odd=None):
    odd = even if odd is None else odd
    return lax.ppermute(x, "dp", [(i, i ^ (odd if i % 2 else even)) for i in range(8)])


def swap_core(x):
    return swap(x, 1)


def swap_first(x):
    return swap(x, 4, 2)


def swap_second(x):
    return swap(x, 2, 4)


def cross(x, bit):
    return lax.ppermute(x, "fsdp", [(i, i ^ bit) for i in range(4)])


def over_z(part):
    return tuple(cross(part, k) for k in (1, 2, 3))


def after(x, *others):
    return lax.optimization_barrier((x, *others))[0]


TURNED = (0, 2, 1, 3)


def exchanged(k, c):
    return jnp.where(c == 0, k, (k & 1) * 2 + (k >> 1))


def column_copies(place, own, pieces, dst, flat, first=0, staged=True):
    f, j, c = place
    rows, cols = own.shape
    r, h = rows // 4, cols // 2
    out = [(own, flat)]
    for refs, half in ((pieces[:4], c), (pieces[4:], 1 - c)):
        for slot, ref in enumerate(refs):
            kj = exchanged(slot, half) if staged else slot
            for kf in range(1, 4):
                start = pl.multiple_of((f ^ kf) * rows + (j ^ kj) * r, 16)
                at = dst.at[pl.ds(start, r), pl.ds(pl.multiple_of(half * h, 128), h)]
                out.append((ref.at[kf - 1, :, pl.ds(first, h)], at))
    return out


def in_copies(place, refs, dst, flat):
    if len(refs) == 1:
        return [(refs[0], dst)]
    return column_copies(place, refs[0], refs[1:], dst, flat, staged=False)


def out_copies(place, refs, dst, flat):
    if len(refs) == 2:
        return [(refs[0], dst)]
    return column_copies(place, refs[0], refs[2:], dst, flat)


def expand_copies(place, refs, dst, flat):
    if len(refs) == 2:
        return [(refs[1], dst)]
    return column_copies(place, refs[1], refs[2:], dst, flat, refs[0].shape[1] // 2)


def shrink_copies(place, refs, dst, flat):
    if len(refs) == 1:
        return [(refs[0], dst)]
    f, j, c = place
    own, pieces = refs[0], refs[1:]
    rows = own.shape[0]
    r = rows // 8
    out = [(own, flat)]
    for refs, half in ((pieces[:4], c), (pieces[4:], 1 - c)):
        for slot, ref in enumerate(refs):
            kj = exchanged(slot, half)
            for kf in range(1, 4):
                start = pl.multiple_of((f ^ kf) * rows + half * (rows // 2) + (j ^ kj) * r, 16)
                out.append((ref.at[kf - 1], dst.at[pl.ds(start, r), :]))
    return out


def own_part(place, pairs, dst, flat):
    if len(pairs) > 1:
        rows = flat.shape[0]
        dst[pl.ds(pl.multiple_of(place[0] * rows, 16), rows), :] = flat[...].astype(BF)


MOST = 25


def begin(pairs, sems):
    for i, (src, dst) in enumerate(pairs):
        pltpu.make_async_copy(src, dst, sems.at[i]).start()


def finish(pairs, sems):
    for i, (src, dst) in enumerate(pairs):
        pltpu.make_async_copy(src, dst, sems.at[i]).wait()


def place_finder(sliced):
    def place():
        f, d = lax.axis_index("fsdp"), lax.axis_index("dp")
        if not sliced:
            f, d = f * 0, d * 0
        return f, d >> 1, d & 1

    return place


def tables(length):
    lane = np.arange(128)
    angles = np.arange(length)[:, None] * (10000.0 ** (-2.0 * ((lane % HEAD) // 2) / HEAD))[None, :]
    sine = np.where((lane % 2 == 0)[None, :], -np.sin(angles), np.sin(angles))
    return [jnp.asarray(part.astype(np.float32)) for part in (np.cos(angles), sine)]


def rotate(u, cosine, sine):
    even = lax.broadcasted_iota(jnp.int32, u.shape, 1) % 2 == 0
    return u * cosine + jnp.where(even, pltpu.roll(u, 127, 1), pltpu.roll(u, 1, 1)) * sine


def turn_columns(value, place, ref):
    f, j, c = place
    turned = value.T
    r = turned.shape[0] // 16
    for fb in range(4):
        for jb in range(4):
            start = pl.multiple_of((exchanged(j ^ jb, c) * 4 + (f ^ fb)) * r, 16)
            ref[pl.ds(start, r), :] = turned[(fb * 4 + jb) * r : (fb * 4 + jb + 1) * r].astype(BF)


def qkv_kernel(*refs, place, pieces):
    x_ref, b_ref, cos_ref, sin_ref = refs[:4]
    w_refs = refs[4 : 4 + pieces]
    o_ref, xt_ref, w_ref, flat_ref, sems = refs[4 + pieces :]

    @pl.when(pl.program_id(0) == 0)
    def _():
        copies = in_copies(place(), w_refs, w_ref, flat_ref)
        begin(copies, sems)
        finish(copies, sems)
        own_part(place(), copies, w_ref, flat_ref)

    x = x_ref[...]
    turn_columns(x.astype(F32), place(), xt_ref)
    cosine, sine = cos_ref[...], sin_ref[...]
    model, width = w_ref.shape
    for col in range(0, width, 256):
        acc = dot_nn(x, w_ref[:, col : col + 256]) + b_ref[:, col : col + 256]
        for tile in range(2):
            lo = col + tile * 128
            u = acc[:, tile * 128 : (tile + 1) * 128]
            if lo < 2 * model:
                u = rotate(u, cosine, sine)
            if lo < model:
                u = u * (1.0 / math.sqrt(HEAD))
            o_ref[:, lo : lo + 128] = u.astype(BF)


def qkv_call(place, x, weight, bias, tabs, length, block=256):
    n, model = x.shape
    per = length // block
    width = bias.shape[1]
    table = pl.BlockSpec((block, 128), lambda i: (i % per, 0))
    spec = pltpu.PrefetchScalarGridSpec(
        num_scalar_prefetch=0,
        grid=(n // block,),
        in_specs=[
            pl.BlockSpec((block, model), lambda i: (i, 0)),
            pl.BlockSpec((1, width), lambda i: (0, 0)),
            table,
            table,
        ]
        + [ANY] * len(weight),
        out_specs=[
            pl.BlockSpec((block, width), lambda i: (i, 0)),
            pl.BlockSpec((model, block), lambda i: (0, i)),
        ],
        scratch_shapes=[
            pltpu.VMEM((model, width), BF),
            pltpu.VMEM((model // 4, width), F32),
            pltpu.SemaphoreType.DMA((MOST,)),
        ],
    )
    return pl.pallas_call(
        functools.partial(qkv_kernel, place=place, pieces=len(weight)),
        grid_spec=spec,
        out_shape=[jax.ShapeDtypeStruct((n, width), BF), jax.ShapeDtypeStruct((model, n), BF)],
        cost_estimate=cost(2 * n * model * width, 2 * (n * model + model * width + n * width)),
        compiler_params=params(),
        name="qkv",
    )(x, bias, *tabs, *weight)


def attend_kernel(live_ref, q_ref, k_ref, v_ref, o_ref, qa_ref, *, block):
    length = q_ref.shape[0]
    live = live_ref[...]
    lane = lax.broadcasted_iota(jnp.int32, (length, 128), 1)
    pos = lax.broadcasted_iota(jnp.int32, (length, 128), 0)
    k, vt = k_ref[...].astype(F32), v_ref[...].astype(F32).T
    keys, values = [], []
    for h in range(2):
        own = (lane // HEAD) == h
        aux = HEAD * (1 - h)
        mask = jnp.where((lane == aux) & (pos >= live), NEG_FILL, 0.0)
        keys.append(jnp.where(own, k, mask).astype(BF))
        values.append(jnp.concatenate([vt[h * HEAD : (h + 1) * HEAD], jnp.ones((16, length), F32)], 0).astype(BF))
    lane = lax.broadcasted_iota(jnp.int32, (block, 128), 1)
    for i in range(length // block):
        rows = slice(i * block, (i + 1) * block)
        q = q_ref[rows, :].astype(F32)
        mixed, stats = [], []
        for h in range(2):
            own = (lane // HEAD) == h
            aux = HEAD * (1 - h)
            scores = dot_nt(keys[h], jnp.where(own, q, jnp.where(lane == aux, 1.0, 0.0)).astype(BF))
            top = jnp.max(scores, 0, keepdims=True)
            summed = dot_nn(values[h], jnp.exp(scores - top).astype(BF))
            total = summed[HEAD : HEAD + 1]
            mixed.append(summed[:HEAD] / total)
            shift = -(top + jnp.log(total))
            hi = shift.astype(BF).astype(F32)
            mid = (shift - hi).astype(BF).astype(F32)
            one = jnp.ones_like(hi)
            stats.append(jnp.concatenate([hi, mid, shift - hi - mid, one, jnp.zeros((HEAD - 4, block), F32)], 0))
        o_ref[rows, :] = jnp.concatenate(mixed, 0).T.astype(BF)
        extra = jnp.concatenate([stats[1], stats[0]], 0).T
        for h in range(2):
            qa_ref[h, rows, :] = jnp.where((lane // HEAD) == h, q, extra).astype(BF)


def attend_call(lengths, qkv, length, first, count, block=1024):
    n, width = qkv.shape
    rows, pairs = n // length, width // 384
    one = lambda off: pl.BlockSpec((length, 128), lambda b, p: (b, off * pairs + first + p))
    spec = pltpu.PrefetchScalarGridSpec(
        num_scalar_prefetch=0,
        grid=(rows, count),
        in_specs=[pl.BlockSpec((None, 1, 128), lambda b, p: (b, 0, 0)), one(0), one(1), one(2)],
        out_specs=[
            pl.BlockSpec((length, 128), lambda b, p: (b, p)),
            pl.BlockSpec((None, 2, length, 128), lambda b, p: (b, p, 0, 0)),
        ],
    )
    return pl.pallas_call(
        functools.partial(attend_kernel, block=block),
        grid_spec=spec,
        out_shape=[
            jax.ShapeDtypeStruct((n, count * 128), BF),
            jax.ShapeDtypeStruct((rows, 2 * count, length, 128), BF),
        ],
        cost_estimate=cost(rows * count * 32 * length * length * 128, 12 * n * count * 128, rows * count * 2 * length * length),
        compiler_params=params(),
        name="attend",
    )(lengths, qkv, qkv, qkv)


def back_kernel(*refs, block, part):
    live_ref, qa_ref, k_ref, v_ref, o_ref, do_ref, cos_ref, sin_ref, xt_ref = refs[:9]
    rest = refs[11:] if part == 1 else refs[9:]
    g_ref, sum_ref, *rest = rest
    theirs_ref = mine_ref = None
    if part != 1:
        theirs_ref, *rest = rest
    if part != 0:
        mine_ref, *rest = rest
    doa_ref, dqt_ref, *rest = rest
    acc_ref = rest[0] if rest else None
    length = k_ref.shape[0]
    pair, row, rows_last = pl.program_id(0) + (part or 0), pl.program_id(1), pl.num_programs(1) - 1
    live = live_ref[...]
    lane = lax.broadcasted_iota(jnp.int32, (length, 128), 1)
    do = do_ref[...].astype(F32)
    prod = do * o_ref[...].astype(F32)
    for h in range(2):
        own = (lane // HEAD) == h
        aux = HEAD * (1 - h)
        shift = -jnp.sum(jnp.where(own, prod, 0.0), -1, keepdims=True)
        hi = shift.astype(BF).astype(F32)
        extra = jnp.where(lane == aux, hi, jnp.where(lane == aux + 1, shift - hi, 0.0))
        doa_ref[h] = jnp.where(own, do, extra).astype(BF)
    lane = lax.broadcasted_iota(jnp.int32, (block, 128), 1)
    pos = lax.broadcasted_iota(jnp.int32, (block, 128), 0)
    dk_sum = jnp.zeros((1, 128), F32)
    dv_sum = jnp.zeros((1, 128), F32)
    for i in range(length // block):
        rows = slice(i * block, (i + 1) * block)
        k, v = k_ref[rows, :].astype(F32), v_ref[rows, :].astype(F32)
        kt = k.T.astype(BF)
        dks, dvs = [], []
        for h in range(2):
            own = (lane // HEAD) == h
            aux = HEAD * (1 - h)
            mask = jnp.where((lane == aux + 3) & (pos + i * block >= live), NEG_FILL, 0.0)
            ka = jnp.where(own, k, jnp.where((lane >= aux) & (lane < aux + 3), 1.0, mask)).astype(BF)
            va = jnp.where(own, v, jnp.where((lane >= aux) & (lane < aux + 2), 1.0, 0.0)).astype(BF)
            qa, doa = qa_ref[h], doa_ref[h]
            p = jnp.exp(dot_nt(ka, qa))
            ds = (p * dot_nt(va, doa)).astype(BF)
            dvs.append(dot_nn(p.astype(BF), doa))
            dks.append(dot_nn(ds, qa))
            dqt = dot_nn(kt[h * HEAD : (h + 1) * HEAD, :], ds)
            if i == 0:
                dqt_ref[h * HEAD : (h + 1) * HEAD, :] = dqt
            else:
                dqt_ref[h * HEAD : (h + 1) * HEAD, :] += dqt
        dk = jnp.where(lane < HEAD, dks[0], dks[1])
        dk = rotate(dk, cos_ref[rows, :], -sin_ref[rows, :]).astype(BF)
        dv = jnp.where(lane < HEAD, dvs[0], dvs[1]).astype(BF)
        g_ref[rows, 128:256] = dk
        g_ref[rows, 256:384] = dv
        dk_sum += jnp.sum(dk.astype(F32), 0, keepdims=True)
        dv_sum += jnp.sum(dv.astype(F32), 0, keepdims=True)
    dq = rotate(dqt_ref[...].T * (1.0 / math.sqrt(HEAD)), cos_ref[...], -sin_ref[...]).astype(BF)
    g_ref[:, 0:128] = dq
    sum_ref[...] = jnp.concatenate([jnp.sum(dq.astype(F32), 0, keepdims=True), dk_sum, dv_sum], -1)
    acc = dot_nn(xt_ref[...], g_ref[...])
    r = acc.shape[0] // 16

    def put(acc, ref, order):
        for slot in range(4):
            for kf in range(4):
                rows = slice((slot * 4 + kf) * r, (slot * 4 + kf + 1) * r)
                ref[order[slot], kf] = acc[rows].astype(BF)

    if acc_ref is not None:
        acc_ref[...] = jnp.where(row == 0, 0.0, acc_ref[...]) + acc

    if theirs_ref is not None:

        @pl.when((pair == 0) & (row == rows_last))
        def _():
            put(acc if acc_ref is None else acc_ref[...], theirs_ref, TURNED)

    if mine_ref is not None:

        @pl.when((pair == 1) & (row == rows_last))
        def _():
            put(acc if acc_ref is None else acc_ref[...], mine_ref, (0, 1, 2, 3))


def back_call(place, lengths, seen, qkv, dattn, xt, tabs, length, span, part=None, into=(), block=256):
    attn, qa = seen
    n, width = qkv.shape
    rows, pairs = n // length, width // 384
    model = width // 3
    which = lambda p: jnp.where(p + (part or 0) == 0, 1 - place()[2], place()[2])
    one = lambda off: pl.BlockSpec((length, 128), lambda p, b: (b, off * pairs + 2 * span + which(p)))
    table = pl.BlockSpec((length, 128), lambda *_: (0, 0))
    grad = pl.BlockSpec((4, 4, model // 16, 384), lambda *_: (0, 0, 0, 0))
    grads = 2 if part is None else 1
    spec = pltpu.PrefetchScalarGridSpec(
        num_scalar_prefetch=0,
        grid=(grads, rows),
        in_specs=[
            pl.BlockSpec((None, 1, 128), lambda p, b: (b, 0, 0)),
            pl.BlockSpec((None, 2, length, 128), lambda p, b: (b, which(p), 0, 0)),
            one(1),
            one(2),
            pl.BlockSpec((length, 128), lambda p, b: (b, which(p))),
            one(0),
            table,
            table,
            pl.BlockSpec((model, length), lambda p, b: (0, b)),
        ]
        + [ANY] * len(into),
        out_specs=[
            pl.BlockSpec((length, 384), lambda p, b: (b, which(p))),
            pl.BlockSpec((None, None, 1, 384), lambda p, b: (b, which(p), 0, 0)),
        ]
        + [grad] * grads,
        scratch_shapes=[pltpu.VMEM((2, length, 128), BF), pltpu.VMEM((128, length), F32)]
        + ([pltpu.VMEM((model, 384), F32)] if rows > 1 else []),
    )
    return pl.pallas_call(
        functools.partial(back_kernel, block=block, part=part),
        grid_spec=spec,
        out_shape=[
            jax.ShapeDtypeStruct((n, 768), BF),
            jax.ShapeDtypeStruct((rows, 2, 1, 384), F32),
        ]
        + [jax.ShapeDtypeStruct((4, 4, model // 16, 384), BF)] * grads,
        input_output_aliases={9: 0, 10: 1} if into else {},
        cost_estimate=cost(rows * 40 * grads * length * length * 128, 24 * n * 128, rows * 4 * length * length),
        compiler_params=params(),
        name="attend_back",
    )(lengths, qa, qkv, qkv, attn, dattn, *tabs, xt, *into)


def norm_forward(u):
    center = u - jnp.mean(u, -1, keepdims=True)
    inverse = lax.rsqrt(jnp.mean(center * center, -1, keepdims=True) + NORM_EPS)
    return center * inverse, inverse


def norm_backward(incoming, normed, inverse, gain):
    scaled = incoming * gain
    mean = jnp.mean(scaled, -1, keepdims=True)
    return inverse * (scaled - mean - normed * jnp.mean(scaled * normed, -1, keepdims=True))


def adder(ref):
    def add(row, value, off=0):
        ref[row : row + 1, off : off + value.shape[1]] += jnp.sum(value, 0, keepdims=True)

    return add


def turn_halves(value, place, ref, cols):
    _, j, c = place
    turned = value.T
    r = turned.shape[0] // 8
    for cb in range(2):
        for jb in range(4):
            start = pl.multiple_of(((c ^ cb) * 4 + exchanged(j ^ jb, c)) * r, 16)
            ref[pl.ds(start, r), cols] = turned[(cb * 4 + jb) * r : (cb * 4 + jb + 1) * r].astype(BF)


def ffn_kernel(*refs, place, length, chunk, attn, side, shrink, blocks):
    live_ref, x_ref, cot_ref, v_ref = refs[:4]
    at_refs = refs[4 : 4 + attn]
    side_refs = refs[4 + attn : 4 + attn + side]
    shrink_refs = refs[4 + attn + side : 4 + attn + side + shrink]
    outs = refs[4 + attn + side + shrink :]
    out_ref, yt_ref, att_ref, dpre_ref, dr1_ref, da_ref, dat_ref, dvec_ref, theirs_ref, mine_ref = outs[:10]
    wo_ref, w1_ref, w2_ref, act_ref, dzt_ref, slope_ref, flat_o, flat_1, flat_2, sem_o, sem_1, sem_2 = outs[10:]
    step = pl.program_id(0)
    block, model = x_ref.shape
    ff = w1_ref.shape[1]
    per = length // block
    live = live_ref[:, :1]
    place = place()
    vec = lambda i: v_ref[i : i + 1, :]

    @pl.when(step == 0)
    def _():
        first = out_copies(place, side_refs, wo_ref, flat_o)
        second = expand_copies(place, side_refs, w1_ref, flat_1)
        third = shrink_copies(place, shrink_refs, w2_ref, flat_2)
        begin(first, sem_o)
        begin(second, sem_1)
        begin(third, sem_2)
        dvec_ref[...] = jnp.zeros_like(dvec_ref)
        finish(first, sem_o)
        own_part(place, first, wo_ref, flat_o)
        finish(second, sem_1)
        own_part(place, second, w1_ref, flat_1)
        finish(third, sem_2)
        own_part(place, third, w2_ref, flat_2)

    @pl.when(step < blocks)
    def _():
        here = pl.ds(pl.multiple_of(step * block, block), block)
        add = adder(dvec_ref)
        at = jnp.concatenate([ref[...] for ref in at_refs], -1)
        turn_columns(at.astype(F32), place, att_ref)
        r1 = x_ref[...].astype(F32) + (dot_nn(at, wo_ref[...]) + vec(7))
        n1, i1 = norm_forward(r1)
        y1 = n1 * vec(0) + vec(2)
        y1b = y1.astype(BF)
        turn_columns(y1, place, yt_ref)
        z = jnp.zeros((block, model), F32)
        for lo in range(0, ff, chunk):
            cols = slice(lo, lo + chunk)
            bias = v_ref[9 + lo // model : 10 + lo // model, lo % model : lo % model + chunk]
            pre = dot_nn(y1b, w1_ref[:, cols]) + bias
            phi = 0.5 * (1.0 + lax.erf(pre * ROOT_HALF))
            act = (pre * phi).astype(BF)
            act_ref[here, cols] = act
            slope_ref[:, cols] = phi + pre * (jnp.exp(-0.5 * pre * pre) * INV_ROOT_TAU)
            z = z + dot_nn(act, w2_ref[cols, :])
        r2 = y1 + (z + vec(8))
        n2, i2 = norm_forward(r2)
        out_ref[...] = (n2 * vec(1) + vec(3)).astype(BF)
        pos = lax.broadcasted_iota(jnp.int32, (block, model), 0) + (step % per) * block
        e = jnp.where(pos < live, cot_ref[...].astype(F32), 0.0)
        dy = norm_backward(e, n2, i2, vec(1))
        turn_halves(dy, place, dzt_ref, here)
        dz = dy.astype(BF)
        add(1, e * n2)
        add(3, e)
        add(8, dz.astype(F32))
        for lo in range(0, ff, chunk):
            cols = slice(lo, lo + chunk)
            dpre = (dot_nt(dz, w2_ref[cols, :]) * slope_ref[:, cols]).astype(BF)
            dpre_ref[:, cols] = dpre
            add(9 + lo // model, dpre.astype(F32), lo % model)
            dy = dy + dot_nt(dpre, w1_ref[:, cols])
        add(0, dy * n1)
        add(2, dy)
        dr1 = norm_backward(dy, n1, i1, vec(0))
        dr1_ref[...] = dr1
        da = dr1.astype(BF)
        da_ref[...] = da
        add(7, da.astype(F32))
        dat_ref[...] = dot_nt(da, wo_ref[...]).astype(BF)

    @pl.when(step >= blocks)
    def _():
        kf = step - blocks
        width = ff // 4
        r = model // 8
        cols = pl.ds(pl.multiple_of((place[0] ^ kf) * width, 128), width)
        acc = dot_nn(dzt_ref[...], act_ref[:, cols])
        for slot in range(4):
            mine_ref[slot] = acc[slot * r : (slot + 1) * r].astype(BF)
            theirs_ref[TURNED[slot]] = acc[(4 + slot) * r : (5 + slot) * r].astype(BF)


def ffn_call(place, lengths, x, attn, cot, side, shrink, vec, length, block=256, chunk=768):
    n, model = x.shape
    ff = 4 * model
    blocks = n // block
    at = lambda i: jnp.minimum(i, blocks - 1)
    tok = pl.BlockSpec((block, model), lambda i, *_: (at(i), 0))
    wide = pl.BlockSpec((block, ff), lambda i, *_: (at(i), 0))
    small = pl.BlockSpec((13, model), lambda i, *_: (0, 0))
    turned = pl.BlockSpec((model, block), lambda i, *_: (0, at(i)))
    grad = pl.BlockSpec((4, None, model // 8, ff // 4), lambda i, *_: (0, jnp.maximum(i - blocks, 0), 0, 0))
    spec = pltpu.PrefetchScalarGridSpec(
        num_scalar_prefetch=0,
        grid=(blocks + 4,),
        in_specs=[pl.BlockSpec((None, 1, 128), lambda i: (at(i) // (length // block), 0, 0)), tok, tok, small]
        + [pl.BlockSpec((block, a.shape[1]), lambda i, *_: (at(i), 0)) for a in attn]
        + [ANY] * (len(side) + len(shrink)),
        out_specs=[tok, turned, turned, wide, tok, tok, tok, small, grad, grad],
        scratch_shapes=[
            pltpu.VMEM((model, model), BF),
            pltpu.VMEM((model, ff), BF),
            pltpu.VMEM((ff, model), BF),
            pltpu.VMEM((n, ff), BF),
            pltpu.VMEM((model, n), BF),
            pltpu.VMEM((block, ff), F32),
            pltpu.VMEM((model // 4, model), F32),
            pltpu.VMEM((model // 4, ff), F32),
            pltpu.VMEM((ff // 4, model), F32),
        ]
        + [pltpu.SemaphoreType.DMA((MOST,))] * 3,
    )
    s = lambda w, t: jax.ShapeDtypeStruct((n, w), t)
    flip = jax.ShapeDtypeStruct((model, n), BF)
    parts = jax.ShapeDtypeStruct((4, 4, model // 8, ff // 4), BF)
    return pl.pallas_call(
        functools.partial(
            ffn_kernel, place=place, length=length, chunk=chunk, attn=len(attn), side=len(side), shrink=len(shrink), blocks=blocks
        ),
        grid_spec=spec,
        out_shape=[
            s(model, BF),
            flip,
            flip,
            s(ff, BF),
            s(model, F32),
            s(model, BF),
            s(model, BF),
            jax.ShapeDtypeStruct((13, model), F32),
            parts,
            parts,
        ],
        cost_estimate=cost(
            2 * n * (3 * model * model + 10 * model * ff), n * (model * 20 + ff * 4) + model * ff * 4, n * ff * 2
        ),
        compiler_params=params(),
        name="ffn",
    )(lengths, x, cot, vec, *attn, *side, *shrink)


def side_grad_kernel(yt_ref, att_any, dpre_ref, da_ref, theirs_ref, mine_ref, att_ref, sem, *, steps):
    step = pl.program_id(0)
    late = pltpu.make_async_copy(att_any, att_ref, sem)
    pl.when(step == 0)(late.start)
    pl.when(step == steps - 1)(late.wait)
    r = yt_ref.shape[0] // 16

    def put(acc, ref, order):
        for slot in range(4):
            for kf in range(4):
                rows = slice((slot * 4 + kf) * r, (slot * 4 + kf + 1) * r)
                ref[order[slot], kf, :, : acc.shape[1]] = acc[rows].astype(BF)

    for first, ref, order in ((0, theirs_ref, TURNED), (steps, mine_ref, (0, 1, 2, 3))):

        @pl.when((step >= first) & (step < first + steps - 1))
        def _(ref=ref, order=order):
            put(dot_nn(yt_ref[...], dpre_ref[...]), ref, order)

        @pl.when(step == first + steps - 1)
        def _(ref=ref, order=order):
            put(dot_nn(att_ref[...], da_ref[...]), ref, order)


def side_grad_call(place, yt, att, dpre, da, block=768):
    model, n = yt.shape
    half = dpre.shape[1] // 2
    steps = half // block + 1
    which = lambda i: jnp.where(i < steps, 1 - place()[2], place()[2])
    turned = pl.BlockSpec((model, n), lambda i: (0, 0))
    width = half + model // 2
    out = lambda first: pl.BlockSpec(
        (4, 4, model // 16, block), lambda i: (0, 0, 0, jnp.clip(i - first, 0, steps - 1))
    )
    spec = pltpu.PrefetchScalarGridSpec(
        num_scalar_prefetch=0,
        grid=(2 * steps,),
        in_specs=[
            turned,
            ANY,
            pl.BlockSpec(
                (n, block), lambda i: (0, which(i) * (steps - 1) + jnp.minimum(i % steps, steps - 2))
            ),
            pl.BlockSpec((n, model // 2), lambda i: (0, which(i))),
        ],
        out_specs=[out(0), out(steps)],
        scratch_shapes=[pltpu.VMEM((model, n), BF), pltpu.SemaphoreType.DMA(())],
    )
    return pl.pallas_call(
        functools.partial(side_grad_kernel, steps=steps),
        grid_spec=spec,
        out_shape=[jax.ShapeDtypeStruct((4, 4, model // 16, width), BF)] * 2,
        cost_estimate=cost(4 * n * model * width, 4 * (n * model + n * width + model * width)),
        compiler_params=params(),
        name="side_grad",
    )(yt, att, dpre, da)


def token_kernel(*refs, place, pieces, parts):
    dr1_ref = refs[0]
    g_refs = refs[1 : 1 + parts]
    w_refs = refs[1 + parts : 1 + parts + pieces]
    o_ref, w_ref, flat_ref, sems = refs[1 + parts + pieces :]
    model = w_ref.shape[0]

    @pl.when(pl.program_id(0) == 0)
    def _():
        copies = in_copies(place(), w_refs, w_ref, flat_ref)
        begin(copies, sems)
        finish(copies, sems)
        own_part(place(), copies, w_ref, flat_ref)

    total = dr1_ref[...]
    for t in range(3):
        tiles = [ref[:, lo + t * 128 : lo + (t + 1) * 128] for ref in g_refs for lo in range(0, ref.shape[1], 384)]
        total = total + dot_nt(jnp.concatenate(tiles, -1), w_ref[:, t * model : (t + 1) * model])
    o_ref[...] = total.astype(BF)


def token_call(place, dr1, grads, weight, block=256):
    n, model = dr1.shape
    tok = lambda w: pl.BlockSpec((block, w), lambda i: (i, 0))
    spec = pltpu.PrefetchScalarGridSpec(
        num_scalar_prefetch=0,
        grid=(n // block,),
        in_specs=[tok(model)] + [tok(g.shape[1]) for g in grads] + [ANY] * len(weight),
        out_specs=tok(model),
        scratch_shapes=[
            pltpu.VMEM((model, 3 * model), BF),
            pltpu.VMEM((model // 4, 3 * model), F32),
            pltpu.SemaphoreType.DMA((MOST,)),
        ],
    )
    return pl.pallas_call(
        functools.partial(token_kernel, place=place, pieces=len(weight), parts=len(grads)),
        grid_spec=spec,
        out_shape=jax.ShapeDtypeStruct((n, model), BF),
        cost_estimate=cost(6 * n * model * model, n * model * 12 + 6 * model * model),
        compiler_params=params(),
        name="token_gradient",
    )(dr1, *grads, *weight)


def sums_kernel(*refs, place, jobs):
    f, step = place()[0], pl.program_id(0)
    at = 0
    outs = refs[sum(mine + recv + got for _, mine, recv, got in jobs) :]
    for kind, mine, recv, got in jobs:
        mines = refs[at : at + mine]
        recvs = refs[at + mine : at + mine + recv]
        gots = refs[at + mine + recv : at + mine + recv + got]
        at += mine + recv + got
        lo = 0
        for i, ref in enumerate(mines):
            cols = slice(lo, lo + ref.shape[-1])
            lo += ref.shape[-1]
            total = ref[...].astype(F32)
            if i < recv:
                total = total + recvs[i][...].astype(F32)
            for other in gots:
                total = total + other[:, :, cols].astype(F32)
            total = total.astype(BF)
            if kind == "own":
                for k in range(2):
                    outs[0][k ^ (f & 1), :, cols] = total[k]
            elif kind == "split":
                for k in range(4):

                    @pl.when(step == k // 2)
                    def _(k=k, total=total, cols=cols, out=outs[k]):
                        out[:, cols] = total[k % 2]

            else:
                outs[0][..., cols] = total
        outs = outs[4 if kind == "split" else 1 :]


def sums_call(place, *jobs):
    arrays, specs, shapes, outs, heads = [], [], [], [], []
    for kind, mine, recv, got in jobs:
        r, width = mine[0].shape[2], sum(m.shape[3] for m in mine)
        slot = {"first": 1, "second": 1, "own": 0, "split": 0}[kind]
        lead = 2 if kind == "first" else None
        block = lambda a, slot=slot, lead=lead: pl.BlockSpec(
            (lead, 2) + a.shape[2:], lambda k, slot=slot: (slot, k, 0, 0)
        )
        half = lambda a: pl.BlockSpec((2,) + a.shape[1:], lambda k: (k, 0, 0))
        arrays += [*mine, *recv, *got]
        specs += [block(a) if a.ndim == 4 else half(a) for a in (*mine, *recv, *got)]
        heads.append((kind, len(mine), len(recv), len(got)))
        if kind == "first":
            shapes.append(jax.ShapeDtypeStruct((2, 4, r, width), BF))
            outs.append(pl.BlockSpec((2, 2, r, width), lambda k: (0, k, 0, 0)))
        elif kind == "split":
            shapes += [jax.ShapeDtypeStruct((r, width), BF)] * 4
            outs += [pl.BlockSpec((r, width), lambda k: (0, 0))] * 4
        else:
            shapes.append(jax.ShapeDtypeStruct((4, r, width), BF))
            turn = kind == "own"
            outs.append(
                pl.BlockSpec((2, r, width), lambda k, t=turn: (k ^ (place()[0] >> 1) if t else k, 0, 0))
            )
    spec = pltpu.PrefetchScalarGridSpec(num_scalar_prefetch=0, grid=(2,), in_specs=specs, out_specs=outs)
    moved = sum(a.size for a in arrays)
    return pl.pallas_call(
        functools.partial(sums_kernel, place=place, jobs=tuple(heads)),
        grid_spec=spec,
        out_shape=shapes,
        cost_estimate=cost(moved, 2 * moved),
        compiler_params=params(),
        name="sums",
    )(*arrays)


def plus(*parts):
    total = parts[0].astype(F32)
    for part in parts[1:]:
        total = total + part.astype(F32)
    return total.astype(BF)


def send_z(own, one, two, three):
    return own, cross(one, 1), cross(two, 2), cross(three, 3)


def over_chips(total):
    return total, swap(total, 2), swap(total, 4), swap(total, 6)


def both_cores(chips):
    return (*chips, *(swap_core(part) for part in chips))


def vector_parts_kernel(rest_ref, *refs, place):
    sums, mine_ref = refs[:-1], refs[-1]
    f, j, c = place()
    rest = rest_ref[...]
    heads = []
    for t in range(3):
        cols = slice(t * 128, (t + 1) * 128)
        tiles = [jnp.sum(ref[:, pair, :, cols], 0) for ref in sums for pair in range(2)]
        heads.append(jnp.concatenate(tiles, -1))
    value = jnp.concatenate([rest[:4], *heads, rest[7:]], 0)
    mine_ref[...] = jnp.zeros_like(mine_ref)
    rows, model = value.shape
    width = model // 16
    for fb in range(4):
        for jb in range(4):
            lo = (fb * 4 + jb) * width
            part = value[:, lo : lo + width].astype(BF)
            mine_ref[exchanged(j ^ jb, c), f ^ fb, :rows, :width] = part


def vector_parts(place, rest, sums, r):
    whole = lambda a: pl.BlockSpec(a.shape, lambda *_, k=a.ndim: (0,) * k)
    spec = pltpu.PrefetchScalarGridSpec(
        num_scalar_prefetch=0,
        grid=(1,),
        in_specs=[whole(a) for a in (rest, *sums)],
        out_specs=pl.BlockSpec((4, 4, r, 128), lambda *_: (0, 0, 0, 0)),
    )
    return pl.pallas_call(
        functools.partial(vector_parts_kernel, place=place),
        grid_spec=spec,
        out_shape=jax.ShapeDtypeStruct((4, 4, r, 128), BF),
        compiler_params=params(),
        name="vector_parts",
    )(rest, *sums)


def adam_update(master, moment, square, gradient, rate, decay):
    momentum = BETA_ONE * moment + (1.0 - BETA_ONE) * gradient
    squares = BETA_TWO * square + (1.0 - BETA_TWO) * gradient * gradient
    corrected = momentum / (1.0 - BETA_ONE**STEP)
    spread = jnp.sqrt(squares / (1.0 - BETA_TWO**STEP))
    return (master - rate * (corrected / (spread + ADAM_EPS) + decay * master), momentum, squares)


def adam_block(state, outs, g, rate):
    w, m, s = (ref[...] for ref in state)
    for ref, value in zip(outs, adam_update(w, m, s, g, rate, WEIGHT_DECAY)):
        ref[...] = value


def adam_side_kernel(*refs, weights, moves, rates):
    state, grad, outs = refs[: 3 * weights], refs[3 * weights], refs[3 * weights + 1 : 6 * weights + 1]
    flats = refs[6 * weights + 1 :]
    step = pl.program_id(0)
    rows = state[0].shape[0]

    @pl.when(step == 0)
    def _():
        r = grad.shape[1]
        for weight, src, width in moves:
            for d in range(8):
                to = slice((d % 2) * width, (d % 2 + 1) * width)
                flats[weight][d // 2 * r : (d // 2 + 1) * r, to] = grad[d, :, src : src + width]

    here = pl.ds(pl.multiple_of(step * rows, rows), rows)
    for i in range(weights):
        cut = slice(3 * i, 3 * i + 3)
        adam_block(state[cut], outs[cut], flats[i][here, :].astype(F32), rates[i])


def adam_side_call(states, grad, moves, rates, steps=2):
    rows = states[0][0].shape[0] // steps
    block = lambda a: pl.BlockSpec((rows, a.shape[1]), lambda i: (i, 0))
    flat = [a for state in states for a in state]
    size = sum(a.size for a in flat)
    return pl.pallas_call(
        functools.partial(adam_side_kernel, weights=len(states), moves=tuple(moves), rates=tuple(rates)),
        grid=(steps,),
        in_specs=[block(a) for a in flat] + [pl.BlockSpec(grad.shape, lambda i: (0, 0, 0))],
        out_specs=[block(a) for a in flat],
        scratch_shapes=[pltpu.VMEM(state[0].shape, BF) for state in states],
        out_shape=[jax.ShapeDtypeStruct(a.shape, F32) for a in flat],
        cost_estimate=cost(size * 4, size * 9),
        compiler_params=params(),
        name="adam_side",
    )(*flat, grad)


def adam_in_kernel(*refs, place, moves, rate, first):
    state, vector, grads, outs, vector_outs = refs[:3], refs[3:6], refs[6:14], refs[14:17], refs[17:20]
    flat, vector_flat = refs[20:]
    _, j, c = place()
    step = pl.program_id(0)
    rows = state[0].shape[0]

    @pl.when(step == 0)
    def _():
        for i, ref in enumerate(grads):
            half = c if i < 4 else 1 - c
            r = ref.shape[0]
            here = pl.ds(pl.multiple_of((j ^ (i % 4)) * r, 16), r)
            for src, to, stride in moves:
                cols = pl.ds(pl.multiple_of(to + half * stride, 128), 128)
                flat[here, cols] = ref[:, src : src + 128]
        count, width = vector_flat.shape
        width = width // 4
        both = lambda k: grads[k][:, first : first + 128].astype(F32) + grads[k + 4][:, first : first + 128].astype(F32)
        parts = [both(k) for k in range(4)]
        for at in range(4):
            k = j ^ at
            part = jnp.where(k == 0, parts[0], jnp.where(k == 1, parts[1], jnp.where(k == 2, parts[2], parts[3])))
            vector_flat[:, at * width : (at + 1) * width] = part[:count, :width]
        w, m, s = (ref[...] for ref in vector)
        for ref, value in zip(vector_outs, adam_update(w, m, s, vector_flat[...], 0.5, 0.0)):
            ref[...] = value

    here = pl.ds(pl.multiple_of(step * rows, rows), rows)
    adam_block(state, outs, flat[here, :].astype(F32), rate)


def adam_in_call(place, state, vector, grads, moves, rate, first, steps=2):
    rows = state[0].shape[0] // steps
    block = pl.BlockSpec((rows, state[0].shape[1]), lambda i: (i, 0))
    small = pl.BlockSpec(vector[0].shape, lambda i: (0, 0))
    return pl.pallas_call(
        functools.partial(adam_in_kernel, place=place, moves=tuple(moves), rate=rate, first=first),
        grid=(steps,),
        in_specs=[block] * 3 + [small] * 3 + [pl.BlockSpec(g.shape, lambda i: (0, 0)) for g in grads],
        out_specs=[block] * 3 + [small] * 3,
        scratch_shapes=[pltpu.VMEM(state[0].shape, BF), pltpu.VMEM(vector[0].shape, F32)],
        out_shape=[jax.ShapeDtypeStruct(state[0].shape, F32)] * 3 + [jax.ShapeDtypeStruct(vector[0].shape, F32)] * 3,
        cost_estimate=cost(state[0].size * 12, state[0].size * 28),
        compiler_params=params(),
        name="adam_in",
    )(*state, *vector, *grads)


def adam_turned_kernel(*refs, rate):
    state, grad, outs, (flat_ref, g_ref) = refs[:3], refs[3], refs[4:7], refs[7:]
    step = pl.program_id(0)
    rows = state[0].shape[0]

    @pl.when(step == 0)
    def _():
        r = grad.shape[1]
        for d in range(8):
            at = (d % 2) * 4 + d // 2
            flat_ref[at * r : (at + 1) * r, :] = grad[d].astype(F32)
        g_ref[...] = flat_ref[...].T

    adam_block(state, outs, g_ref[pl.ds(pl.multiple_of(step * rows, rows), rows), :], rate)


def adam_turned_call(state, grad, rate, steps=2):
    total, cols = state[0].shape
    block = pl.BlockSpec((total // steps, cols), lambda i: (i, 0))
    return pl.pallas_call(
        functools.partial(adam_turned_kernel, rate=rate),
        grid=(steps,),
        in_specs=[block] * 3 + [pl.BlockSpec(grad.shape, lambda i: (0, 0, 0))],
        out_specs=[block] * 3,
        scratch_shapes=[pltpu.VMEM((cols, total), F32), pltpu.VMEM((total, cols), F32)],
        out_shape=[jax.ShapeDtypeStruct(state[0].shape, F32)] * 3,
        cost_estimate=cost(total * cols * 12, total * cols * 28),
        compiler_params=params(),
        name="adam_turned",
    )(*state, grad)


def vector_rows(rest, sums):
    heads = jnp.concatenate([jnp.sum(s, 0) for s in sums], 0).reshape(-1, 3, 128)
    heads = heads.transpose(1, 0, 2).reshape(3, -1)
    return jnp.concatenate([rest[:4], heads, rest[7:]], 0)


def local(
    tokens,
    cotangent,
    lengths,
    inward_weight,
    inward_moment,
    inward_square,
    outward_weight,
    outward_moment,
    outward_square,
    expand_weight,
    expand_moment,
    expand_square,
    shrink_weight,
    shrink_moment,
    shrink_square,
    vectors,
    vector_moment,
    vector_square,
    sliced,
):
    _, length, model = tokens.shape
    x, cot = tokens.reshape(-1, model), cotangent.reshape(-1, model)
    tabs = tables(length)
    ff = 4 * model
    pairs = model // 128
    inward = (inward_weight, inward_moment, inward_square)
    outward = (outward_weight, outward_moment, outward_square)
    expand = (expand_weight, expand_moment, expand_square)
    shrink = (shrink_weight, shrink_moment, shrink_square)
    vector = (vectors, vector_moment, vector_square)
    rate_d, rate_o, rate_f = 1.0 / math.sqrt(model), 1.0 / math.sqrt(OUT_FAN), 1.0 / math.sqrt(ff)
    f, d = lax.axis_index("fsdp"), lax.axis_index("dp")
    j, c = d // 2, d % 2
    place = place_finder(sliced)
    lengths = jnp.broadcast_to(lengths[:, None, None], (lengths.shape[0], 1, 128))
    spans = [(0, 2), (2, 2), (4, 2)]

    if not sliced:
        low = [w.astype(BF) for w in (inward_weight, outward_weight, expand_weight, shrink_weight, vectors)]
        whole = [lax.all_gather(w, "fsdp", axis=0, tiled=True) for w in low[:4]]
        in_pieces, side_pieces, shrink_pieces = (whole[0],), (whole[1], whole[2]), (whole[3],)
        vec = lax.all_gather(low[4], "fsdp", axis=1, tiled=True).astype(F32)
        qkv, xt = qkv_call(place, x, in_pieces, vec[4:7].reshape(1, -1), tabs, length)
        seen = [attend_call(lengths, qkv, length, *span) for span in spans]
        out, yt, att, dpre, dr1, da, dattn, vec_rest, far, near = ffn_call(
            place, lengths, x, [a for a, _ in seen], cot, side_pieces, shrink_pieces, vec, length
        )
        order = jnp.array(TURNED)
        shrink_grad = jnp.concatenate([near, far[order]]).transpose(1, 3, 0, 2).reshape(ff, model)
        far, near = side_grad_call(place, yt, att, dpre, da)
        both = jnp.stack([near, far[order]]).transpose(2, 1, 3, 0, 4).reshape(model, 2, -1)
        expand_grad = both[:, :, : ff // 2].reshape(model, ff)
        outward_grad = both[:, :, ff // 2 :].reshape(model, model)
        backs = [back_call(place, lengths, seen[i], qkv, dattn, xt, tabs, length, i) for i in range(len(spans))]
        token_gradient = token_call(place, dr1, [b[0] for b in backs], in_pieces)
        parts = jnp.stack([part for _, _, far, near in backs for part in (near, far[order])])
        parts = parts.transpose(2, 1, 3, 0, 4).reshape(model, pairs, 3, 128)
        inward_grad = parts.transpose(0, 2, 1, 3).reshape(model, 3 * model)

        def reduced(g, axis=0):
            return lax.psum(lax.psum_scatter(g, "fsdp", scatter_dimension=axis, tiled=True).astype(F32), "dp")

        inward_new = adam_update(*inward, reduced(inward_grad), rate_d, WEIGHT_DECAY)
        outward_new = adam_update(*outward, reduced(outward_grad), rate_o, WEIGHT_DECAY)
        expand_new = adam_update(*expand, reduced(expand_grad), rate_d, WEIGHT_DECAY)
        shrink_new = adam_update(*shrink, reduced(shrink_grad), rate_f, WEIGHT_DECAY)
        vec_sum = reduced(vector_rows(vec_rest, [b[1] for b in backs]), 1)
        vector_new = adam_update(*vector, vec_sum, 0.5, 0.0)
    else:
        shard = model // 4
        r = shard // 4

        def columns(w):
            half = w.shape[1] // 2
            return lax.dynamic_slice(w, (j * r, c * half), (r, half))

        def rows(w):
            r = w.shape[0] // 8
            return lax.dynamic_slice(w, ((c * 4 + j) * r, 0), (r, w.shape[1]))

        low_vec = vectors.astype(BF)
        third = r + r // 3
        beside = jnp.pad(low_vec.reshape(-1, third), ((0, r - 3 * vectors.shape[0]), (0, 128 - third)))
        part_in = jnp.concatenate([columns(inward_weight).astype(BF), beside], -1)
        part_side = jnp.concatenate([columns(outward_weight), columns(expand_weight)], -1).astype(BF)
        part_shrink = rows(shrink_weight).astype(BF)
        z_in, lengths = after((jnp.stack(over_z(part_in)), lengths), part_side, part_shrink)
        chips_in, z_side = after((over_chips(z_in), over_z(after(part_side, z_in))))
        in_pieces = (inward_weight, *both_cores(chips_in))
        by = z_in[:, : 3 * vectors.shape[0], part_in.shape[1] - 128 : part_in.shape[1] - 128 + third]
        by = (low_vec, *by.reshape(3, vectors.shape[0], shard))
        ordered = []
        for at in range(4):
            k = f ^ at
            ordered.append(jnp.where(k == 0, by[0], jnp.where(k == 1, by[1], jnp.where(k == 2, by[2], by[3]))))
        vec = jnp.concatenate(ordered, 1).astype(F32)
        z_side = jnp.stack(z_side)
        first_side, second_side = swap_first(z_side), swap_second(z_side)
        qkv, xt = qkv_call(place, x, after(in_pieces, z_side, vec), vec[4:7].reshape(1, -1), tabs, length)
        first_side, second_side = after((first_side, second_side), qkv)
        third_side = swap_second(first_side)
        z_shrink = over_z(after(part_shrink, first_side))
        far_z_side = swap_core(after(z_side, qkv))
        seen = [attend_call(lengths, after(qkv, first_side), length, *spans[0])]
        third_side, far_z_side, z_shrink = after((third_side, far_z_side, z_shrink), seen[0])
        z_shrink = jnp.stack(z_shrink)
        first_shrink, second_shrink = swap_first(z_shrink), swap_second(z_shrink)
        far_side = tuple(swap_core(part) for part in after((second_side, first_side, third_side), z_shrink))
        seen.append(attend_call(lengths, after(qkv, third_side, z_shrink), length, *spans[1]))
        first_shrink, second_shrink, far_side = after((first_shrink, second_shrink, far_side), seen[1])
        third_shrink = swap_second(first_shrink)
        shrink_near = (z_shrink, second_shrink, first_shrink)
        shrink_far = tuple(swap_core(part) for part in shrink_near)
        side_pieces = (outward_weight, expand_weight, z_side, second_side, first_side, third_side, far_z_side, *far_side)
        seen.append(attend_call(lengths, after(qkv, first_shrink), length, *spans[2]))
        third_shrink, shrink_far = after((third_shrink, shrink_far), seen[2])
        shrink_pieces = (shrink_weight, *shrink_near, third_shrink, *shrink_far, swap_core(third_shrink))

        out, yt, att, dpre, dr1, da, dattn, vec_rest, theirs_s, mine_s = ffn_call(
            place, lengths, x, [a for a, _ in seen], cot, side_pieces, shrink_pieces, vec, length
        )

        def back(span, wait, *part):
            return back_call(place, lengths, seen[span], qkv, after(dattn, wait), xt, tabs, length, span, *part)

        recv_s = swap_core(theirs_s)
        to_s = sums_call(place, ("first", [mine_s], [recv_s], []))[0]
        got_s = swap_first(to_s)
        theirs_d, mine_d = side_grad_call(place, yt, att, after(dpre, to_s), da)
        got_s = after(got_s, theirs_d)
        on_s = sums_call(place, ("second", [mine_s], [recv_s], [got_s]))[0]
        last_s = swap_second(on_s)
        recv_d = swap_core(after(theirs_d, on_s))
        g0, sum0, theirs_0, mine_0 = back(0, on_s)
        last_s, recv_d = after((last_s, recv_d), g0)
        to_d, z_s = sums_call(
            place, ("first", [mine_d], [recv_d], []), ("own", [mine_s], [recv_s], [got_s, last_s])
        )
        got_d = swap_first(to_d)
        part_s = lax.psum_scatter(z_s, "fsdp", scatter_dimension=0)
        recv_0 = swap_core(after(theirs_0, to_d))
        g1, sum1, theirs_1, mine_1 = back(1, to_d)
        got_d, recv_0 = after((got_d, recv_0), g1)
        on_d = sums_call(place, ("second", [mine_d], [recv_d], [got_d]))[0]
        last_d = swap_second(on_d)
        recv_1 = swap_core(after(theirs_1, on_d))
        sum_s = lax.all_gather(after(part_s, on_d), "dp")
        g2, sum2, theirs_2, mine_2 = back(2, on_d)
        last_d, recv_1, theirs_2 = after((last_d, recv_1, theirs_2), g2)
        recv_2 = swap_core(theirs_2)
        z_d = sums_call(place, ("own", [mine_d], [recv_d], [got_d, last_d]))[0]
        part_d = lax.psum_scatter(z_d, "fsdp", scatter_dimension=0)
        mine_v = vector_parts(place, after(vec_rest, z_d), [sum0, sum1, sum2], r)
        mine_e = [mine_0, mine_1, mine_2, mine_v]
        recv_e = [recv_0, recv_1, after(recv_2, mine_v)]
        to_e = sums_call(place, ("first", mine_e, recv_e, []))[0]
        got_e = swap_first(to_e)
        token_gradient = token_call(place, after(dr1, to_e), [g0, g1, g2], in_pieces)
        got_e = after(got_e, token_gradient)
        on_e = sums_call(place, ("second", mine_e, recv_e, [got_e]))[0]
        last_e = swap_second(on_e)
        shrink_new = adam_turned_call((after(shrink[0], on_e), *shrink[1:]), sum_s, rate_f)
        last_e, part_d = after((last_e, part_d), shrink_new[0])
        sum_d = lax.all_gather(part_d, "dp")
        z_e = send_z(*sums_call(place, ("split", mine_e, recv_e, [got_e, last_e])))
        moves = [(0, ff // 2, model // 2), (1, 0, ff // 2)]
        sum_e = both_cores(over_chips(plus(*z_e)))
        moves_e = []
        for span in range(3):
            for t in range(3):
                moves_e.append((span * 384 + t * 128, t * model + span * 256, 128))
        both_new = adam_in_call(place, inward, vector, sum_e, moves_e, rate_d, 3 * model // 2)
        inward_new, vector_new = both_new[:3], both_new[3:]
        side_states = [(after(outward[0], inward_new[0]), *outward[1:]), expand]
        side_new = adam_side_call(side_states, sum_d, moves, [rate_o, rate_d])
        outward_new, expand_new = side_new[:3], side_new[3:]
    return (
        out.reshape(tokens.shape),
        token_gradient.reshape(tokens.shape),
        *inward_new,
        *outward_new,
        *expand_new,
        *shrink_new,
        *vector_new,
    )


def solution(mesh):
    both = P(("dp", "fsdp"), None, None)
    in_specs = (both, both, P(("dp", "fsdp"))) + (P("fsdp", None),) * 12 + (P(None, "fsdp"),) * 3
    out_specs = (both, both) + (P("fsdp", None),) * 12 + (P(None, "fsdp"),) * 3
    sliced = mesh.shape["dp"] == 8 and mesh.shape["fsdp"] == 4
    step = functools.partial(local, sliced=sliced)
    return jax.shard_map(step, mesh=mesh, in_specs=in_specs, out_specs=out_specs, check_vma=False)
```

```python
import functools
import math

import jax
import jax.numpy as jnp
import numpy as np
from jax import lax
from jax.experimental import pallas as pl
from jax.experimental.pallas import tpu as pltpu
from jax.sharding import PartitionSpec as P

BF = jnp.bfloat16
F32 = jnp.float32
HEAD = 64
STEP = 10
OUT_FAN = 3
BETA_ONE = 0.5
BETA_TWO = 0.5
ADAM_EPS = 1e-08
WEIGHT_DECAY = 0.01
NORM_EPS = 1e-12
NEG_FILL = -1000000000.0
ROOT_HALF = 0.7071067811865476
INV_ROOT_TAU = 0.3989422804014327
ANY = pl.BlockSpec(memory_space=pl.ANY)


def dot_nn(a, b):
    return lax.dot_general(a, b, (((1,), (0,)), ((), ())), preferred_element_type=F32)


def dot_nt(a, b):
    return lax.dot_general(a, b, (((1,), (1,)), ((), ())), preferred_element_type=F32)


def dot_tn(a, b):
    return lax.dot_general(a, b, (((0,), (0,)), ((), ())), preferred_element_type=F32)


def params():
    return pltpu.CompilerParams(vmem_limit_bytes=64 * 1024 * 1024)


def cost(flops, moved, trans=0):
    return pl.CostEstimate(flops=int(flops), bytes_accessed=int(moved), transcendentals=int(trans))


def swap(x, even, odd=None):
    odd = even if odd is None else odd
    return lax.ppermute(x, "dp", [(i, i ^ (odd if i % 2 else even)) for i in range(8)])


def swap_core(x):
    return swap(x, 1)


def swap_first(x):
    return swap(x, 4, 2)


def swap_second(x):
    return swap(x, 2, 4)


def cross(x, bit):
    return lax.ppermute(x, "fsdp", [(i, i ^ bit) for i in range(4)])


def over_z(part):
    return tuple(cross(part, k) for k in (1, 2, 3))


def after(x, *others):
    return lax.optimization_barrier((x, *others))[0]


TURNED = (0, 2, 1, 3)


def exchanged(k, c):
    return jnp.where(c == 0, k, (k & 1) * 2 + (k >> 1))


def column_copies(place, own, pieces, dst, flat, first=0, staged=True):
    f, j, c = place
    rows, cols = own.shape
    r, h = rows // 4, cols // 2
    out = [(own, flat)]
    for refs, half in ((pieces[:4], c), (pieces[4:], 1 - c)):
        for slot, ref in enumerate(refs):
            kj = exchanged(slot, half) if staged else slot
            for kf in range(1, 4):
                start = pl.multiple_of((f ^ kf) * rows + (j ^ kj) * r, 16)
                at = dst.at[pl.ds(start, r), pl.ds(pl.multiple_of(half * h, 128), h)]
                out.append((ref.at[kf - 1, :, pl.ds(first, h)], at))
    return out


def in_copies(place, refs, dst, flat):
    if len(refs) == 1:
        return [(refs[0], dst)]
    return column_copies(place, refs[0], refs[1:], dst, flat, staged=False)


def out_copies(place, refs, dst, flat):
    if len(refs) == 2:
        return [(refs[0], dst)]
    return column_copies(place, refs[0], refs[2:], dst, flat)


def expand_copies(place, refs, dst, flat):
    if len(refs) == 2:
        return [(refs[1], dst)]
    return column_copies(place, refs[1], refs[2:], dst, flat, refs[0].shape[1] // 2)


def shrink_copies(place, refs, dst, flat):
    if len(refs) == 1:
        return [(refs[0], dst)]
    f, j, c = place
    own, pieces = refs[0], refs[1:]
    rows = own.shape[0]
    r = rows // 8
    out = [(own, flat)]
    for refs, half in ((pieces[:4], c), (pieces[4:], 1 - c)):
        for slot, ref in enumerate(refs):
            kj = exchanged(slot, half)
            for kf in range(1, 4):
                start = pl.multiple_of((f ^ kf) * rows + half * (rows // 2) + (j ^ kj) * r, 16)
                out.append((ref.at[kf - 1], dst.at[pl.ds(start, r), :]))
    return out


def own_part(place, pairs, dst, flat):
    if len(pairs) > 1:
        rows = flat.shape[0]
        dst[pl.ds(pl.multiple_of(place[0] * rows, 16), rows), :] = flat[...].astype(BF)


MOST = 25


def begin(pairs, sems):
    for i, (src, dst) in enumerate(pairs):
        pltpu.make_async_copy(src, dst, sems.at[i]).start()


def finish(pairs, sems):
    for i, (src, dst) in enumerate(pairs):
        pltpu.make_async_copy(src, dst, sems.at[i]).wait()


def place_finder(sliced):
    def place():
        f, d = lax.axis_index("fsdp"), lax.axis_index("dp")
        if not sliced:
            f, d = f * 0, d * 0
        return f, d >> 1, d & 1

    return place


def tables(length):
    lane = np.arange(128)
    angles = np.arange(length)[:, None] * (10000.0 ** (-2.0 * ((lane % HEAD) // 2) / HEAD))[None, :]
    sine = np.where((lane % 2 == 0)[None, :], -np.sin(angles), np.sin(angles))
    return [jnp.asarray(part.astype(np.float32)) for part in (np.cos(angles), sine)]


def rotate(u, cosine, sine):
    even = lax.broadcasted_iota(jnp.int32, u.shape, 1) % 2 == 0
    return u * cosine + jnp.where(even, pltpu.roll(u, 127, 1), pltpu.roll(u, 1, 1)) * sine


def turn_columns(value, place, ref):
    f, j, c = place
    turned = value.T
    r = turned.shape[0] // 16
    for fb in range(4):
        for jb in range(4):
            start = pl.multiple_of((exchanged(j ^ jb, c) * 4 + (f ^ fb)) * r, 16)
            ref[pl.ds(start, r), :] = turned[(fb * 4 + jb) * r : (fb * 4 + jb + 1) * r].astype(BF)


def qkv_kernel(*refs, place, pieces):
    x_ref, b_ref, cos_ref, sin_ref = refs[:4]
    w_refs = refs[4 : 4 + pieces]
    o_ref, xt_ref, w_ref, flat_ref, sems = refs[4 + pieces :]

    @pl.when(pl.program_id(0) == 0)
    def _():
        copies = in_copies(place(), w_refs, w_ref, flat_ref)
        begin(copies, sems)
        finish(copies, sems)
        own_part(place(), copies, w_ref, flat_ref)

    x = x_ref[...]
    turn_columns(x.astype(F32), place(), xt_ref)
    cosine, sine = cos_ref[...], sin_ref[...]
    model, width = w_ref.shape
    for col in range(0, width, 256):
        acc = dot_nn(x, w_ref[:, col : col + 256]) + b_ref[:, col : col + 256]
        for tile in range(2):
            lo = col + tile * 128
            u = acc[:, tile * 128 : (tile + 1) * 128]
            if lo < 2 * model:
                u = rotate(u, cosine, sine)
            if lo < model:
                u = u * (1.0 / math.sqrt(HEAD))
            o_ref[:, lo : lo + 128] = u.astype(BF)


def qkv_call(place, x, weight, bias, tabs, length, block=256):
    n, model = x.shape
    per = length // block
    width = bias.shape[1]
    table = pl.BlockSpec((block, 128), lambda i: (i % per, 0))
    spec = pltpu.PrefetchScalarGridSpec(
        num_scalar_prefetch=0,
        grid=(n // block,),
        in_specs=[
            pl.BlockSpec((block, model), lambda i: (i, 0)),
            pl.BlockSpec((1, width), lambda i: (0, 0)),
            table,
            table,
        ]
        + [ANY] * len(weight),
        out_specs=[
            pl.BlockSpec((block, width), lambda i: (i, 0)),
            pl.BlockSpec((model, block), lambda i: (0, i)),
        ],
        scratch_shapes=[
            pltpu.VMEM((model, width), BF),
            pltpu.VMEM((model // 4, width), F32),
            pltpu.SemaphoreType.DMA((MOST,)),
        ],
    )
    return pl.pallas_call(
        functools.partial(qkv_kernel, place=place, pieces=len(weight)),
        grid_spec=spec,
        out_shape=[jax.ShapeDtypeStruct((n, width), BF), jax.ShapeDtypeStruct((model, n), BF)],
        cost_estimate=cost(2 * n * model * width, 2 * (n * model + model * width + n * width)),
        compiler_params=params(),
        name="qkv",
    )(x, bias, *tabs, *weight)


def attend_kernel(live_ref, q_ref, k_ref, v_ref, o_ref, qa_ref, *, block):
    length = q_ref.shape[0]
    live = live_ref[...]
    lane = lax.broadcasted_iota(jnp.int32, (length, 128), 1)
    pos = lax.broadcasted_iota(jnp.int32, (length, 128), 0)
    k, vt = k_ref[...].astype(F32), v_ref[...].astype(F32).T
    keys, values = [], []
    for h in range(2):
        own = (lane // HEAD) == h
        aux = HEAD * (1 - h)
        mask = jnp.where((lane == aux) & (pos >= live), NEG_FILL, 0.0)
        keys.append(jnp.where(own, k, mask).astype(BF))
        values.append(jnp.concatenate([vt[h * HEAD : (h + 1) * HEAD], jnp.ones((16, length), F32)], 0).astype(BF))
    lane = lax.broadcasted_iota(jnp.int32, (block, 128), 1)
    for i in range(length // block):
        rows = slice(i * block, (i + 1) * block)
        q = q_ref[rows, :].astype(F32)
        mixed, stats = [], []
        for h in range(2):
            own = (lane // HEAD) == h
            aux = HEAD * (1 - h)
            scores = dot_nt(keys[h], jnp.where(own, q, jnp.where(lane == aux, 1.0, 0.0)).astype(BF))
            top = jnp.max(scores, 0, keepdims=True)
            summed = dot_nn(values[h], jnp.exp(scores - top).astype(BF))
            total = summed[HEAD : HEAD + 1]
            mixed.append(summed[:HEAD] / total)
            shift = -(top + jnp.log(total))
            hi = shift.astype(BF).astype(F32)
            mid = (shift - hi).astype(BF).astype(F32)
            one = jnp.ones_like(hi)
            stats.append(jnp.concatenate([hi, mid, shift - hi - mid, one, jnp.zeros((HEAD - 4, block), F32)], 0))
        o_ref[rows, :] = jnp.concatenate(mixed, 0).T.astype(BF)
        extra = jnp.concatenate([stats[1], stats[0]], 0).T
        for h in range(2):
            qa_ref[h, rows, :] = jnp.where((lane // HEAD) == h, q, extra).astype(BF)


def attend_call(lengths, qkv, length, first, count, block=1024):
    n, width = qkv.shape
    rows, pairs = n // length, width // 384
    one = lambda off: pl.BlockSpec((length, 128), lambda b, p: (b, off * pairs + first + p))
    spec = pltpu.PrefetchScalarGridSpec(
        num_scalar_prefetch=0,
        grid=(rows, count),
        in_specs=[pl.BlockSpec((None, 1, 128), lambda b, p: (b, 0, 0)), one(0), one(1), one(2)],
        out_specs=[
            pl.BlockSpec((length, 128), lambda b, p: (b, p)),
            pl.BlockSpec((None, 2, length, 128), lambda b, p: (b, p, 0, 0)),
        ],
    )
    return pl.pallas_call(
        functools.partial(attend_kernel, block=block),
        grid_spec=spec,
        out_shape=[
            jax.ShapeDtypeStruct((n, count * 128), BF),
            jax.ShapeDtypeStruct((rows, 2 * count, length, 128), BF),
        ],
        cost_estimate=cost(rows * count * 32 * length * length * 128, 12 * n * count * 128, rows * count * 2 * length * length),
        compiler_params=params(),
        name="attend",
    )(lengths, qkv, qkv, qkv)


def back_kernel(*refs, block, part):
    live_ref, qa_ref, k_ref, v_ref, o_ref, do_ref, cos_ref, sin_ref, xt_ref = refs[:9]
    rest = refs[11:] if part == 1 else refs[9:]
    g_ref, sum_ref, *rest = rest
    theirs_ref = mine_ref = None
    if part != 1:
        theirs_ref, *rest = rest
    if part != 0:
        mine_ref, *rest = rest
    doa_ref, dqt_ref, *rest = rest
    acc_ref = rest[0] if rest else None
    length = k_ref.shape[0]
    pair, row, rows_last = pl.program_id(0) + (part or 0), pl.program_id(1), pl.num_programs(1) - 1
    live = live_ref[...]
    lane = lax.broadcasted_iota(jnp.int32, (length, 128), 1)
    do = do_ref[...].astype(F32)
    prod = do * o_ref[...].astype(F32)
    for h in range(2):
        own = (lane // HEAD) == h
        aux = HEAD * (1 - h)
        shift = -jnp.sum(jnp.where(own, prod, 0.0), -1, keepdims=True)
        hi = shift.astype(BF).astype(F32)
        extra = jnp.where(lane == aux, hi, jnp.where(lane == aux + 1, shift - hi, 0.0))
        doa_ref[h] = jnp.where(own, do, extra).astype(BF)
    lane = lax.broadcasted_iota(jnp.int32, (block, 128), 1)
    pos = lax.broadcasted_iota(jnp.int32, (block, 128), 0)
    dk_sum = jnp.zeros((1, 128), F32)
    dv_sum = jnp.zeros((1, 128), F32)
    for i in range(length // block):
        rows = slice(i * block, (i + 1) * block)
        k, v = k_ref[rows, :].astype(F32), v_ref[rows, :].astype(F32)
        kt = k.T.astype(BF)
        dks, dvs = [], []
        for h in range(2):
            own = (lane // HEAD) == h
            aux = HEAD * (1 - h)
            mask = jnp.where((lane == aux + 3) & (pos + i * block >= live), NEG_FILL, 0.0)
            ka = jnp.where(own, k, jnp.where((lane >= aux) & (lane < aux + 3), 1.0, mask)).astype(BF)
            va = jnp.where(own, v, jnp.where((lane >= aux) & (lane < aux + 2), 1.0, 0.0)).astype(BF)
            qa, doa = qa_ref[h], doa_ref[h]
            p = jnp.exp(dot_nt(ka, qa))
            ds = (p * dot_nt(va, doa)).astype(BF)
            dvs.append(dot_nn(p.astype(BF), doa))
            dks.append(dot_nn(ds, qa))
            dqt = dot_nn(kt[h * HEAD : (h + 1) * HEAD, :], ds)
            if i == 0:
                dqt_ref[h * HEAD : (h + 1) * HEAD, :] = dqt
            else:
                dqt_ref[h * HEAD : (h + 1) * HEAD, :] += dqt
        dk = jnp.where(lane < HEAD, dks[0], dks[1])
        dk = rotate(dk, cos_ref[rows, :], -sin_ref[rows, :]).astype(BF)
        dv = jnp.where(lane < HEAD, dvs[0], dvs[1]).astype(BF)
        g_ref[rows, 128:256] = dk
        g_ref[rows, 256:384] = dv
        dk_sum += jnp.sum(dk.astype(F32), 0, keepdims=True)
        dv_sum += jnp.sum(dv.astype(F32), 0, keepdims=True)
    dq = rotate(dqt_ref[...].T * (1.0 / math.sqrt(HEAD)), cos_ref[...], -sin_ref[...]).astype(BF)
    g_ref[:, 0:128] = dq
    sum_ref[...] = jnp.concatenate([jnp.sum(dq.astype(F32), 0, keepdims=True), dk_sum, dv_sum], -1)
    acc = dot_nn(xt_ref[...], g_ref[...])
    r = acc.shape[0] // 16

    def put(acc, ref, order):
        for slot in range(4):
            for kf in range(4):
                rows = slice((slot * 4 + kf) * r, (slot * 4 + kf + 1) * r)
                ref[order[slot], kf] = acc[rows].astype(BF)

    if acc_ref is not None:
        acc_ref[...] = jnp.where(row == 0, 0.0, acc_ref[...]) + acc

    if theirs_ref is not None:

        @pl.when((pair == 0) & (row == rows_last))
        def _():
            put(acc if acc_ref is None else acc_ref[...], theirs_ref, TURNED)

    if mine_ref is not None:

        @pl.when((pair == 1) & (row == rows_last))
        def _():
            put(acc if acc_ref is None else acc_ref[...], mine_ref, (0, 1, 2, 3))


def back_call(place, lengths, seen, qkv, dattn, xt, tabs, length, span, part=None, into=(), block=256):
    attn, qa = seen
    n, width = qkv.shape
    rows, pairs = n // length, width // 384
    model = width // 3
    which = lambda p: jnp.where(p + (part or 0) == 0, 1 - place()[2], place()[2])
    one = lambda off: pl.BlockSpec((length, 128), lambda p, b: (b, off * pairs + 2 * span + which(p)))
    table = pl.BlockSpec((length, 128), lambda *_: (0, 0))
    grad = pl.BlockSpec((4, 4, model // 16, 384), lambda *_: (0, 0, 0, 0))
    grads = 2 if part is None else 1
    spec = pltpu.PrefetchScalarGridSpec(
        num_scalar_prefetch=0,
        grid=(grads, rows),
        in_specs=[
            pl.BlockSpec((None, 1, 128), lambda p, b: (b, 0, 0)),
            pl.BlockSpec((None, 2, length, 128), lambda p, b: (b, which(p), 0, 0)),
            one(1),
            one(2),
            pl.BlockSpec((length, 128), lambda p, b: (b, which(p))),
            one(0),
            table,
            table,
            pl.BlockSpec((model, length), lambda p, b: (0, b)),
        ]
        + [ANY] * len(into),
        out_specs=[
            pl.BlockSpec((length, 384), lambda p, b: (b, which(p))),
            pl.BlockSpec((None, None, 1, 384), lambda p, b: (b, which(p), 0, 0)),
        ]
        + [grad] * grads,
        scratch_shapes=[pltpu.VMEM((2, length, 128), BF), pltpu.VMEM((128, length), F32)]
        + ([pltpu.VMEM((model, 384), F32)] if rows > 1 else []),
    )
    return pl.pallas_call(
        functools.partial(back_kernel, block=block, part=part),
        grid_spec=spec,
        out_shape=[
            jax.ShapeDtypeStruct((n, 768), BF),
            jax.ShapeDtypeStruct((rows, 2, 1, 384), F32),
        ]
        + [jax.ShapeDtypeStruct((4, 4, model // 16, 384), BF)] * grads,
        input_output_aliases={9: 0, 10: 1} if into else {},
        cost_estimate=cost(rows * 40 * grads * length * length * 128, 24 * n * 128, rows * 4 * length * length),
        compiler_params=params(),
        name="attend_back",
    )(lengths, qa, qkv, qkv, attn, dattn, *tabs, xt, *into)


def norm_forward(u):
    center = u - jnp.mean(u, -1, keepdims=True)
    inverse = lax.rsqrt(jnp.mean(center * center, -1, keepdims=True) + NORM_EPS)
    return center * inverse, inverse


def norm_backward(incoming, normed, inverse, gain):
    scaled = incoming * gain
    mean = jnp.mean(scaled, -1, keepdims=True)
    return inverse * (scaled - mean - normed * jnp.mean(scaled * normed, -1, keepdims=True))


def adder(ref):
    def add(row, value, off=0):
        ref[row : row + 1, off : off + value.shape[1]] += jnp.sum(value, 0, keepdims=True)

    return add


def turn_halves(value, place, ref, cols):
    _, j, c = place
    turned = value.T
    r = turned.shape[0] // 8
    for cb in range(2):
        for jb in range(4):
            start = pl.multiple_of(((c ^ cb) * 4 + exchanged(j ^ jb, c)) * r, 16)
            ref[pl.ds(start, r), cols] = turned[(cb * 4 + jb) * r : (cb * 4 + jb + 1) * r].astype(BF)


def ffn_kernel(*refs, place, length, chunk, attn, side, shrink, blocks):
    live_ref, x_ref, cot_ref, v_ref = refs[:4]
    at_refs = refs[4 : 4 + attn]
    side_refs = refs[4 + attn : 4 + attn + side]
    shrink_refs = refs[4 + attn + side : 4 + attn + side + shrink]
    outs = refs[4 + attn + side + shrink :]
    out_ref, yt_ref, att_ref, dpre_ref, dr1_ref, da_ref, dat_ref, dvec_ref, late_ref, soon_ref, mine_ref = outs[:11]
    wo_ref, w1_ref, w2_ref, act_ref, dzt_ref, slope_ref, flat_o, flat_1, flat_2, sem_o, sem_1, sem_2 = outs[11:]
    step = pl.program_id(0)
    block, model = x_ref.shape
    ff = w1_ref.shape[1]
    per = length // block
    live = live_ref[:, :1]
    place = place()
    vec = lambda i: v_ref[i : i + 1, :]

    @pl.when(step == 0)
    def _():
        first = out_copies(place, side_refs, wo_ref, flat_o)
        second = expand_copies(place, side_refs, w1_ref, flat_1)
        third = shrink_copies(place, shrink_refs, w2_ref, flat_2)
        begin(first, sem_o)
        begin(second, sem_1)
        begin(third, sem_2)
        dvec_ref[...] = jnp.zeros_like(dvec_ref)
        finish(first, sem_o)
        own_part(place, first, wo_ref, flat_o)
        finish(second, sem_1)
        own_part(place, second, w1_ref, flat_1)
        finish(third, sem_2)
        own_part(place, third, w2_ref, flat_2)

    @pl.when(step < blocks)
    def _():
        here = pl.ds(pl.multiple_of(step * block, block), block)
        add = adder(dvec_ref)
        at = jnp.concatenate([ref[...] for ref in at_refs], -1)
        turn_columns(at.astype(F32), place, att_ref)
        r1 = x_ref[...].astype(F32) + (dot_nn(at, wo_ref[...]) + vec(7))
        n1, i1 = norm_forward(r1)
        y1 = n1 * vec(0) + vec(2)
        y1b = y1.astype(BF)
        turn_columns(y1, place, yt_ref)
        z = jnp.zeros((block, model), F32)
        for lo in range(0, ff, chunk):
            cols = slice(lo, lo + chunk)
            bias = v_ref[9 + lo // model : 10 + lo // model, lo % model : lo % model + chunk]
            pre = dot_nn(y1b, w1_ref[:, cols]) + bias
            phi = 0.5 * (1.0 + lax.erf(pre * ROOT_HALF))
            act = (pre * phi).astype(BF)
            act_ref[here, cols] = act
            slope_ref[:, cols] = phi + pre * (jnp.exp(-0.5 * pre * pre) * INV_ROOT_TAU)
            z = z + dot_nn(act, w2_ref[cols, :])
        r2 = y1 + (z + vec(8))
        n2, i2 = norm_forward(r2)
        out_ref[...] = (n2 * vec(1) + vec(3)).astype(BF)
        pos = lax.broadcasted_iota(jnp.int32, (block, model), 0) + (step % per) * block
        e = jnp.where(pos < live, cot_ref[...].astype(F32), 0.0)
        dy = norm_backward(e, n2, i2, vec(1))
        turn_halves(dy, place, dzt_ref, here)
        dz = dy.astype(BF)
        add(1, e * n2)
        add(3, e)
        add(8, dz.astype(F32))
        for lo in range(0, ff, chunk):
            cols = slice(lo, lo + chunk)
            dpre = (dot_nt(dz, w2_ref[cols, :]) * slope_ref[:, cols]).astype(BF)
            dpre_ref[:, cols] = dpre
            add(9 + lo // model, dpre.astype(F32), lo % model)
            dy = dy + dot_nt(dpre, w1_ref[:, cols])
        add(0, dy * n1)
        add(2, dy)
        dr1 = norm_backward(dy, n1, i1, vec(0))
        dr1_ref[...] = dr1
        da = dr1.astype(BF)
        da_ref[...] = da
        add(7, da.astype(F32))
        dat_ref[...] = dot_nt(da, wo_ref[...]).astype(BF)

    @pl.when(step >= blocks)
    def _():
        kf = step - blocks
        width = ff // 4
        r = model // 8
        cols = pl.ds(pl.multiple_of((place[0] ^ kf) * width, 128), width)
        acc = dot_nn(dzt_ref[...], act_ref[:, cols])
        for slot in range(4):
            mine_ref[slot] = acc[slot * r : (slot + 1) * r].astype(BF)
            to = TURNED[slot]
            (late_ref if to < 2 else soon_ref)[to % 2] = acc[(4 + slot) * r : (5 + slot) * r].astype(BF)


def ffn_call(place, lengths, x, attn, cot, side, shrink, vec, length, block=256, chunk=768):
    n, model = x.shape
    ff = 4 * model
    blocks = n // block
    at = lambda i: jnp.minimum(i, blocks - 1)
    tok = pl.BlockSpec((block, model), lambda i, *_: (at(i), 0))
    wide = pl.BlockSpec((block, ff), lambda i, *_: (at(i), 0))
    small = pl.BlockSpec((13, model), lambda i, *_: (0, 0))
    turned = pl.BlockSpec((model, block), lambda i, *_: (0, at(i)))
    grad = lambda slots: pl.BlockSpec((slots, None, model // 8, ff // 4), lambda i, *_: (0, jnp.maximum(i - blocks, 0), 0, 0))
    spec = pltpu.PrefetchScalarGridSpec(
        num_scalar_prefetch=0,
        grid=(blocks + 4,),
        in_specs=[pl.BlockSpec((None, 1, 128), lambda i: (at(i) // (length // block), 0, 0)), tok, tok, small]
        + [pl.BlockSpec((block, a.shape[1]), lambda i, *_: (at(i), 0)) for a in attn]
        + [ANY] * (len(side) + len(shrink)),
        out_specs=[tok, turned, turned, wide, tok, tok, tok, small, grad(2), grad(2), grad(4)],
        scratch_shapes=[
            pltpu.VMEM((model, model), BF),
            pltpu.VMEM((model, ff), BF),
            pltpu.VMEM((ff, model), BF),
            pltpu.VMEM((n, ff), BF),
            pltpu.VMEM((model, n), BF),
            pltpu.VMEM((block, ff), F32),
            pltpu.VMEM((model // 4, model), F32),
            pltpu.VMEM((model // 4, ff), F32),
            pltpu.VMEM((ff // 4, model), F32),
        ]
        + [pltpu.SemaphoreType.DMA((MOST,))] * 3,
    )
    s = lambda w, t: jax.ShapeDtypeStruct((n, w), t)
    flip = jax.ShapeDtypeStruct((model, n), BF)
    parts = lambda slots: jax.ShapeDtypeStruct((slots, 4, model // 8, ff // 4), BF)
    return pl.pallas_call(
        functools.partial(
            ffn_kernel, place=place, length=length, chunk=chunk, attn=len(attn), side=len(side), shrink=len(shrink), blocks=blocks
        ),
        grid_spec=spec,
        out_shape=[
            s(model, BF),
            flip,
            flip,
            s(ff, BF),
            s(model, F32),
            s(model, BF),
            s(model, BF),
            jax.ShapeDtypeStruct((13, model), F32),
            parts(2),
            parts(2),
            parts(4),
        ],
        cost_estimate=cost(
            2 * n * (3 * model * model + 10 * model * ff), n * (model * 20 + ff * 4) + model * ff * 4, n * ff * 2
        ),
        compiler_params=params(),
        name="ffn",
    )(lengths, x, cot, vec, *attn, *side, *shrink)


def side_grad_kernel(yt_ref, att_any, dpre_ref, da_ref, theirs_ref, mine_ref, att_ref, sem, *, steps):
    step = pl.program_id(0)
    late = pltpu.make_async_copy(att_any, att_ref, sem)
    pl.when(step == 0)(late.start)
    pl.when(step == steps - 1)(late.wait)
    r = yt_ref.shape[0] // 16

    def put(acc, ref, order):
        for slot in range(4):
            for kf in range(4):
                rows = slice((slot * 4 + kf) * r, (slot * 4 + kf + 1) * r)
                ref[order[slot], kf, :, : acc.shape[1]] = acc[rows].astype(BF)

    for first, ref, order in ((0, theirs_ref, TURNED), (steps, mine_ref, (0, 1, 2, 3))):

        @pl.when((step >= first) & (step < first + steps - 1))
        def _(ref=ref, order=order):
            put(dot_nn(yt_ref[...], dpre_ref[...]), ref, order)

        @pl.when(step == first + steps - 1)
        def _(ref=ref, order=order):
            put(dot_nn(att_ref[...], da_ref[...]), ref, order)


def side_grad_call(place, yt, att, dpre, da, block=768):
    model, n = yt.shape
    half = dpre.shape[1] // 2
    steps = half // block + 1
    which = lambda i: jnp.where(i < steps, 1 - place()[2], place()[2])
    turned = pl.BlockSpec((model, n), lambda i: (0, 0))
    width = half + model // 2
    out = lambda first: pl.BlockSpec(
        (4, 4, model // 16, block), lambda i: (0, 0, 0, jnp.clip(i - first, 0, steps - 1))
    )
    spec = pltpu.PrefetchScalarGridSpec(
        num_scalar_prefetch=0,
        grid=(2 * steps,),
        in_specs=[
            turned,
            ANY,
            pl.BlockSpec(
                (n, block), lambda i: (0, which(i) * (steps - 1) + jnp.minimum(i % steps, steps - 2))
            ),
            pl.BlockSpec((n, model // 2), lambda i: (0, which(i))),
        ],
        out_specs=[out(0), out(steps)],
        scratch_shapes=[pltpu.VMEM((model, n), BF), pltpu.SemaphoreType.DMA(())],
    )
    return pl.pallas_call(
        functools.partial(side_grad_kernel, steps=steps),
        grid_spec=spec,
        out_shape=[jax.ShapeDtypeStruct((4, 4, model // 16, width), BF)] * 2,
        cost_estimate=cost(4 * n * model * width, 4 * (n * model + n * width + model * width)),
        compiler_params=params(),
        name="side_grad",
    )(yt, att, dpre, da)


def token_kernel(*refs, place, pieces, parts):
    dr1_ref = refs[0]
    g_refs = refs[1 : 1 + parts]
    w_refs = refs[1 + parts : 1 + parts + pieces]
    o_ref, w_ref, flat_ref, sems = refs[1 + parts + pieces :]
    model = w_ref.shape[0]

    @pl.when(pl.program_id(0) == 0)
    def _():
        copies = in_copies(place(), w_refs, w_ref, flat_ref)
        begin(copies, sems)
        finish(copies, sems)
        own_part(place(), copies, w_ref, flat_ref)

    total = dr1_ref[...]
    for t in range(3):
        tiles = [ref[:, lo + t * 128 : lo + (t + 1) * 128] for ref in g_refs for lo in range(0, ref.shape[1], 384)]
        total = total + dot_nt(jnp.concatenate(tiles, -1), w_ref[:, t * model : (t + 1) * model])
    o_ref[...] = total.astype(BF)


def token_call(place, dr1, grads, weight, block=256):
    n, model = dr1.shape
    tok = lambda w: pl.BlockSpec((block, w), lambda i: (i, 0))
    spec = pltpu.PrefetchScalarGridSpec(
        num_scalar_prefetch=0,
        grid=(n // block,),
        in_specs=[tok(model)] + [tok(g.shape[1]) for g in grads] + [ANY] * len(weight),
        out_specs=tok(model),
        scratch_shapes=[
            pltpu.VMEM((model, 3 * model), BF),
            pltpu.VMEM((model // 4, 3 * model), F32),
            pltpu.SemaphoreType.DMA((MOST,)),
        ],
    )
    return pl.pallas_call(
        functools.partial(token_kernel, place=place, pieces=len(weight), parts=len(grads)),
        grid_spec=spec,
        out_shape=jax.ShapeDtypeStruct((n, model), BF),
        cost_estimate=cost(6 * n * model * model, n * model * 12 + 6 * model * model),
        compiler_params=params(),
        name="token_gradient",
    )(dr1, *grads, *weight)


def sums_kernel(*refs, place, jobs):
    f, step = place()[0], pl.program_id(0)
    at = 0
    outs = refs[sum(mine + recv + got for _, mine, recv, got in jobs) :]
    for kind, mine, recv, got in jobs:
        mines = refs[at : at + mine]
        recvs = refs[at + mine : at + mine + recv]
        gots = refs[at + mine + recv : at + mine + recv + got]
        at += mine + recv + got
        lo = 0
        for i, ref in enumerate(mines):
            cols = slice(lo, lo + ref.shape[-1])
            lo += ref.shape[-1]
            total = ref[...].astype(F32)
            if i < recv:
                total = total + recvs[i][...].astype(F32)
            for other in gots:
                total = total + other[:, :, cols].astype(F32)
            total = total.astype(BF)
            if kind == "own":
                for k in range(2):
                    outs[0][k ^ (f & 1), :, cols] = total[k]
            elif kind == "split":
                for k in range(4):

                    @pl.when(step == k // 2)
                    def _(k=k, total=total, cols=cols, out=outs[k]):
                        out[:, cols] = total[k % 2]

            else:
                outs[0][..., cols] = total
        outs = outs[4 if kind == "split" else 1 :]


def sums_call(place, *jobs):
    arrays, specs, shapes, outs, heads = [], [], [], [], []
    for kind, mine, recv, got in jobs:
        r, width = mine[0].shape[2], sum(m.shape[3] for m in mine)
        slot = {"first": 1, "second": 1, "own": 0, "split": 0}[kind]
        lead = 2 if kind == "first" else None
        block = lambda a, slot=slot, lead=lead: pl.BlockSpec(
            (lead, 2) + a.shape[2:], lambda k, slot=0 if lead and a.shape[0] == 2 else slot: (slot, k, 0, 0)
        )
        half = lambda a: pl.BlockSpec((2,) + a.shape[1:], lambda k: (k, 0, 0))
        arrays += [*mine, *recv, *got]
        specs += [block(a) if a.ndim == 4 else half(a) for a in (*mine, *recv, *got)]
        heads.append((kind, len(mine), len(recv), len(got)))
        if kind == "first":
            shapes.append(jax.ShapeDtypeStruct((2, 4, r, width), BF))
            outs.append(pl.BlockSpec((2, 2, r, width), lambda k: (0, k, 0, 0)))
        elif kind == "split":
            shapes += [jax.ShapeDtypeStruct((r, width), BF)] * 4
            outs += [pl.BlockSpec((r, width), lambda k: (0, 0))] * 4
        else:
            shapes.append(jax.ShapeDtypeStruct((4, r, width), BF))
            turn = kind == "own"
            outs.append(
                pl.BlockSpec((2, r, width), lambda k, t=turn: (k ^ (place()[0] >> 1) if t else k, 0, 0))
            )
    spec = pltpu.PrefetchScalarGridSpec(num_scalar_prefetch=0, grid=(2,), in_specs=specs, out_specs=outs)
    moved = sum(a.size for a in arrays)
    return pl.pallas_call(
        functools.partial(sums_kernel, place=place, jobs=tuple(heads)),
        grid_spec=spec,
        out_shape=shapes,
        cost_estimate=cost(moved, 2 * moved),
        compiler_params=params(),
        name="sums",
    )(*arrays)


def plus(*parts):
    total = parts[0].astype(F32)
    for part in parts[1:]:
        total = total + part.astype(F32)
    return total.astype(BF)


def send_z(own, one, two, three):
    return own, cross(one, 1), cross(two, 2), cross(three, 3)


def over_chips(total):
    return total, swap(total, 2), swap(total, 4), swap(total, 6)


def both_cores(chips):
    return (*chips, *(swap_core(part) for part in chips))


def vector_parts_kernel(rest_ref, *refs, place):
    sums, mine_ref = refs[:-1], refs[-1]
    f, j, c = place()
    rest = rest_ref[...]
    heads = []
    for t in range(3):
        cols = slice(t * 128, (t + 1) * 128)
        tiles = [jnp.sum(ref[:, pair, :, cols], 0) for ref in sums for pair in range(2)]
        heads.append(jnp.concatenate(tiles, -1))
    value = jnp.concatenate([rest[:4], *heads, rest[7:]], 0)
    mine_ref[...] = jnp.zeros_like(mine_ref)
    rows, model = value.shape
    width = model // 16
    for fb in range(4):
        for jb in range(4):
            lo = (fb * 4 + jb) * width
            part = value[:, lo : lo + width].astype(BF)
            mine_ref[exchanged(j ^ jb, c), f ^ fb, :rows, :width] = part


def vector_parts(place, rest, sums, r):
    whole = lambda a: pl.BlockSpec(a.shape, lambda *_, k=a.ndim: (0,) * k)
    spec = pltpu.PrefetchScalarGridSpec(
        num_scalar_prefetch=0,
        grid=(1,),
        in_specs=[whole(a) for a in (rest, *sums)],
        out_specs=pl.BlockSpec((4, 4, r, 128), lambda *_: (0, 0, 0, 0)),
    )
    return pl.pallas_call(
        functools.partial(vector_parts_kernel, place=place),
        grid_spec=spec,
        out_shape=jax.ShapeDtypeStruct((4, 4, r, 128), BF),
        compiler_params=params(),
        name="vector_parts",
    )(rest, *sums)


def adam_update(master, moment, square, gradient, rate, decay):
    momentum = BETA_ONE * moment + (1.0 - BETA_ONE) * gradient
    squares = BETA_TWO * square + (1.0 - BETA_TWO) * gradient * gradient
    corrected = momentum / (1.0 - BETA_ONE**STEP)
    spread = jnp.sqrt(squares / (1.0 - BETA_TWO**STEP))
    return (master - rate * (corrected / (spread + ADAM_EPS) + decay * master), momentum, squares)


def adam_block(state, outs, g, rate):
    w, m, s = (ref[...] for ref in state)
    for ref, value in zip(outs, adam_update(w, m, s, g, rate, WEIGHT_DECAY)):
        ref[...] = value


def adam_side_kernel(*refs, weights, moves, rates):
    state, grad, outs = refs[: 3 * weights], refs[3 * weights], refs[3 * weights + 1 : 6 * weights + 1]
    flats = refs[6 * weights + 1 :]
    step = pl.program_id(0)
    rows = state[0].shape[0]

    @pl.when(step == 0)
    def _():
        r = grad.shape[1]
        for weight, src, width in moves:
            for d in range(8):
                to = slice((d % 2) * width, (d % 2 + 1) * width)
                flats[weight][d // 2 * r : (d // 2 + 1) * r, to] = grad[d, :, src : src + width]

    here = pl.ds(pl.multiple_of(step * rows, rows), rows)
    for i in range(weights):
        cut = slice(3 * i, 3 * i + 3)
        adam_block(state[cut], outs[cut], flats[i][here, :].astype(F32), rates[i])


def adam_in_kernel(*refs, place, moves, rate, first):
    state, vector, grads, outs, vector_outs = refs[:3], refs[3:6], refs[6:14], refs[14:17], refs[17:20]
    flat, vector_flat = refs[20:]
    _, j, c = place()
    step = pl.program_id(0)
    rows = state[0].shape[0]

    @pl.when(step == 0)
    def _():
        for i, ref in enumerate(grads):
            half = c if i < 4 else 1 - c
            r = ref.shape[0]
            here = pl.ds(pl.multiple_of((j ^ (i % 4)) * r, 16), r)
            for src, to, stride in moves:
                cols = pl.ds(pl.multiple_of(to + half * stride, 128), 128)
                flat[here, cols] = ref[:, src : src + 128]
        count, width = vector_flat.shape
        width = width // 4
        both = lambda k: grads[k][:, first : first + 128].astype(F32) + grads[k + 4][:, first : first + 128].astype(F32)
        parts = [both(k) for k in range(4)]
        for at in range(4):
            k = j ^ at
            part = jnp.where(k == 0, parts[0], jnp.where(k == 1, parts[1], jnp.where(k == 2, parts[2], parts[3])))
            vector_flat[:, at * width : (at + 1) * width] = part[:count, :width]
        w, m, s = (ref[...] for ref in vector)
        for ref, value in zip(vector_outs, adam_update(w, m, s, vector_flat[...], 0.5, 0.0)):
            ref[...] = value

    here = pl.ds(pl.multiple_of(step * rows, rows), rows)
    adam_block(state, outs, flat[here, :].astype(F32), rate)


def adam_last_kernel(*refs, place, moves, rate, first, side_moves, side_rates):
    near, side, grads, side_grad, outs, flats = refs[:6], refs[6:12], refs[12:20], refs[20], refs[21:33], refs[33:]
    adam_in_kernel(*near, *grads, *outs[:6], *flats[:2], place=place, moves=moves, rate=rate, first=first)
    adam_side_kernel(*side, side_grad, *outs[6:], *flats[2:], weights=2, moves=side_moves, rates=side_rates)


def adam_last_call(place, state, vector, grads, moves, rate, first, sides, side_grad, side_moves, side_rates, steps=2):
    rows = state[0].shape[0] // steps
    block = lambda a: pl.BlockSpec((rows, a.shape[1]), lambda i: (i, 0))
    whole = lambda a: pl.BlockSpec(a.shape, lambda i, k=a.ndim: (0,) * k)
    flat = [a for side in sides for a in side]
    states = [*state, *vector, *flat]
    specs = [block(a) for a in state] + [whole(a) for a in vector] + [block(a) for a in flat]
    size = sum(a.size for a in states)
    return pl.pallas_call(
        functools.partial(
            adam_last_kernel,
            place=place,
            moves=tuple(moves),
            rate=rate,
            first=first,
            side_moves=tuple(side_moves),
            side_rates=tuple(side_rates),
        ),
        grid=(steps,),
        in_specs=specs + [whole(g) for g in grads] + [whole(side_grad)],
        out_specs=specs,
        scratch_shapes=[pltpu.VMEM(state[0].shape, BF), pltpu.VMEM(vector[0].shape, F32)]
        + [pltpu.VMEM(side[0].shape, BF) for side in sides],
        out_shape=[jax.ShapeDtypeStruct(a.shape, F32) for a in states],
        cost_estimate=cost(size * 4, size * 9),
        compiler_params=params(),
        name="adam_last",
    )(*states, *grads, side_grad)


def adam_turned_kernel(*refs, rate):
    state, grad, outs, (flat_ref, g_ref) = refs[:3], refs[3], refs[4:7], refs[7:]
    step = pl.program_id(0)
    rows = state[0].shape[0]

    @pl.when(step == 0)
    def _():
        r = grad.shape[1]
        for d in range(8):
            at = (d % 2) * 4 + d // 2
            flat_ref[at * r : (at + 1) * r, :] = grad[d].astype(F32)
        g_ref[...] = flat_ref[...].T

    adam_block(state, outs, g_ref[pl.ds(pl.multiple_of(step * rows, rows), rows), :], rate)


def adam_turned_call(state, grad, rate, steps=2):
    total, cols = state[0].shape
    block = pl.BlockSpec((total // steps, cols), lambda i: (i, 0))
    return pl.pallas_call(
        functools.partial(adam_turned_kernel, rate=rate),
        grid=(steps,),
        in_specs=[block] * 3 + [pl.BlockSpec(grad.shape, lambda i: (0, 0, 0))],
        out_specs=[block] * 3,
        scratch_shapes=[pltpu.VMEM((cols, total), F32), pltpu.VMEM((total, cols), F32)],
        out_shape=[jax.ShapeDtypeStruct(state[0].shape, F32)] * 3,
        cost_estimate=cost(total * cols * 12, total * cols * 28),
        compiler_params=params(),
        name="adam_turned",
    )(*state, grad)


def vector_rows(rest, sums):
    heads = jnp.concatenate([jnp.sum(s, 0) for s in sums], 0).reshape(-1, 3, 128)
    heads = heads.transpose(1, 0, 2).reshape(3, -1)
    return jnp.concatenate([rest[:4], heads, rest[7:]], 0)


def local(
    tokens,
    cotangent,
    lengths,
    inward_weight,
    inward_moment,
    inward_square,
    outward_weight,
    outward_moment,
    outward_square,
    expand_weight,
    expand_moment,
    expand_square,
    shrink_weight,
    shrink_moment,
    shrink_square,
    vectors,
    vector_moment,
    vector_square,
    sliced,
):
    _, length, model = tokens.shape
    x, cot = tokens.reshape(-1, model), cotangent.reshape(-1, model)
    tabs = tables(length)
    ff = 4 * model
    pairs = model // 128
    inward = (inward_weight, inward_moment, inward_square)
    outward = (outward_weight, outward_moment, outward_square)
    expand = (expand_weight, expand_moment, expand_square)
    shrink = (shrink_weight, shrink_moment, shrink_square)
    vector = (vectors, vector_moment, vector_square)
    rate_d, rate_o, rate_f = 1.0 / math.sqrt(model), 1.0 / math.sqrt(OUT_FAN), 1.0 / math.sqrt(ff)
    f, d = lax.axis_index("fsdp"), lax.axis_index("dp")
    j, c = d // 2, d % 2
    place = place_finder(sliced)
    lengths = jnp.broadcast_to(lengths[:, None, None], (lengths.shape[0], 1, 128))
    spans = [(0, 2), (2, 2), (4, 2)]

    if not sliced:
        low = [w.astype(BF) for w in (inward_weight, outward_weight, expand_weight, shrink_weight, vectors)]
        whole = [lax.all_gather(w, "fsdp", axis=0, tiled=True) for w in low[:4]]
        in_pieces, side_pieces, shrink_pieces = (whole[0],), (whole[1], whole[2]), (whole[3],)
        vec = lax.all_gather(low[4], "fsdp", axis=1, tiled=True).astype(F32)
        qkv, xt = qkv_call(place, x, in_pieces, vec[4:7].reshape(1, -1), tabs, length)
        seen = [attend_call(lengths, qkv, length, *span) for span in spans]
        out, yt, att, dpre, dr1, da, dattn, vec_rest, *far, near = ffn_call(
            place, lengths, x, [a for a, _ in seen], cot, side_pieces, shrink_pieces, vec, length
        )
        far = jnp.concatenate(far)
        order = jnp.array(TURNED)
        shrink_grad = jnp.concatenate([near, far[order]]).transpose(1, 3, 0, 2).reshape(ff, model)
        far, near = side_grad_call(place, yt, att, dpre, da)
        both = jnp.stack([near, far[order]]).transpose(2, 1, 3, 0, 4).reshape(model, 2, -1)
        expand_grad = both[:, :, : ff // 2].reshape(model, ff)
        outward_grad = both[:, :, ff // 2 :].reshape(model, model)
        backs = [back_call(place, lengths, seen[i], qkv, dattn, xt, tabs, length, i) for i in range(len(spans))]
        token_gradient = token_call(place, dr1, [b[0] for b in backs], in_pieces)
        parts = jnp.stack([part for _, _, far, near in backs for part in (near, far[order])])
        parts = parts.transpose(2, 1, 3, 0, 4).reshape(model, pairs, 3, 128)
        inward_grad = parts.transpose(0, 2, 1, 3).reshape(model, 3 * model)

        def reduced(g, axis=0):
            return lax.psum(lax.psum_scatter(g, "fsdp", scatter_dimension=axis, tiled=True).astype(F32), "dp")

        inward_new = adam_update(*inward, reduced(inward_grad), rate_d, WEIGHT_DECAY)
        outward_new = adam_update(*outward, reduced(outward_grad), rate_o, WEIGHT_DECAY)
        expand_new = adam_update(*expand, reduced(expand_grad), rate_d, WEIGHT_DECAY)
        shrink_new = adam_update(*shrink, reduced(shrink_grad), rate_f, WEIGHT_DECAY)
        vec_sum = reduced(vector_rows(vec_rest, [b[1] for b in backs]), 1)
        vector_new = adam_update(*vector, vec_sum, 0.5, 0.0)
    else:
        shard = model // 4
        r = shard // 4

        def columns(w):
            half = w.shape[1] // 2
            return lax.dynamic_slice(w, (j * r, c * half), (r, half))

        def rows(w):
            r = w.shape[0] // 8
            return lax.dynamic_slice(w, ((c * 4 + j) * r, 0), (r, w.shape[1]))

        low_vec = vectors.astype(BF)
        third = r + r // 3
        beside = jnp.pad(low_vec.reshape(-1, third), ((0, r - 3 * vectors.shape[0]), (0, 128 - third)))
        part_in = jnp.concatenate([columns(inward_weight).astype(BF), beside], -1)
        part_side = jnp.concatenate([columns(outward_weight), columns(expand_weight)], -1).astype(BF)
        part_shrink = rows(shrink_weight).astype(BF)
        z_in, lengths = after((jnp.stack(over_z(part_in)), lengths), part_side, part_shrink)
        by = z_in[:, : 3 * vectors.shape[0], part_in.shape[1] - 128 : part_in.shape[1] - 128 + third]
        by = (low_vec, *by.reshape(3, vectors.shape[0], shard))
        ordered = []
        for at in range(4):
            k = f ^ at
            ordered.append(jnp.where(k == 0, by[0], jnp.where(k == 1, by[1], jnp.where(k == 2, by[2], by[3]))))
        vec = jnp.concatenate(ordered, 1).astype(F32)
        bias = vec[4:7].reshape(1, -1)
        chips_in, z_side, vec, bias = after((over_chips(z_in), over_z(after(part_side, z_in)), vec, bias))
        in_pieces = (inward_weight, *both_cores(chips_in))
        z_side = jnp.stack(z_side)
        first_side, second_side = swap_first(z_side), swap_second(z_side)
        qkv, xt = qkv_call(place, x, after(in_pieces, z_side), bias, tabs, length)
        first_side, second_side = after((first_side, second_side), qkv)
        third_side = swap_second(first_side)
        z_shrink = over_z(after(part_shrink, first_side))
        far_z_side = swap_core(after(z_side, qkv))
        seen = [attend_call(lengths, after(qkv, first_side), length, *spans[0])]
        third_side, far_z_side, z_shrink = after((third_side, far_z_side, z_shrink), seen[0])
        z_shrink = jnp.stack(z_shrink)
        first_shrink, second_shrink = swap_first(z_shrink), swap_second(z_shrink)
        far_side = tuple(swap_core(part) for part in after((second_side, first_side, third_side), z_shrink))
        seen.append(attend_call(lengths, after(qkv, third_side, z_shrink), length, *spans[1]))
        first_shrink, second_shrink, far_side = after((first_shrink, second_shrink, far_side), seen[1])
        third_shrink = swap_second(first_shrink)
        shrink_near = (z_shrink, second_shrink, first_shrink)
        shrink_far = tuple(swap_core(part) for part in shrink_near)
        side_pieces = (outward_weight, expand_weight, z_side, second_side, first_side, third_side, far_z_side, *far_side)
        seen.append(attend_call(lengths, after(qkv, first_shrink), length, *spans[2]))
        third_shrink, shrink_far = after((third_shrink, shrink_far), seen[2])
        shrink_pieces = (shrink_weight, *shrink_near, third_shrink, *shrink_far, swap_core(third_shrink))

        out, yt, att, dpre, dr1, da, dattn, vec_rest, late_s, soon_s, mine_s = ffn_call(
            place, lengths, x, [a for a, _ in seen], cot, side_pieces, shrink_pieces, vec, length
        )

        def back(span, wait, *part):
            return back_call(place, lengths, seen[span], qkv, after(dattn, wait), xt, tabs, length, span, *part)

        to_s = sums_call(place, ("first", [mine_s], [swap_core(soon_s)], []))[0]
        got_s = swap_first(to_s)
        recv_s = swap_core(after(late_s, to_s))
        theirs_d, mine_d = side_grad_call(place, yt, att, after(dpre, to_s), da)
        got_s, recv_s = after((got_s, recv_s), theirs_d)
        on_s = sums_call(place, ("second", [mine_s], [recv_s], [got_s]))[0]
        last_s = swap_second(on_s)
        recv_d = swap_core(after(theirs_d, on_s))
        g0, sum0, theirs_0, mine_0 = back(0, on_s)
        last_s, recv_d = after((last_s, recv_d), g0)
        to_d, z_s = sums_call(
            place, ("first", [mine_d], [recv_d], []), ("own", [mine_s], [recv_s], [got_s, last_s])
        )
        got_d = swap_first(to_d)
        part_s = lax.psum_scatter(z_s, "fsdp", scatter_dimension=0)
        recv_0 = swap_core(after(theirs_0, to_d))
        g1, sum1, theirs_1, mine_1 = back(1, to_d)
        got_d, recv_0 = after((got_d, recv_0), g1)
        on_d = sums_call(place, ("second", [mine_d], [recv_d], [got_d]))[0]
        last_d = swap_second(on_d)
        recv_1 = swap_core(after(theirs_1, on_d))
        sum_s = lax.all_gather(after(part_s, on_d), "dp")
        g2, sum2, theirs_2, mine_2 = back(2, on_d)
        last_d, recv_1, theirs_2 = after((last_d, recv_1, theirs_2), g2)
        recv_2 = swap_core(theirs_2)
        z_d = sums_call(place, ("own", [mine_d], [recv_d], [got_d, last_d]))[0]
        part_d = lax.psum_scatter(z_d, "fsdp", scatter_dimension=0)
        mine_v = vector_parts(place, after(vec_rest, z_d), [sum0, sum1, sum2], r)
        mine_e = [mine_0, mine_1, mine_2, mine_v]
        recv_e = [recv_0, recv_1, after(recv_2, mine_v)]
        to_e = sums_call(place, ("first", mine_e, recv_e, []))[0]
        got_e = swap_first(to_e)
        token_gradient = token_call(place, after(dr1, to_e), [g0, g1, g2], in_pieces)
        got_e = after(got_e, token_gradient)
        on_e = sums_call(place, ("second", mine_e, recv_e, [got_e]))[0]
        last_e = swap_second(on_e)
        shrink_new = adam_turned_call((after(shrink[0], on_e), *shrink[1:]), sum_s, rate_f)
        last_e, part_d = after((last_e, part_d), shrink_new[0])
        sum_d = lax.all_gather(part_d, "dp")
        z_e = send_z(*sums_call(place, ("split", mine_e, recv_e, [got_e, last_e])))
        moves = [(0, ff // 2, model // 2), (1, 0, ff // 2)]
        sum_e = both_cores(over_chips(plus(*z_e)))
        moves_e = []
        for span in range(3):
            for t in range(3):
                moves_e.append((span * 384 + t * 128, t * model + span * 256, 128))
        new = adam_last_call(
            place,
            inward,
            vector,
            sum_e,
            moves_e,
            rate_d,
            3 * model // 2,
            [outward, expand],
            sum_d,
            moves,
            [rate_o, rate_d],
        )
        inward_new, vector_new, outward_new, expand_new = new[:3], new[3:6], new[6:9], new[9:]
    return (
        out.reshape(tokens.shape),
        token_gradient.reshape(tokens.shape),
        *inward_new,
        *outward_new,
        *expand_new,
        *shrink_new,
        *vector_new,
    )


def solution(mesh):
    both = P(("dp", "fsdp"), None, None)
    in_specs = (both, both, P(("dp", "fsdp"))) + (P("fsdp", None),) * 12 + (P(None, "fsdp"),) * 3
    out_specs = (both, both) + (P("fsdp", None),) * 12 + (P(None, "fsdp"),) * 3
    sliced = mesh.shape["dp"] == 8 and mesh.shape["fsdp"] == 4
    step = functools.partial(local, sliced=sliced)
    return jax.shard_map(step, mesh=mesh, in_specs=in_specs, out_specs=out_specs, check_vma=False)
```

```python
import functools
import math

import jax
import jax.numpy as jnp
import numpy as np
from jax import lax
from jax.experimental import pallas as pl
from jax.experimental.pallas import tpu as pltpu
from jax.sharding import PartitionSpec as P

BF = jnp.bfloat16
F32 = jnp.float32
HEAD = 64
STEP = 10
OUT_FAN = 3
BETA_ONE = 0.5
BETA_TWO = 0.5
ADAM_EPS = 1e-08
WEIGHT_DECAY = 0.01
NORM_EPS = 1e-12
NEG_FILL = -1000000000.0
ROOT_HALF = 0.7071067811865476
INV_ROOT_TAU = 0.3989422804014327
ANY = pl.BlockSpec(memory_space=pl.ANY)


def dot_nn(a, b):
    return lax.dot_general(a, b, (((1,), (0,)), ((), ())), preferred_element_type=F32)


def dot_nt(a, b):
    return lax.dot_general(a, b, (((1,), (1,)), ((), ())), preferred_element_type=F32)


def dot_tn(a, b):
    return lax.dot_general(a, b, (((0,), (0,)), ((), ())), preferred_element_type=F32)


def params():
    return pltpu.CompilerParams(vmem_limit_bytes=64 * 1024 * 1024)


def cost(flops, moved, trans=0):
    return pl.CostEstimate(flops=int(flops), bytes_accessed=int(moved), transcendentals=int(trans))


def swap(x, even, odd=None):
    odd = even if odd is None else odd
    return lax.ppermute(x, "dp", [(i, i ^ (odd if i % 2 else even)) for i in range(8)])


def swap_core(x):
    return swap(x, 1)


def swap_first(x):
    return swap(x, 4, 2)


def swap_second(x):
    return swap(x, 2, 4)


def cross(x, bit):
    return lax.ppermute(x, "fsdp", [(i, i ^ bit) for i in range(4)])


def over_z(part):
    return tuple(cross(part, k) for k in (1, 2, 3))


def after(x, *others):
    return lax.optimization_barrier((x, *others))[0]


TURNED = (0, 2, 1, 3)


def exchanged(k, c):
    return jnp.where(c == 0, k, (k & 1) * 2 + (k >> 1))


def column_copies(place, own, pieces, dst, flat, first=0, staged=True):
    f, j, c = place
    rows, cols = own.shape
    r, h = rows // 4, cols // 2
    out = [(own, flat)]
    for refs, half in ((pieces[:4], c), (pieces[4:], 1 - c)):
        for slot, ref in enumerate(refs):
            kj = exchanged(slot, half) if staged else slot
            for kf in range(1, 4):
                start = pl.multiple_of((f ^ kf) * rows + (j ^ kj) * r, 16)
                at = dst.at[pl.ds(start, r), pl.ds(pl.multiple_of(half * h, 128), h)]
                out.append((ref.at[kf - 1, :, pl.ds(first, h)], at))
    return out


def in_copies(place, refs, dst, flat):
    if len(refs) == 1:
        return [(refs[0], dst)]
    return column_copies(place, refs[0], refs[1:], dst, flat, staged=False)


def out_copies(place, refs, dst, flat):
    if len(refs) == 2:
        return [(refs[0], dst)]
    return column_copies(place, refs[0], refs[2:], dst, flat)


def expand_copies(place, refs, dst, flat):
    if len(refs) == 2:
        return [(refs[1], dst)]
    return column_copies(place, refs[1], refs[2:], dst, flat, refs[0].shape[1] // 2)


def shrink_copies(place, refs, dst, flat):
    if len(refs) == 1:
        return [(refs[0], dst)]
    f, j, c = place
    own, pieces = refs[0], refs[1:]
    rows = own.shape[0]
    r = rows // 8
    out = [(own, flat)]
    for refs, half in ((pieces[:4], c), (pieces[4:], 1 - c)):
        for slot, ref in enumerate(refs):
            kj = exchanged(slot, half)
            for kf in range(1, 4):
                start = pl.multiple_of((f ^ kf) * rows + half * (rows // 2) + (j ^ kj) * r, 16)
                out.append((ref.at[kf - 1], dst.at[pl.ds(start, r), :]))
    return out


def own_part(place, pairs, dst, flat):
    if len(pairs) > 1:
        rows = flat.shape[0]
        dst[pl.ds(pl.multiple_of(place[0] * rows, 16), rows), :] = flat[...].astype(BF)


MOST = 25


def begin(pairs, sems):
    for i, (src, dst) in enumerate(pairs):
        pltpu.make_async_copy(src, dst, sems.at[i]).start()


def finish(pairs, sems):
    for i, (src, dst) in enumerate(pairs):
        pltpu.make_async_copy(src, dst, sems.at[i]).wait()


def place_finder(sliced):
    def place():
        f, d = lax.axis_index("fsdp"), lax.axis_index("dp")
        if not sliced:
            f, d = f * 0, d * 0
        return f, d >> 1, d & 1

    return place


def tables(length):
    lane = np.arange(128)
    angles = np.arange(length)[:, None] * (10000.0 ** (-2.0 * ((lane % HEAD) // 2) / HEAD))[None, :]
    sine = np.where((lane % 2 == 0)[None, :], -np.sin(angles), np.sin(angles))
    return [jnp.asarray(part.astype(np.float32)) for part in (np.cos(angles), sine)]


def rotate(u, cosine, sine):
    even = lax.broadcasted_iota(jnp.int32, u.shape, 1) % 2 == 0
    return u * cosine + jnp.where(even, pltpu.roll(u, 127, 1), pltpu.roll(u, 1, 1)) * sine


def turn_columns(value, place, ref):
    f, j, c = place
    turned = value.T
    r = turned.shape[0] // 16
    for fb in range(4):
        for jb in range(4):
            start = pl.multiple_of((exchanged(j ^ jb, c) * 4 + (f ^ fb)) * r, 16)
            ref[pl.ds(start, r), :] = turned[(fb * 4 + jb) * r : (fb * 4 + jb + 1) * r].astype(BF)


def qkv_kernel(*refs, place, pieces):
    x_ref, b_ref, cos_ref, sin_ref = refs[:4]
    w_refs = refs[4 : 4 + pieces]
    o_ref, xt_ref, w_ref, flat_ref, sems = refs[4 + pieces :]

    @pl.when(pl.program_id(0) == 0)
    def _():
        copies = in_copies(place(), w_refs, w_ref, flat_ref)
        begin(copies, sems)
        finish(copies, sems)
        own_part(place(), copies, w_ref, flat_ref)

    x = x_ref[...]
    turn_columns(x.astype(F32), place(), xt_ref)
    cosine, sine = cos_ref[...], sin_ref[...]
    model, width = w_ref.shape
    for col in range(0, width, 256):
        acc = dot_nn(x, w_ref[:, col : col + 256]) + b_ref[:, col : col + 256]
        for tile in range(2):
            lo = col + tile * 128
            u = acc[:, tile * 128 : (tile + 1) * 128]
            if lo < 2 * model:
                u = rotate(u, cosine, sine)
            if lo < model:
                u = u * (1.0 / math.sqrt(HEAD))
            o_ref[:, lo : lo + 128] = u.astype(BF)


def qkv_call(place, x, weight, bias, tabs, length, block=256):
    n, model = x.shape
    per = length // block
    width = bias.shape[1]
    table = pl.BlockSpec((block, 128), lambda i: (i % per, 0))
    spec = pltpu.PrefetchScalarGridSpec(
        num_scalar_prefetch=0,
        grid=(n // block,),
        in_specs=[
            pl.BlockSpec((block, model), lambda i: (i, 0)),
            pl.BlockSpec((1, width), lambda i: (0, 0)),
            table,
            table,
        ]
        + [ANY] * len(weight),
        out_specs=[
            pl.BlockSpec((block, width), lambda i: (i, 0)),
            pl.BlockSpec((model, block), lambda i: (0, i)),
        ],
        scratch_shapes=[
            pltpu.VMEM((model, width), BF),
            pltpu.VMEM((model // 4, width), F32),
            pltpu.SemaphoreType.DMA((MOST,)),
        ],
    )
    return pl.pallas_call(
        functools.partial(qkv_kernel, place=place, pieces=len(weight)),
        grid_spec=spec,
        out_shape=[jax.ShapeDtypeStruct((n, width), BF), jax.ShapeDtypeStruct((model, n), BF)],
        cost_estimate=cost(2 * n * model * width, 2 * (n * model + model * width + n * width)),
        compiler_params=params(),
        name="qkv",
    )(x, bias, *tabs, *weight)


def attend_kernel(live_ref, q_ref, k_ref, v_ref, o_ref, qa_ref, *, block):
    length = q_ref.shape[0]
    live = live_ref[...]
    lane = lax.broadcasted_iota(jnp.int32, (length, 128), 1)
    pos = lax.broadcasted_iota(jnp.int32, (length, 128), 0)
    k, vt = k_ref[...].astype(F32), v_ref[...].astype(F32).T
    keys, values = [], []
    for h in range(2):
        own = (lane // HEAD) == h
        aux = HEAD * (1 - h)
        mask = jnp.where((lane == aux) & (pos >= live), NEG_FILL, 0.0)
        keys.append(jnp.where(own, k, mask).astype(BF))
        values.append(jnp.concatenate([vt[h * HEAD : (h + 1) * HEAD], jnp.ones((16, length), F32)], 0).astype(BF))
    lane = lax.broadcasted_iota(jnp.int32, (block, 128), 1)
    for i in range(length // block):
        rows = slice(i * block, (i + 1) * block)
        q = q_ref[rows, :].astype(F32)
        mixed, stats = [], []
        for h in range(2):
            own = (lane // HEAD) == h
            aux = HEAD * (1 - h)
            scores = dot_nt(keys[h], jnp.where(own, q, jnp.where(lane == aux, 1.0, 0.0)).astype(BF))
            top = jnp.max(scores, 0, keepdims=True)
            summed = dot_nn(values[h], jnp.exp(scores - top).astype(BF))
            total = summed[HEAD : HEAD + 1]
            mixed.append(summed[:HEAD] / total)
            shift = -(top + jnp.log(total))
            hi = shift.astype(BF).astype(F32)
            mid = (shift - hi).astype(BF).astype(F32)
            one = jnp.ones_like(hi)
            stats.append(jnp.concatenate([hi, mid, shift - hi - mid, one, jnp.zeros((HEAD - 4, block), F32)], 0))
        o_ref[rows, :] = jnp.concatenate(mixed, 0).T.astype(BF)
        extra = jnp.concatenate([stats[1], stats[0]], 0).T
        for h in range(2):
            qa_ref[h, rows, :] = jnp.where((lane // HEAD) == h, q, extra).astype(BF)


def attend_call(lengths, qkv, length, first, count, block=1024):
    n, width = qkv.shape
    rows, pairs = n // length, width // 384
    one = lambda off: pl.BlockSpec((length, 128), lambda b, p: (b, off * pairs + first + p))
    spec = pltpu.PrefetchScalarGridSpec(
        num_scalar_prefetch=0,
        grid=(rows, count),
        in_specs=[pl.BlockSpec((None, 1, 128), lambda b, p: (b, 0, 0)), one(0), one(1), one(2)],
        out_specs=[
            pl.BlockSpec((length, 128), lambda b, p: (b, p)),
            pl.BlockSpec((None, 2, length, 128), lambda b, p: (b, p, 0, 0)),
        ],
    )
    return pl.pallas_call(
        functools.partial(attend_kernel, block=block),
        grid_spec=spec,
        out_shape=[
            jax.ShapeDtypeStruct((n, count * 128), BF),
            jax.ShapeDtypeStruct((rows, 2 * count, length, 128), BF),
        ],
        cost_estimate=cost(rows * count * 32 * length * length * 128, 12 * n * count * 128, rows * count * 2 * length * length),
        compiler_params=params(),
        name="attend",
    )(lengths, qkv, qkv, qkv)


def back_kernel(*refs, block, part):
    live_ref, qa_ref, k_ref, v_ref, o_ref, do_ref, cos_ref, sin_ref, xt_ref = refs[:9]
    rest = refs[11:] if part == 1 else refs[9:]
    g_ref, sum_ref, *rest = rest
    theirs_ref = mine_ref = None
    if part != 1:
        theirs_ref, *rest = rest
    if part != 0:
        mine_ref, *rest = rest
    doa_ref, dqt_ref, *rest = rest
    acc_ref = rest[0] if rest else None
    length = k_ref.shape[0]
    pair, row, rows_last = pl.program_id(0) + (part or 0), pl.program_id(1), pl.num_programs(1) - 1
    live = live_ref[...]
    lane = lax.broadcasted_iota(jnp.int32, (length, 128), 1)
    do = do_ref[...].astype(F32)
    prod = do * o_ref[...].astype(F32)
    for h in range(2):
        own = (lane // HEAD) == h
        aux = HEAD * (1 - h)
        shift = -jnp.sum(jnp.where(own, prod, 0.0), -1, keepdims=True)
        hi = shift.astype(BF).astype(F32)
        extra = jnp.where(lane == aux, hi, jnp.where(lane == aux + 1, shift - hi, 0.0))
        doa_ref[h] = jnp.where(own, do, extra).astype(BF)
    lane = lax.broadcasted_iota(jnp.int32, (block, 128), 1)
    pos = lax.broadcasted_iota(jnp.int32, (block, 128), 0)
    dk_sum = jnp.zeros((1, 128), F32)
    dv_sum = jnp.zeros((1, 128), F32)
    for i in range(length // block):
        rows = slice(i * block, (i + 1) * block)
        k, v = k_ref[rows, :].astype(F32), v_ref[rows, :].astype(F32)
        kt = k.T.astype(BF)
        dks, dvs = [], []
        for h in range(2):
            own = (lane // HEAD) == h
            aux = HEAD * (1 - h)
            mask = jnp.where((lane == aux + 3) & (pos + i * block >= live), NEG_FILL, 0.0)
            ka = jnp.where(own, k, jnp.where((lane >= aux) & (lane < aux + 3), 1.0, mask)).astype(BF)
            va = jnp.where(own, v, jnp.where((lane >= aux) & (lane < aux + 2), 1.0, 0.0)).astype(BF)
            qa, doa = qa_ref[h], doa_ref[h]
            p = jnp.exp(dot_nt(ka, qa))
            ds = (p * dot_nt(va, doa)).astype(BF)
            dvs.append(dot_nn(p.astype(BF), doa))
            dks.append(dot_nn(ds, qa))
            dqt = dot_nn(kt[h * HEAD : (h + 1) * HEAD, :], ds)
            if i == 0:
                dqt_ref[h * HEAD : (h + 1) * HEAD, :] = dqt
            else:
                dqt_ref[h * HEAD : (h + 1) * HEAD, :] += dqt
        dk = jnp.where(lane < HEAD, dks[0], dks[1])
        dk = rotate(dk, cos_ref[rows, :], -sin_ref[rows, :]).astype(BF)
        dv = jnp.where(lane < HEAD, dvs[0], dvs[1]).astype(BF)
        g_ref[rows, 128:256] = dk
        g_ref[rows, 256:384] = dv
        dk_sum += jnp.sum(dk.astype(F32), 0, keepdims=True)
        dv_sum += jnp.sum(dv.astype(F32), 0, keepdims=True)
    dq = rotate(dqt_ref[...].T * (1.0 / math.sqrt(HEAD)), cos_ref[...], -sin_ref[...]).astype(BF)
    g_ref[:, 0:128] = dq
    sum_ref[...] = jnp.concatenate([jnp.sum(dq.astype(F32), 0, keepdims=True), dk_sum, dv_sum], -1)
    acc = dot_nn(xt_ref[...], g_ref[...])
    r = acc.shape[0] // 16

    def put(acc, ref, order):
        for slot in range(4):
            for kf in range(4):
                rows = slice((slot * 4 + kf) * r, (slot * 4 + kf + 1) * r)
                ref[order[slot], kf] = acc[rows].astype(BF)

    if acc_ref is not None:
        acc_ref[...] = jnp.where(row == 0, 0.0, acc_ref[...]) + acc

    if theirs_ref is not None:

        @pl.when((pair == 0) & (row == rows_last))
        def _():
            put(acc if acc_ref is None else acc_ref[...], theirs_ref, TURNED)

    if mine_ref is not None:

        @pl.when((pair == 1) & (row == rows_last))
        def _():
            put(acc if acc_ref is None else acc_ref[...], mine_ref, (0, 1, 2, 3))


def back_call(place, lengths, seen, qkv, dattn, xt, tabs, length, span, part=None, into=(), block=256):
    attn, qa = seen
    n, width = qkv.shape
    rows, pairs = n // length, width // 384
    model = width // 3
    which = lambda p: jnp.where(p + (part or 0) == 0, 1 - place()[2], place()[2])
    one = lambda off: pl.BlockSpec((length, 128), lambda p, b: (b, off * pairs + 2 * span + which(p)))
    table = pl.BlockSpec((length, 128), lambda *_: (0, 0))
    grad = pl.BlockSpec((4, 4, model // 16, 384), lambda *_: (0, 0, 0, 0))
    grads = 2 if part is None else 1
    spec = pltpu.PrefetchScalarGridSpec(
        num_scalar_prefetch=0,
        grid=(grads, rows),
        in_specs=[
            pl.BlockSpec((None, 1, 128), lambda p, b: (b, 0, 0)),
            pl.BlockSpec((None, 2, length, 128), lambda p, b: (b, which(p), 0, 0)),
            one(1),
            one(2),
            pl.BlockSpec((length, 128), lambda p, b: (b, which(p))),
            one(0),
            table,
            table,
            pl.BlockSpec((model, length), lambda p, b: (0, b)),
        ]
        + [ANY] * len(into),
        out_specs=[
            pl.BlockSpec((length, 384), lambda p, b: (b, which(p))),
            pl.BlockSpec((None, None, 1, 384), lambda p, b: (b, which(p), 0, 0)),
        ]
        + [grad] * grads,
        scratch_shapes=[pltpu.VMEM((2, length, 128), BF), pltpu.VMEM((128, length), F32)]
        + ([pltpu.VMEM((model, 384), F32)] if rows > 1 else []),
    )
    return pl.pallas_call(
        functools.partial(back_kernel, block=block, part=part),
        grid_spec=spec,
        out_shape=[
            jax.ShapeDtypeStruct((n, 768), BF),
            jax.ShapeDtypeStruct((rows, 2, 1, 384), F32),
        ]
        + [jax.ShapeDtypeStruct((4, 4, model // 16, 384), BF)] * grads,
        input_output_aliases={9: 0, 10: 1} if into else {},
        cost_estimate=cost(rows * 40 * grads * length * length * 128, 24 * n * 128, rows * 4 * length * length),
        compiler_params=params(),
        name="attend_back",
    )(lengths, qa, qkv, qkv, attn, dattn, *tabs, xt, *into)


def norm_forward(u):
    center = u - jnp.mean(u, -1, keepdims=True)
    inverse = lax.rsqrt(jnp.mean(center * center, -1, keepdims=True) + NORM_EPS)
    return center * inverse, inverse


def norm_backward(incoming, normed, inverse, gain):
    scaled = incoming * gain
    mean = jnp.mean(scaled, -1, keepdims=True)
    return inverse * (scaled - mean - normed * jnp.mean(scaled * normed, -1, keepdims=True))


def adder(ref):
    def add(row, value, off=0):
        ref[row : row + 1, off : off + value.shape[1]] += jnp.sum(value, 0, keepdims=True)

    return add


def turn_halves(value, place, ref, cols):
    _, j, c = place
    turned = value.T
    r = turned.shape[0] // 8
    for cb in range(2):
        for jb in range(4):
            start = pl.multiple_of(((c ^ cb) * 4 + exchanged(j ^ jb, c)) * r, 16)
            ref[pl.ds(start, r), cols] = turned[(cb * 4 + jb) * r : (cb * 4 + jb + 1) * r].astype(BF)


def ffn_kernel(*refs, place, length, chunk, attn, side, shrink, blocks):
    live_ref, x_ref, cot_ref, v_ref = refs[:4]
    at_refs = refs[4 : 4 + attn]
    side_refs = refs[4 + attn : 4 + attn + side]
    shrink_refs = refs[4 + attn + side : 4 + attn + side + shrink]
    outs = refs[4 + attn + side + shrink :]
    out_ref, yt_ref, att_ref, dpre_ref, dr1_ref, da_ref, dat_ref, dvec_ref, late_ref, soon_ref, mine_ref = outs[:11]
    wo_ref, w1_ref, w2_ref, act_ref, dzt_ref, slope_ref, flat_o, flat_1, flat_2, sem_o, sem_1, sem_2 = outs[11:]
    step = pl.program_id(0)
    block, model = x_ref.shape
    ff = w1_ref.shape[1]
    per = length // block
    live = live_ref[:, :1]
    place = place()
    vec = lambda i: v_ref[i : i + 1, :]

    @pl.when(step == 0)
    def _():
        first = out_copies(place, side_refs, wo_ref, flat_o)
        second = expand_copies(place, side_refs, w1_ref, flat_1)
        third = shrink_copies(place, shrink_refs, w2_ref, flat_2)
        begin(first, sem_o)
        begin(second, sem_1)
        begin(third, sem_2)
        dvec_ref[...] = jnp.zeros_like(dvec_ref)
        finish(first, sem_o)
        own_part(place, first, wo_ref, flat_o)
        finish(second, sem_1)
        own_part(place, second, w1_ref, flat_1)
        finish(third, sem_2)
        own_part(place, third, w2_ref, flat_2)

    @pl.when(step < blocks)
    def _():
        here = pl.ds(pl.multiple_of(step * block, block), block)
        add = adder(dvec_ref)
        at = jnp.concatenate([ref[...] for ref in at_refs], -1)
        turn_columns(at.astype(F32), place, att_ref)
        r1 = x_ref[...].astype(F32) + (dot_nn(at, wo_ref[...]) + vec(7))
        n1, i1 = norm_forward(r1)
        y1 = n1 * vec(0) + vec(2)
        y1b = y1.astype(BF)
        turn_columns(y1, place, yt_ref)
        z = jnp.zeros((block, model), F32)
        for lo in range(0, ff, chunk):
            cols = slice(lo, lo + chunk)
            bias = v_ref[9 + lo // model : 10 + lo // model, lo % model : lo % model + chunk]
            pre = dot_nn(y1b, w1_ref[:, cols]) + bias
            phi = 0.5 * (1.0 + lax.erf(pre * ROOT_HALF))
            act = (pre * phi).astype(BF)
            act_ref[here, cols] = act
            slope_ref[:, cols] = phi + pre * (jnp.exp(-0.5 * pre * pre) * INV_ROOT_TAU)
            z = z + dot_nn(act, w2_ref[cols, :])
        r2 = y1 + (z + vec(8))
        n2, i2 = norm_forward(r2)
        out_ref[...] = (n2 * vec(1) + vec(3)).astype(BF)
        pos = lax.broadcasted_iota(jnp.int32, (block, model), 0) + (step % per) * block
        e = jnp.where(pos < live, cot_ref[...].astype(F32), 0.0)
        dy = norm_backward(e, n2, i2, vec(1))
        turn_halves(dy, place, dzt_ref, here)
        dz = dy.astype(BF)
        add(1, e * n2)
        add(3, e)
        add(8, dz.astype(F32))
        for lo in range(0, ff, chunk):
            cols = slice(lo, lo + chunk)
            dpre = (dot_nt(dz, w2_ref[cols, :]) * slope_ref[:, cols]).astype(BF)
            dpre_ref[:, cols] = dpre
            add(9 + lo // model, dpre.astype(F32), lo % model)
            dy = dy + dot_nt(dpre, w1_ref[:, cols])
        add(0, dy * n1)
        add(2, dy)
        dr1 = norm_backward(dy, n1, i1, vec(0))
        dr1_ref[...] = dr1
        da = dr1.astype(BF)
        da_ref[...] = da
        add(7, da.astype(F32))
        dat_ref[...] = dot_nt(da, wo_ref[...]).astype(BF)

    @pl.when(step >= blocks)
    def _():
        kf = step - blocks
        width = ff // 4
        r = model // 8
        cols = pl.ds(pl.multiple_of((place[0] ^ kf) * width, 128), width)
        acc = dot_nn(dzt_ref[...], act_ref[:, cols])
        for slot in range(4):
            mine_ref[slot] = acc[slot * r : (slot + 1) * r].astype(BF)
            to = TURNED[slot]
            (late_ref if to < 2 else soon_ref)[to % 2] = acc[(4 + slot) * r : (5 + slot) * r].astype(BF)


def ffn_call(place, lengths, x, attn, cot, side, shrink, vec, length, block=256, chunk=768):
    n, model = x.shape
    ff = 4 * model
    blocks = n // block
    at = lambda i: jnp.minimum(i, blocks - 1)
    tok = pl.BlockSpec((block, model), lambda i, *_: (at(i), 0))
    wide = pl.BlockSpec((block, ff), lambda i, *_: (at(i), 0))
    small = pl.BlockSpec((13, model), lambda i, *_: (0, 0))
    turned = pl.BlockSpec((model, block), lambda i, *_: (0, at(i)))
    grad = lambda slots: pl.BlockSpec((slots, None, model // 8, ff // 4), lambda i, *_: (0, jnp.maximum(i - blocks, 0), 0, 0))
    spec = pltpu.PrefetchScalarGridSpec(
        num_scalar_prefetch=0,
        grid=(blocks + 4,),
        in_specs=[pl.BlockSpec((None, 1, 128), lambda i: (at(i) // (length // block), 0, 0)), tok, tok, small]
        + [pl.BlockSpec((block, a.shape[1]), lambda i, *_: (at(i), 0)) for a in attn]
        + [ANY] * (len(side) + len(shrink)),
        out_specs=[tok, turned, turned, wide, tok, tok, tok, small, grad(2), grad(2), grad(4)],
        scratch_shapes=[
            pltpu.VMEM((model, model), BF),
            pltpu.VMEM((model, ff), BF),
            pltpu.VMEM((ff, model), BF),
            pltpu.VMEM((n, ff), BF),
            pltpu.VMEM((model, n), BF),
            pltpu.VMEM((block, ff), F32),
            pltpu.VMEM((model // 4, model), F32),
            pltpu.VMEM((model // 4, ff), F32),
            pltpu.VMEM((ff // 4, model), F32),
        ]
        + [pltpu.SemaphoreType.DMA((MOST,))] * 3,
    )
    s = lambda w, t: jax.ShapeDtypeStruct((n, w), t)
    flip = jax.ShapeDtypeStruct((model, n), BF)
    parts = lambda slots: jax.ShapeDtypeStruct((slots, 4, model // 8, ff // 4), BF)
    return pl.pallas_call(
        functools.partial(
            ffn_kernel, place=place, length=length, chunk=chunk, attn=len(attn), side=len(side), shrink=len(shrink), blocks=blocks
        ),
        grid_spec=spec,
        out_shape=[
            s(model, BF),
            flip,
            flip,
            s(ff, BF),
            s(model, F32),
            s(model, BF),
            s(model, BF),
            jax.ShapeDtypeStruct((13, model), F32),
            parts(2),
            parts(2),
            parts(4),
        ],
        cost_estimate=cost(
            2 * n * (3 * model * model + 10 * model * ff), n * (model * 20 + ff * 4) + model * ff * 4, n * ff * 2
        ),
        compiler_params=params(),
        name="ffn",
    )(lengths, x, cot, vec, *attn, *side, *shrink)


def side_grad_kernel(yt_ref, att_any, dpre_ref, da_ref, theirs_ref, mine_ref, att_ref, sem, *, steps):
    step = pl.program_id(0)
    late = pltpu.make_async_copy(att_any, att_ref, sem)
    pl.when(step == 0)(late.start)
    pl.when(step == steps - 1)(late.wait)
    r = yt_ref.shape[0] // 16

    def put(acc, ref, order):
        for slot in range(4):
            for kf in range(4):
                rows = slice((slot * 4 + kf) * r, (slot * 4 + kf + 1) * r)
                ref[order[slot], kf, :, : acc.shape[1]] = acc[rows].astype(BF)

    for first, ref, order in ((0, theirs_ref, TURNED), (steps, mine_ref, (0, 1, 2, 3))):

        @pl.when((step >= first) & (step < first + steps - 1))
        def _(ref=ref, order=order):
            put(dot_nn(yt_ref[...], dpre_ref[...]), ref, order)

        @pl.when(step == first + steps - 1)
        def _(ref=ref, order=order):
            put(dot_nn(att_ref[...], da_ref[...]), ref, order)


def side_grad_call(place, yt, att, dpre, da, block=768):
    model, n = yt.shape
    half = dpre.shape[1] // 2
    steps = half // block + 1
    which = lambda i: jnp.where(i < steps, 1 - place()[2], place()[2])
    turned = pl.BlockSpec((model, n), lambda i: (0, 0))
    width = half + model // 2
    out = lambda first: pl.BlockSpec(
        (4, 4, model // 16, block), lambda i: (0, 0, 0, jnp.clip(i - first, 0, steps - 1))
    )
    spec = pltpu.PrefetchScalarGridSpec(
        num_scalar_prefetch=0,
        grid=(2 * steps,),
        in_specs=[
            turned,
            ANY,
            pl.BlockSpec(
                (n, block), lambda i: (0, which(i) * (steps - 1) + jnp.minimum(i % steps, steps - 2))
            ),
            pl.BlockSpec((n, model // 2), lambda i: (0, which(i))),
        ],
        out_specs=[out(0), out(steps)],
        scratch_shapes=[pltpu.VMEM((model, n), BF), pltpu.SemaphoreType.DMA(())],
    )
    return pl.pallas_call(
        functools.partial(side_grad_kernel, steps=steps),
        grid_spec=spec,
        out_shape=[jax.ShapeDtypeStruct((4, 4, model // 16, width), BF)] * 2,
        cost_estimate=cost(4 * n * model * width, 4 * (n * model + n * width + model * width)),
        compiler_params=params(),
        name="side_grad",
    )(yt, att, dpre, da)


def token_kernel(*refs, place, pieces, parts):
    dr1_ref = refs[0]
    g_refs = refs[1 : 1 + parts]
    w_refs = refs[1 + parts : 1 + parts + pieces]
    o_ref, w_ref, flat_ref, sems = refs[1 + parts + pieces :]
    model = w_ref.shape[0]

    @pl.when(pl.program_id(0) == 0)
    def _():
        copies = in_copies(place(), w_refs, w_ref, flat_ref)
        begin(copies, sems)
        finish(copies, sems)
        own_part(place(), copies, w_ref, flat_ref)

    total = dr1_ref[...]
    for t in range(3):
        tiles = [ref[:, lo + t * 128 : lo + (t + 1) * 128] for ref in g_refs for lo in range(0, ref.shape[1], 384)]
        total = total + dot_nt(jnp.concatenate(tiles, -1), w_ref[:, t * model : (t + 1) * model])
    o_ref[...] = total.astype(BF)


def token_call(place, dr1, grads, weight, block=256):
    n, model = dr1.shape
    tok = lambda w: pl.BlockSpec((block, w), lambda i: (i, 0))
    spec = pltpu.PrefetchScalarGridSpec(
        num_scalar_prefetch=0,
        grid=(n // block,),
        in_specs=[tok(model)] + [tok(g.shape[1]) for g in grads] + [ANY] * len(weight),
        out_specs=tok(model),
        scratch_shapes=[
            pltpu.VMEM((model, 3 * model), BF),
            pltpu.VMEM((model // 4, 3 * model), F32),
            pltpu.SemaphoreType.DMA((MOST,)),
        ],
    )
    return pl.pallas_call(
        functools.partial(token_kernel, place=place, pieces=len(weight), parts=len(grads)),
        grid_spec=spec,
        out_shape=jax.ShapeDtypeStruct((n, model), BF),
        cost_estimate=cost(6 * n * model * model, n * model * 12 + 6 * model * model),
        compiler_params=params(),
        name="token_gradient",
    )(dr1, *grads, *weight)


def sums_kernel(*refs, place, jobs):
    f, step = place()[0], pl.program_id(0)
    at = 0
    outs = refs[sum(mine + recv + got for _, mine, recv, got in jobs) :]
    for kind, mine, recv, got in jobs:
        mines = refs[at : at + mine]
        recvs = refs[at + mine : at + mine + recv]
        gots = refs[at + mine + recv : at + mine + recv + got]
        at += mine + recv + got
        lo = 0
        for i, ref in enumerate(mines):
            cols = slice(lo, lo + ref.shape[-1])
            lo += ref.shape[-1]
            total = ref[...].astype(F32)
            if i < recv:
                total = total + recvs[i][...].astype(F32)
            for other in gots:
                total = total + other[:, :, cols].astype(F32)
            total = total.astype(BF)
            if kind == "own":
                for k in range(2):
                    outs[0][k ^ (f & 1), :, cols] = total[k]
            elif kind == "split":
                for k in range(4):

                    @pl.when(step == k // 2)
                    def _(k=k, total=total, cols=cols, out=outs[k]):
                        out[:, cols] = total[k % 2]

            else:
                outs[0][..., cols] = total
        outs = outs[4 if kind == "split" else 1 :]


def sums_call(place, *jobs):
    arrays, specs, shapes, outs, heads = [], [], [], [], []
    for kind, mine, recv, got in jobs:
        r, width = mine[0].shape[2], sum(m.shape[3] for m in mine)
        slot = {"first": 1, "second": 1, "own": 0, "split": 0}[kind]
        lead = 2 if kind == "first" else None
        block = lambda a, slot=slot, lead=lead: pl.BlockSpec(
            (lead, 2) + a.shape[2:], lambda k, slot=0 if lead and a.shape[0] == 2 else slot: (slot, k, 0, 0)
        )
        half = lambda a: pl.BlockSpec((2,) + a.shape[1:], lambda k: (k, 0, 0))
        arrays += [*mine, *recv, *got]
        specs += [block(a) if a.ndim == 4 else half(a) for a in (*mine, *recv, *got)]
        heads.append((kind, len(mine), len(recv), len(got)))
        if kind == "first":
            shapes.append(jax.ShapeDtypeStruct((2, 4, r, width), BF))
            outs.append(pl.BlockSpec((2, 2, r, width), lambda k: (0, k, 0, 0)))
        elif kind == "split":
            shapes += [jax.ShapeDtypeStruct((r, width), BF)] * 4
            outs += [pl.BlockSpec((r, width), lambda k: (0, 0))] * 4
        else:
            shapes.append(jax.ShapeDtypeStruct((4, r, width), BF))
            turn = kind == "own"
            outs.append(
                pl.BlockSpec((2, r, width), lambda k, t=turn: (k ^ (place()[0] >> 1) if t else k, 0, 0))
            )
    spec = pltpu.PrefetchScalarGridSpec(num_scalar_prefetch=0, grid=(2,), in_specs=specs, out_specs=outs)
    moved = sum(a.size for a in arrays)
    return pl.pallas_call(
        functools.partial(sums_kernel, place=place, jobs=tuple(heads)),
        grid_spec=spec,
        out_shape=shapes,
        cost_estimate=cost(moved, 2 * moved),
        compiler_params=params(),
        name="sums",
    )(*arrays)


def plus(*parts):
    total = parts[0].astype(F32)
    for part in parts[1:]:
        total = total + part.astype(F32)
    return total.astype(BF)


def send_z(own, one, two, three):
    return own, cross(one, 1), cross(two, 2), cross(three, 3)


def over_chips(total):
    return total, swap(total, 2), swap(total, 4), swap(total, 6)


def both_cores(chips):
    return (*chips, *(swap_core(part) for part in chips))


def vector_parts_kernel(rest_ref, *refs, place):
    sums, mine_ref, wide_ref = refs[:-2], refs[-2], refs[-1]
    f, j, c = place()
    rest = rest_ref[...]
    heads = []
    for t in range(3):
        cols = slice(t * 128, (t + 1) * 128)
        tiles = [jnp.sum(ref[:, pair, :, cols], 0) for ref in sums for pair in range(2)]
        heads.append(jnp.concatenate(tiles, -1))
    value = jnp.concatenate([rest[:4], *heads, rest[7:]], 0)
    wide_ref[...] = jnp.zeros_like(wide_ref)
    rows, model = value.shape
    width = model // 16
    for fb in range(4):
        for jb in range(4):
            lo = (fb * 4 + jb) * width
            wide_ref[exchanged(j ^ jb, c), f ^ fb, :rows, :width] = value[:, lo : lo + width]
    mine_ref[...] = wide_ref[...].astype(BF)


def vector_parts(place, rest, sums, r):
    whole = lambda a: pl.BlockSpec(a.shape, lambda *_, k=a.ndim: (0,) * k)
    spec = pltpu.PrefetchScalarGridSpec(
        num_scalar_prefetch=0,
        grid=(1,),
        in_specs=[whole(a) for a in (rest, *sums)],
        out_specs=pl.BlockSpec((4, 4, r, 128), lambda *_: (0, 0, 0, 0)),
        scratch_shapes=[pltpu.VMEM((4, 4, r, 128), F32)],
    )
    return pl.pallas_call(
        functools.partial(vector_parts_kernel, place=place),
        grid_spec=spec,
        out_shape=jax.ShapeDtypeStruct((4, 4, r, 128), BF),
        compiler_params=params(),
        name="vector_parts",
    )(rest, *sums)


def adam_update(master, moment, square, gradient, rate, decay):
    momentum = BETA_ONE * moment + (1.0 - BETA_ONE) * gradient
    squares = BETA_TWO * square + (1.0 - BETA_TWO) * gradient * gradient
    corrected = momentum / (1.0 - BETA_ONE**STEP)
    spread = jnp.sqrt(squares / (1.0 - BETA_TWO**STEP))
    return (master - rate * (corrected / (spread + ADAM_EPS) + decay * master), momentum, squares)


def adam_block(state, outs, g, rate):
    w, m, s = (ref[...] for ref in state)
    for ref, value in zip(outs, adam_update(w, m, s, g, rate, WEIGHT_DECAY)):
        ref[...] = value


def adam_side_kernel(*refs, weights, moves, rates):
    state, grad, outs = refs[: 3 * weights], refs[3 * weights], refs[3 * weights + 1 : 6 * weights + 1]
    flats = refs[6 * weights + 1 :]
    step = pl.program_id(0)
    rows = state[0].shape[0]

    @pl.when(step == 0)
    def _():
        r = grad.shape[1]
        for weight, src, width in moves:
            for d in range(8):
                to = slice((d % 2) * width, (d % 2 + 1) * width)
                flats[weight][d // 2 * r : (d // 2 + 1) * r, to] = grad[d, :, src : src + width]

    here = pl.ds(pl.multiple_of(step * rows, rows), rows)
    for i in range(weights):
        cut = slice(3 * i, 3 * i + 3)
        adam_block(state[cut], outs[cut], flats[i][here, :].astype(F32), rates[i])


def adam_in_kernel(*refs, place, moves, rate, first):
    state, vector, grads, outs, vector_outs = refs[:3], refs[3:6], refs[6:14], refs[14:17], refs[17:20]
    flat, vector_flat = refs[20:]
    _, j, c = place()
    step = pl.program_id(0)
    rows = state[0].shape[0]

    @pl.when(step == 0)
    def _():
        for i, ref in enumerate(grads):
            half = c if i < 4 else 1 - c
            r = ref.shape[0]
            here = pl.ds(pl.multiple_of((j ^ (i % 4)) * r, 16), r)
            for src, to, stride in moves:
                cols = pl.ds(pl.multiple_of(to + half * stride, 128), 128)
                flat[here, cols] = ref[:, src : src + 128]
        count, width = vector_flat.shape
        width = width // 4
        both = lambda k: grads[k][:, first : first + 128].astype(F32) + grads[k + 4][:, first : first + 128].astype(F32)
        parts = [both(k) for k in range(4)]
        for at in range(4):
            k = j ^ at
            part = jnp.where(k == 0, parts[0], jnp.where(k == 1, parts[1], jnp.where(k == 2, parts[2], parts[3])))
            vector_flat[:, at * width : (at + 1) * width] = part[:count, :width]
        w, m, s = (ref[...] for ref in vector)
        for ref, value in zip(vector_outs, adam_update(w, m, s, vector_flat[...], 0.5, 0.0)):
            ref[...] = value

    here = pl.ds(pl.multiple_of(step * rows, rows), rows)
    adam_block(state, outs, flat[here, :].astype(F32), rate)


def adam_last_kernel(*refs, place, moves, rate, first, side_moves, side_rates):
    near, side, grads, side_grad, outs, flats = refs[:6], refs[6:12], refs[12:20], refs[20], refs[21:33], refs[33:]
    adam_in_kernel(*near, *grads, *outs[:6], *flats[:2], place=place, moves=moves, rate=rate, first=first)
    adam_side_kernel(*side, side_grad, *outs[6:], *flats[2:], weights=2, moves=side_moves, rates=side_rates)


def adam_last_call(place, state, vector, grads, moves, rate, first, sides, side_grad, side_moves, side_rates, steps=2):
    rows = state[0].shape[0] // steps
    block = lambda a: pl.BlockSpec((rows, a.shape[1]), lambda i: (i, 0))
    whole = lambda a: pl.BlockSpec(a.shape, lambda i, k=a.ndim: (0,) * k)
    flat = [a for side in sides for a in side]
    states = [*state, *vector, *flat]
    specs = [block(a) for a in state] + [whole(a) for a in vector] + [block(a) for a in flat]
    size = sum(a.size for a in states)
    return pl.pallas_call(
        functools.partial(
            adam_last_kernel,
            place=place,
            moves=tuple(moves),
            rate=rate,
            first=first,
            side_moves=tuple(side_moves),
            side_rates=tuple(side_rates),
        ),
        grid=(steps,),
        in_specs=specs + [whole(g) for g in grads] + [whole(side_grad)],
        out_specs=specs,
        scratch_shapes=[pltpu.VMEM(state[0].shape, BF), pltpu.VMEM(vector[0].shape, F32)]
        + [pltpu.VMEM(side[0].shape, BF) for side in sides],
        out_shape=[jax.ShapeDtypeStruct(a.shape, F32) for a in states],
        cost_estimate=cost(size * 4, size * 9),
        compiler_params=params(),
        name="adam_last",
    )(*states, *grads, side_grad)


def adam_turned_kernel(*refs, rate):
    state, grad, outs, (flat_ref, g_ref) = refs[:3], refs[3], refs[4:7], refs[7:]
    step = pl.program_id(0)
    rows = state[0].shape[0]

    @pl.when(step == 0)
    def _():
        r = grad.shape[1]
        for d in range(8):
            at = (d % 2) * 4 + d // 2
            flat_ref[at * r : (at + 1) * r, :] = grad[d].astype(F32)
        g_ref[...] = flat_ref[...].T

    adam_block(state, outs, g_ref[pl.ds(pl.multiple_of(step * rows, rows), rows), :], rate)


def adam_turned_call(state, grad, rate, steps=2):
    total, cols = state[0].shape
    block = pl.BlockSpec((total // steps, cols), lambda i: (i, 0))
    return pl.pallas_call(
        functools.partial(adam_turned_kernel, rate=rate),
        grid=(steps,),
        in_specs=[block] * 3 + [pl.BlockSpec(grad.shape, lambda i: (0, 0, 0))],
        out_specs=[block] * 3,
        scratch_shapes=[pltpu.VMEM((cols, total), F32), pltpu.VMEM((total, cols), F32)],
        out_shape=[jax.ShapeDtypeStruct(state[0].shape, F32)] * 3,
        cost_estimate=cost(total * cols * 12, total * cols * 28),
        compiler_params=params(),
        name="adam_turned",
    )(*state, grad)


def vector_rows(rest, sums):
    heads = jnp.concatenate([jnp.sum(s, 0) for s in sums], 0).reshape(-1, 3, 128)
    heads = heads.transpose(1, 0, 2).reshape(3, -1)
    return jnp.concatenate([rest[:4], heads, rest[7:]], 0)


def local(
    tokens,
    cotangent,
    lengths,
    inward_weight,
    inward_moment,
    inward_square,
    outward_weight,
    outward_moment,
    outward_square,
    expand_weight,
    expand_moment,
    expand_square,
    shrink_weight,
    shrink_moment,
    shrink_square,
    vectors,
    vector_moment,
    vector_square,
    sliced,
):
    _, length, model = tokens.shape
    x, cot = tokens.reshape(-1, model), cotangent.reshape(-1, model)
    tabs = tables(length)
    ff = 4 * model
    pairs = model // 128
    inward = (inward_weight, inward_moment, inward_square)
    outward = (outward_weight, outward_moment, outward_square)
    expand = (expand_weight, expand_moment, expand_square)
    shrink = (shrink_weight, shrink_moment, shrink_square)
    vector = (vectors, vector_moment, vector_square)
    rate_d, rate_o, rate_f = 1.0 / math.sqrt(model), 1.0 / math.sqrt(OUT_FAN), 1.0 / math.sqrt(ff)
    f, d = lax.axis_index("fsdp"), lax.axis_index("dp")
    j, c = d // 2, d % 2
    place = place_finder(sliced)
    lengths = jnp.broadcast_to(lengths[:, None, None], (lengths.shape[0], 1, 128))
    spans = [(0, 2), (2, 2), (4, 2)]

    if not sliced:
        low = [w.astype(BF) for w in (inward_weight, outward_weight, expand_weight, shrink_weight, vectors)]
        whole = [lax.all_gather(w, "fsdp", axis=0, tiled=True) for w in low[:4]]
        in_pieces, side_pieces, shrink_pieces = (whole[0],), (whole[1], whole[2]), (whole[3],)
        vec = lax.all_gather(low[4], "fsdp", axis=1, tiled=True).astype(F32)
        qkv, xt = qkv_call(place, x, in_pieces, vec[4:7].reshape(1, -1), tabs, length)
        seen = [attend_call(lengths, qkv, length, *span) for span in spans]
        out, yt, att, dpre, dr1, da, dattn, vec_rest, *far, near = ffn_call(
            place, lengths, x, [a for a, _ in seen], cot, side_pieces, shrink_pieces, vec, length
        )
        far = jnp.concatenate(far)
        order = jnp.array(TURNED)
        shrink_grad = jnp.concatenate([near, far[order]]).transpose(1, 3, 0, 2).reshape(ff, model)
        far, near = side_grad_call(place, yt, att, dpre, da)
        both = jnp.stack([near, far[order]]).transpose(2, 1, 3, 0, 4).reshape(model, 2, -1)
        expand_grad = both[:, :, : ff // 2].reshape(model, ff)
        outward_grad = both[:, :, ff // 2 :].reshape(model, model)
        backs = [back_call(place, lengths, seen[i], qkv, dattn, xt, tabs, length, i) for i in range(len(spans))]
        token_gradient = token_call(place, dr1, [b[0] for b in backs], in_pieces)
        parts = jnp.stack([part for _, _, far, near in backs for part in (near, far[order])])
        parts = parts.transpose(2, 1, 3, 0, 4).reshape(model, pairs, 3, 128)
        inward_grad = parts.transpose(0, 2, 1, 3).reshape(model, 3 * model)

        def reduced(g, axis=0):
            return lax.psum(lax.psum_scatter(g, "fsdp", scatter_dimension=axis, tiled=True).astype(F32), "dp")

        inward_new = adam_update(*inward, reduced(inward_grad), rate_d, WEIGHT_DECAY)
        outward_new = adam_update(*outward, reduced(outward_grad), rate_o, WEIGHT_DECAY)
        expand_new = adam_update(*expand, reduced(expand_grad), rate_d, WEIGHT_DECAY)
        shrink_new = adam_update(*shrink, reduced(shrink_grad), rate_f, WEIGHT_DECAY)
        vec_sum = reduced(vector_rows(vec_rest, [b[1] for b in backs]), 1)
        vector_new = adam_update(*vector, vec_sum, 0.5, 0.0)
    else:
        shard = model // 4
        r = shard // 4

        def columns(w):
            half = w.shape[1] // 2
            return lax.dynamic_slice(w, (j * r, c * half), (r, half))

        def rows(w):
            r = w.shape[0] // 8
            return lax.dynamic_slice(w, ((c * 4 + j) * r, 0), (r, w.shape[1]))

        low_vec = vectors.astype(BF)
        third = r + r // 3
        beside = jnp.pad(low_vec.reshape(-1, third), ((0, r - 3 * vectors.shape[0]), (0, 128 - third)))
        part_in = jnp.concatenate([columns(inward_weight).astype(BF), beside], -1)
        part_side = jnp.concatenate([columns(outward_weight), columns(expand_weight)], -1).astype(BF)
        part_shrink = rows(shrink_weight).astype(BF)
        z_in, lengths = after((jnp.stack(over_z(part_in)), lengths), part_side, part_shrink)
        by = z_in[:, : 3 * vectors.shape[0], part_in.shape[1] - 128 : part_in.shape[1] - 128 + third]
        by = (low_vec, *by.reshape(3, vectors.shape[0], shard))
        ordered = []
        for at in range(4):
            k = f ^ at
            ordered.append(jnp.where(k == 0, by[0], jnp.where(k == 1, by[1], jnp.where(k == 2, by[2], by[3]))))
        vec = jnp.concatenate(ordered, 1).astype(F32)
        bias = vec[4:7].reshape(1, -1)
        chips_in, z_side, vec, bias = after((over_chips(z_in), over_z(after(part_side, z_in)), vec, bias))
        in_pieces = (inward_weight, *both_cores(chips_in))
        z_side = jnp.stack(z_side)
        first_side, second_side = swap_first(z_side), swap_second(z_side)
        qkv, xt = qkv_call(place, x, after(in_pieces, z_side), bias, tabs, length)
        first_side, second_side = after((first_side, second_side), qkv)
        third_side = swap_second(first_side)
        z_shrink = over_z(after(part_shrink, first_side))
        far_z_side = swap_core(after(z_side, qkv))
        seen = [attend_call(lengths, after(qkv, first_side), length, *spans[0])]
        third_side, far_z_side, z_shrink = after((third_side, far_z_side, z_shrink), seen[0])
        z_shrink = jnp.stack(z_shrink)
        first_shrink, second_shrink = swap_first(z_shrink), swap_second(z_shrink)
        far_side = tuple(swap_core(part) for part in after((second_side, first_side, third_side), z_shrink))
        seen.append(attend_call(lengths, after(qkv, third_side, z_shrink), length, *spans[1]))
        first_shrink, second_shrink, far_side = after((first_shrink, second_shrink, far_side), seen[1])
        third_shrink = swap_second(first_shrink)
        shrink_near = (z_shrink, second_shrink, first_shrink)
        shrink_far = tuple(swap_core(part) for part in shrink_near)
        side_pieces = (outward_weight, expand_weight, z_side, second_side, first_side, third_side, far_z_side, *far_side)
        seen.append(attend_call(lengths, after(qkv, first_shrink), length, *spans[2]))
        third_shrink, shrink_far = after((third_shrink, shrink_far), seen[2])
        shrink_pieces = (shrink_weight, *shrink_near, third_shrink, *shrink_far, swap_core(third_shrink))

        out, yt, att, dpre, dr1, da, dattn, vec_rest, late_s, soon_s, mine_s = ffn_call(
            place, lengths, x, [a for a, _ in seen], cot, side_pieces, shrink_pieces, vec, length
        )

        def back(span, wait, *part):
            return back_call(place, lengths, seen[span], qkv, after(dattn, wait), xt, tabs, length, span, *part)

        to_s = sums_call(place, ("first", [mine_s], [swap_core(soon_s)], []))[0]
        got_s = swap_first(to_s)
        recv_s = swap_core(after(late_s, to_s))
        theirs_d, mine_d = side_grad_call(place, yt, att, after(dpre, to_s), da)
        got_s, recv_s = after((got_s, recv_s), theirs_d)
        on_s = sums_call(place, ("second", [mine_s], [recv_s], [got_s]))[0]
        last_s = swap_second(on_s)
        recv_d = swap_core(after(theirs_d, on_s))
        g0, sum0, theirs_0, mine_0 = back(0, on_s)
        last_s, recv_d = after((last_s, recv_d), g0)
        to_d, z_s = sums_call(
            place, ("first", [mine_d], [recv_d], []), ("own", [mine_s], [recv_s], [got_s, last_s])
        )
        got_d = swap_first(to_d)
        part_s = lax.psum_scatter(z_s, "fsdp", scatter_dimension=0)
        recv_0 = swap_core(after(theirs_0, to_d))
        g1, sum1, theirs_1, mine_1 = back(1, to_d)
        got_d, recv_0 = after((got_d, recv_0), g1)
        on_d = sums_call(place, ("second", [mine_d], [recv_d], [got_d]))[0]
        last_d = swap_second(on_d)
        recv_1 = swap_core(after(theirs_1, on_d))
        sum_s = lax.all_gather(after(part_s, on_d), "dp")
        g2, sum2, theirs_2, mine_2 = back(2, on_d)
        last_d, recv_1, theirs_2 = after((last_d, recv_1, theirs_2), g2)
        recv_2 = swap_core(theirs_2)
        z_d = sums_call(place, ("own", [mine_d], [recv_d], [got_d, last_d]))[0]
        part_d = lax.psum_scatter(z_d, "fsdp", scatter_dimension=0)
        mine_v = vector_parts(place, after(vec_rest, z_d), [sum0, sum1, sum2], r)
        mine_e = [mine_0, mine_1, mine_2, mine_v]
        recv_e = [recv_0, recv_1, after(recv_2, mine_v)]
        to_e = sums_call(place, ("first", mine_e, recv_e, []))[0]
        got_e = swap_first(to_e)
        token_gradient = token_call(place, after(dr1, to_e), [g0, g1, g2], in_pieces)
        got_e = after(got_e, token_gradient)
        on_e = sums_call(place, ("second", mine_e, recv_e, [got_e]))[0]
        last_e = swap_second(on_e)
        shrink_new = adam_turned_call((after(shrink[0], on_e), *shrink[1:]), sum_s, rate_f)
        last_e, part_d = after((last_e, part_d), shrink_new[0])
        sum_d = lax.all_gather(part_d, "dp")
        z_e = send_z(*sums_call(place, ("split", mine_e, recv_e, [got_e, last_e])))
        moves = [(0, ff // 2, model // 2), (1, 0, ff // 2)]
        sum_e = both_cores(over_chips(plus(*z_e)))
        moves_e = []
        for span in range(3):
            for t in range(3):
                moves_e.append((span * 384 + t * 128, t * model + span * 256, 128))
        new = adam_last_call(
            place,
            inward,
            vector,
            sum_e,
            moves_e,
            rate_d,
            3 * model // 2,
            [outward, expand],
            sum_d,
            moves,
            [rate_o, rate_d],
        )
        inward_new, vector_new, outward_new, expand_new = new[:3], new[3:6], new[6:9], new[9:]
    return (
        out.reshape(tokens.shape),
        token_gradient.reshape(tokens.shape),
        *inward_new,
        *outward_new,
        *expand_new,
        *shrink_new,
        *vector_new,
    )


def solution(mesh):
    both = P(("dp", "fsdp"), None, None)
    in_specs = (both, both, P(("dp", "fsdp"))) + (P("fsdp", None),) * 12 + (P(None, "fsdp"),) * 3
    out_specs = (both, both) + (P("fsdp", None),) * 12 + (P(None, "fsdp"),) * 3
    sliced = mesh.shape["dp"] == 8 and mesh.shape["fsdp"] == 4
    step = functools.partial(local, sliced=sliced)
    return jax.shard_map(step, mesh=mesh, in_specs=in_specs, out_specs=out_specs, check_vma=False)
```
